32 devices in a mesh: groups: 2 (over x), agent: 8 (over z, y), tm: 2 (over core).
Axes of the slice: x: 2, y: 2, z: 4, core: 2. Of those that a mesh axis runs over, the one named last changes fastest.
Arguments:
- embedded: bfloat16 [64, 1024, 512], P(('groups', 'tm'), 'agent'), parts along dimension 0, may hold values from -6 to 6
- block_lists: int32 [16, 32, 2], P(('groups', 'agent'), 'tm'), parts along dimension 0, may hold values from 0 to 7, all different within a row; in each aligned block of 16 rows (0 to 15, 16 to 31, ..., all dimensions but the last counted through in order) at most 8 rows name the same one
- done_flags: int32 [64, 1024], P(('groups', 'tm'), 'agent'), parts along dimension 0, may hold values 0 or 1
- rewards: float32 [64, 1024], P(('groups', 'tm'), 'agent'), parts along dimension 0, may hold values from -1.2 to 1.2
- bootstrap: float32 [2048], P(('groups', 'agent')), parts along dimension 0, may hold values from -6 to 6
- agent_proj: bfloat16 [512, 1536], replicated, may hold values from -2 to 2
- agent_merge: bfloat16 [512, 512], replicated, may hold values from -0.75 to 0.75
- time_proj: bfloat16 [512, 1536], replicated, may hold values from -2 to 2
- time_merge: bfloat16 [512, 512], replicated, may hold values from -0.75 to 0.75
- value_weight: float32 [512], replicated, may hold values from -0.25 to 0.25
Outputs:
- values: float32 [64, 1024], P(('groups', 'tm'), 'agent'), parts along dimension 0
- advantages: float32 [64, 1024], P(('groups', 'tm'), 'agent'), parts along dimension 0
The draws below stay inside these ranges and needn't reach their ends.
There are 2 independent parts, one for each index of `groups`. The reference program is written for one: setup_inputs(seed, part) draws one part's arguments, and reference() takes and returns one part's arrays. A program takes and returns all parts, laid end to end along the dimension named above; an argument that names none is the same for every part. Nothing has to cross between parts.
Inputs may be any that keep to these rules, and one draw needn't show every extreme that they name: `block_lists`: each row names 2 different agent blocks. Within the 16 rows of one block along the second dimension no agent block is named more than 8 times, and some agent block is named exactly 8 times.
All inputs are finite; a program needn't handle non-finite values. No bound on the sum of `done_flags` on one device may be relied on, other than what follows from the above.
Results may differ from the reference program's by a relative error of at most 0.0085.
Values may be sent and summed in bfloat16 or wider, within the bound.
No kernel may reach another device: no remote copies, remote signals or barrier semaphores. Data moves between devices by JAX's collectives and lax.ppermute only.
A program may use at most 128 MiB of HBM per device.

```python
import math
import jax
import jax.numpy as jnp
import numpy as np
from jax import lax

D = 512
HEADS = 8
HEAD = 64
AGT_DEV = 128
STEPS_DEV = 16
WINDOW = 16
LIST = 2
CAP = 8
BLOCKS = 8
AGENTS = 1024
STEPS = 32


def projection_draw(key):
    queries = jax.random.normal(jax.random.fold_in(key, 11), (D, HEADS, HEAD), jnp.float32) * D ** (-0.5)
    keys_part = jax.random.normal(jax.random.fold_in(key, 12), (D, HEADS, HEAD), jnp.float32) * D ** (-0.5)
    values_part = jax.random.normal(jax.random.fold_in(key, 13), (D, HEADS, HEAD), jnp.float32) * D ** (-0.5)
    stacked = jnp.stack([queries, keys_part, values_part], axis=1)
    stacked = jnp.clip(stacked, -2.0, 2.0)
    return stacked.reshape(D, 3 * D).astype(jnp.bfloat16)


def draw_agent_proj(key, part):
    return projection_draw(jax.random.fold_in(key, 1))


def draw_time_proj(key, part):
    return projection_draw(jax.random.fold_in(key, 2))


def set_ends(values, own_key, smallest, largest):
    longest = values.shape.index(max(values.shape))
    spots = []
    for shift in (0, 1):
        where = [jax.random.randint(jax.random.fold_in(own_key, axis), (), 0, length) for axis, length in enumerate(values.shape)]
        where[longest] = (where[longest] + shift) % values.shape[longest]
        spots.append(tuple(where))
    return values.at[spots[0]].set(smallest).at[spots[1]].set(largest)


def block_scale(rng, shape, split, least, high):
    def one(position, shards_of):
        draws = jax.random.uniform(jax.random.fold_in(jax.random.fold_in(rng, 6), position), (shards_of,), jnp.float32, least / len(split), high / len(split))
        return jnp.repeat(jnp.exp(draws), shape[position] // shards_of).reshape((-1,) + (1,) * (len(shape) - position - 1))

    gain = one(*split[0])
    for cut in split[1:]:
        gain = gain * one(*cut)
    return gain


def assign_block(rng, own, number, rows, amount, top, limit, slope):
    ranking = jax.random.permutation(rng, amount)
    crowded, ordinary = load_shares(amount, rows * top, limit, slope, True), load_shares(amount, rows * top, limit, slope, False)
    places = jnp.arange(amount)

    def named(sizes, offset_by):
        used = int((sizes > 0).sum())
        fixed = max(1, used // 4)
        moved = fixed + (places - fixed + offset_by * (used - fixed)) % max(1, amount - fixed)
        return jnp.zeros((amount,), jnp.int32).at[ranking[jnp.where(places < fixed, places, moved)]].set(jnp.asarray(sizes, jnp.int32))

    sizes = jnp.where(number % 4 == 0, named(crowded, number // 4), named(ordinary, number - number // 4 - 1))
    mixed = jax.random.permutation(jax.random.fold_in(own, 3), amount)
    donor, receiver = mixed[0:amount // 2 * 2:2], mixed[1:amount // 2 * 2:2]
    room = jnp.minimum(sizes[donor] - 1, limit - sizes[receiver]) // 2
    room = jnp.where((donor == ranking[0]) | (receiver == ranking[0]) | (sizes[receiver] == 0), 0, jnp.maximum(room, 0))
    moved = jax.random.randint(jax.random.fold_in(own, 4), (amount // 2,), 0, 1 << 20) % (room + 1)
    sizes = sizes.at[donor].add(-moved).at[receiver].add(moved)
    items = jnp.searchsorted(jnp.cumsum(sizes), jnp.arange(rows * top), side="right").astype(jnp.int32)
    listing = items.reshape(top, rows).T
    listing = listing[jax.random.permutation(jax.random.fold_in(own, 1), rows)]
    offset_by = jax.random.randint(jax.random.fold_in(own, 2), (rows, 1), 0, top)
    return jnp.take_along_axis(listing, (jnp.arange(top)[None, :] + offset_by) % top, axis=1)


def load_shares(amount, total, reach, skew, full):
    portions = [(1 << 20) // math.isqrt(grade ** skew) + 1 for grade in range(1, amount + 1)]
    largest = reach if full else min(reach, max(-(-total // amount), total * portions[0] // sum(portions)))
    least = 1 if total - largest >= amount - 1 else 0
    holding, surplus = [largest] + [least] * (amount - 1), total - largest - least * (amount - 1)
    while surplus > 0:
        movable = [i for i in range(1, amount) if holding[i] < largest] or [i for i in range(1, amount) if holding[i] < reach]
        pool, remaining = sum([portions[i] for i in movable]), surplus
        for i in movable:
            addition = min(reach - holding[i], max(1, remaining * portions[i] // pool), surplus)
            holding[i] = holding[i] + addition
            surplus = surplus - addition
    return np.array(holding)


def normal_values(rng, shape, spread, most, split=(), kind=jnp.bfloat16):
    values = spread * jax.random.normal(rng, shape, jnp.float32)
    if split:
        values = values * block_scale(rng, shape, split, -0.22, 0.18)
    return jnp.clip(values, -most, most).astype(kind)


def setup_inputs(seed: int = 0, part: int = 0) -> dict:
    splits = jax.random.split(jax.random.key(seed), 11)
    part_keys = jax.random.split(jax.random.fold_in(splits[10], part), 11)
    embedded = normal_values(part_keys[0], (STEPS, AGENTS, D), 1.0, 6.0, ((0, 2), (1, 8)))
    block_lists_keys = jax.random.split(jax.random.fold_in(part_keys[1], 1), BLOCKS * STEPS // STEPS_DEV)
    block_lists_turns = jax.random.permutation(jax.random.fold_in(part_keys[1], 3), BLOCKS * STEPS // STEPS_DEV)
    block_lists = jax.vmap(lambda own, number: assign_block(jax.random.fold_in(part_keys[1], 2), own, number, STEPS_DEV, BLOCKS, LIST, CAP, 2))(block_lists_keys, block_lists_turns).reshape((BLOCKS, STEPS, LIST))
    done_flags = set_ends((jax.random.randint(part_keys[2], (STEPS, AGENTS), 0, 32) < 1).astype(jnp.int32), jax.random.fold_in(part_keys[2], 1), 0, 1)
    rewards = normal_values(part_keys[3], (STEPS, AGENTS), 0.2, 1.2, ((0, 2), (1, 8)), jnp.float32)
    bootstrap = normal_values(part_keys[4], (AGENTS,), 1.0, 6.0, ((0, 8),), jnp.float32)
    agent_proj = draw_agent_proj(jax.random.fold_in(splits[10], 71), part)
    agent_merge = normal_values(splits[6], (D, D), HEAD ** -0.5, 0.75)
    time_proj = draw_time_proj(jax.random.fold_in(splits[10], 71), part)
    time_merge = normal_values(splits[8], (D, D), HEAD ** -0.5, 0.75)
    value_weight = normal_values(splits[9], (D,), D ** -0.5, 0.25, (), jnp.float32)
    return {"embedded": embedded, "block_lists": block_lists, "done_flags": done_flags, "rewards": rewards, "bootstrap": bootstrap, "agent_proj": agent_proj, "agent_merge": agent_merge, "time_proj": time_proj, "time_merge": time_merge, "value_weight": value_weight}


discount = 0.9997
trace_decay = 0.995
epsilon = 1e-06

def rms_norm(values):
    return values * lax.rsqrt(lax.optimization_barrier(jnp.mean(values * values, axis=-1, keepdims=True)) + epsilon)

def softmax_rows(scores):
    shifted = scores - lax.optimization_barrier(jnp.max(scores, axis=-1, keepdims=True))
    exponent = jnp.exp(shifted)
    return exponent / lax.optimization_barrier(jnp.sum(exponent, axis=-1, keepdims=True))

def reference(embedded, block_lists, done_flags, rewards, bootstrap, agent_proj, agent_merge, time_proj, time_merge, value_weight):
    tokens = STEPS * AGENTS
    score_scale = HEAD ** (-0.5)
    residual = embedded.astype(jnp.float32).reshape(tokens, D)
    normed = rms_norm(residual).astype(jnp.bfloat16)
    projected = jnp.dot(normed, agent_proj, preferred_element_type=jnp.float32).astype(jnp.bfloat16)
    projected = projected.reshape(STEPS, BLOCKS, AGT_DEV, 3, HEADS, HEAD)

    def agent_step(step):
        step_rows = projected[step]
        listed = step_rows[block_lists[:, step, :]]
        all_keys = jnp.concatenate([step_rows[:, None], listed], axis=1)
        all_keys = all_keys.reshape(BLOCKS, (1 + LIST) * AGT_DEV, 3, HEADS, HEAD)
        queries = step_rows[:, :, 0].astype(jnp.float32)
        scores = jnp.einsum('bqhe,bkhe->bhqk', queries, all_keys[:, :, 1].astype(jnp.float32)) * score_scale
        attention = softmax_rows(scores).astype(jnp.bfloat16)
        attended = jnp.einsum('bhqk,bkhe->bqhe', attention.astype(jnp.float32), all_keys[:, :, 2].astype(jnp.float32))
        return attended.astype(jnp.bfloat16).reshape(AGENTS, D)
    attended = lax.map(agent_step, jnp.arange(STEPS))
    residual = residual + jnp.dot(attended.reshape(tokens, D), agent_merge, preferred_element_type=jnp.float32)
    normed = rms_norm(residual).astype(jnp.bfloat16)
    projected = jnp.dot(normed, time_proj, preferred_element_type=jnp.float32).astype(jnp.bfloat16)
    projected = projected.reshape(STEPS, AGENTS, 3 * D)
    time_keys = projected[:, :, D:]
    padded = jnp.concatenate([jnp.zeros((WINDOW, AGENTS, 2 * D), jnp.bfloat16), time_keys], axis=0)
    block_count = STEPS // WINDOW
    previous = padded[:STEPS].reshape(block_count, WINDOW, AGENTS, 2, HEADS, HEAD)
    current = padded[WINDOW:].reshape(block_count, WINDOW, AGENTS, 2, HEADS, HEAD)
    key_blocks = jnp.concatenate([previous, current], axis=1)
    query_blocks = projected[:, :, :D].reshape(block_count, WINDOW, AGENTS, HEADS, HEAD)
    block_starts = jnp.arange(block_count) * WINDOW

    def time_block(inputs):
        query_block, key_block, start_step = inputs
        query_step = start_step + jnp.arange(WINDOW)
        key_step = start_step - WINDOW + jnp.arange(2 * WINDOW)
        allowed = (key_step[None, :] <= query_step[:, None]) & (key_step[None, :] > query_step[:, None] - WINDOW) & (key_step[None, :] >= 0)
        scores = jnp.einsum('qahe,kahe->ahqk', query_block.astype(jnp.float32), key_block[:, :, 0].astype(jnp.float32)) * score_scale
        scores = jnp.where(allowed[None, None], scores, -1e+30)
        attention = softmax_rows(scores).astype(jnp.bfloat16)
        result = jnp.einsum('ahqk,kahe->qahe', attention.astype(jnp.float32), key_block[:, :, 1].astype(jnp.float32))
        return result.astype(jnp.bfloat16)
    attended = lax.map(time_block, (query_blocks, key_blocks, block_starts))
    residual = residual + jnp.dot(attended.reshape(tokens, D), time_merge, preferred_element_type=jnp.float32)
    values = lax.optimization_barrier(jnp.sum(rms_norm(residual) * value_weight, axis=-1)).reshape(STEPS, AGENTS)
    living = 1.0 - done_flags.astype(jnp.float32)
    following = jnp.concatenate([values[1:], bootstrap[None, :]], axis=0)
    changes = rewards + discount * living * following - values
    factors = discount * trace_decay * living

    def backward(running, inputs):
        change, factor = inputs
        running = change + factor * running
        return (running, running)
    final_carry, advantages = lax.scan(backward, jnp.zeros((AGENTS,), jnp.float32), (changes, factors), reverse=True)
    return (values, advantages)
```

```python
import functools

import jax
import jax.numpy as jnp
from jax import lax
from jax.experimental import pallas as pl
from jax.experimental.pallas import tpu as pltpu
from jax.sharding import PartitionSpec as P

HEADS = 8
WINDOW = 16
discount = 0.9997
trace_decay = 0.995
epsilon = 1e-06
bf16 = jnp.bfloat16
f32 = jnp.float32
VMEM_LIMIT = 48 * 1024 * 1024


def rms(values):
    return values * lax.rsqrt(jnp.mean(values * values, axis=-1, keepdims=True) + epsilon)


def dot(a, b):
    return jnp.dot(a, b, preferred_element_type=f32)


def dot_t(a, b):
    return lax.dot_general(a, b, (((1,), (1,)), ((), ())), preferred_element_type=f32)


def attend(queries, keys, values, head_size, bias):
    rows, width = queries.shape
    scale = head_size ** (-0.5)
    pair = 2 * head_size
    lane = lax.broadcasted_iota(jnp.int32, (rows, pair), 1)
    first = lane < head_size
    ones = jnp.ones((keys.shape[0], pair), bf16)
    mixed = []
    for at in range(0, width, pair):
        both = queries[:, at : at + pair]
        none = jnp.zeros_like(both)
        stacked = jnp.concatenate(
            [jnp.where(first, both, none), jnp.where(first, none, both)], axis=0
        )
        scores = dot_t(stacked, keys[:, at : at + pair]) * scale
        if bias is not None:
            scores = scores + bias
        weights = jnp.exp(scores - jnp.max(scores, axis=-1, keepdims=True)).astype(bf16)
        summed = dot(weights, jnp.concatenate([values[:, at : at + pair], ones], axis=1))
        result = summed[:, :pair] / summed[:, pair:]
        mixed.append(jnp.where(first, result[:rows], result[rows:]).astype(bf16))
    return jnp.concatenate(mixed, axis=1)


def agent_kernel(list_length, head_size, where_ref, *refs):
    own_ref, listed_refs = refs[0], refs[1 : 1 + list_length]
    proj_ref, merge_ref, residual_ref, normed_ref = refs[1 + list_length :]
    width = own_ref.shape[-1]
    own = own_ref[0].astype(f32)
    rows = [rms(own).astype(bf16)]
    for listed in listed_refs:
        rows.append(rms(listed[0].astype(f32)).astype(bf16))
    queries = dot(rows[0], proj_ref[:, :width]).astype(bf16)
    keyvals = dot(jnp.concatenate(rows, axis=0), proj_ref[:, width:]).astype(bf16)
    mixed = attend(queries, keyvals[:, :width], keyvals[:, width:], head_size, None)
    residual = own + dot(mixed, merge_ref[...])
    residual_ref[0] = residual
    normed_ref[0] = rms(residual).astype(bf16)


def agent_stage(embedded, pool, where, first_step, steps, proj, merge):
    _, agents, width = embedded.shape
    list_length = where.shape[0] // steps
    piece = (1, agents, width)

    def listed_spec(j):
        return pl.BlockSpec(piece, lambda i, w: (w[i * list_length + j], 0, 0))

    whole = lambda i, w: (0, 0)
    return pl.pallas_call(
        functools.partial(agent_kernel, list_length, width // HEADS),
        grid_spec=pltpu.PrefetchScalarGridSpec(
            num_scalar_prefetch=1,
            grid=(steps,),
            in_specs=[pl.BlockSpec(piece, lambda i, w: (first_step + i, 0, 0))]
            + [listed_spec(j) for j in range(list_length)]
            + [pl.BlockSpec(proj.shape, whole), pl.BlockSpec(merge.shape, whole)],
            out_specs=[pl.BlockSpec(piece, lambda i, w: (i, 0, 0))] * 2,
        ),
        out_shape=[
            jax.ShapeDtypeStruct((steps, agents, width), f32),
            jax.ShapeDtypeStruct((steps, agents, width), bf16),
        ],
        compiler_params=pltpu.CompilerParams(vmem_limit_bytes=VMEM_LIMIT),
        name="agent_stage",
    )(where, embedded, *([pool] * list_length), proj, merge)


def suffix(values, rewards, done, next_value, next_advantage):
    steps = values.shape[0]
    living = 1.0 - done.astype(f32)
    running, following, rows = next_advantage, next_value, [None] * steps
    for step in range(steps - 1, -1, -1):
        alive = living[step : step + 1]
        value = values[step : step + 1]
        change = rewards[step : step + 1] + discount * alive * following - value
        running = change + discount * trace_decay * alive * running
        rows[step] = running
        following = value
    return rows


def time_kernel(parts, steps, tile, head_size, offset_ref, *refs):
    refs = list(refs)
    residual_refs = [refs.pop(0) for _ in range(parts)]
    rim_refs = [refs.pop(0) for _ in range(parts)]
    proj_ref, merge_ref, weight_ref, done_ref, rewards_ref, boot_ref = refs[:6]
    values_ref, edge_ref, bias_ref = refs[6:]
    width = proj_ref.shape[0]
    turn = pl.program_id(0)
    group = 8
    rows = steps * group
    agents = values_ref.shape[1]

    @pl.when(turn == 0)
    def _():
        r = lax.broadcasted_iota(jnp.int32, (2 * rows, 2 * rows), 0) % rows
        c = lax.broadcasted_iota(jnp.int32, (2 * rows, 2 * rows), 1)
        query_step = r // group
        key_step = c // group - steps
        allowed = (
            (r % group == c % group)
            & (key_step <= query_step)
            & (key_step > query_step - WINDOW)
            & (key_step + offset_ref[0] >= 0)
        )
        bias_ref[...] = jnp.where(allowed, 0.0, -1e30)
        values_ref[...] = jnp.zeros_like(values_ref)

    def pieces(part_refs):
        whole = jnp.concatenate([ref[...].astype(f32) for ref in part_refs], axis=0)
        return [
            whole[:, at : at + group].reshape(rows, width) for at in range(0, tile, group)
        ]

    residuals = pieces(residual_refs)
    current = jnp.concatenate([rms(r).astype(bf16) for r in residuals], axis=0)
    behind = jnp.concatenate([r.astype(bf16) for r in pieces(rim_refs)], axis=0)
    projected = dot(current, proj_ref[...]).astype(bf16)
    before = dot(behind, proj_ref[:, width:]).astype(bf16)
    bias = bias_ref[...]
    mixed = []
    for at in range(0, tile * steps, rows):
        mine, past = projected[at : at + rows], before[at : at + rows]
        keys = jnp.concatenate([past[:, :width], mine[:, width : 2 * width]], axis=0)
        held = jnp.concatenate([past[:, width:], mine[:, 2 * width :]], axis=0)
        mixed.append(attend(mine[:, :width], keys, held, head_size, bias))
    merged = dot(jnp.concatenate(mixed, axis=0), merge_ref[...])
    lane = lax.broadcasted_iota(jnp.int32, (steps, group, agents), 2)
    place = lax.broadcasted_iota(jnp.int32, (steps, group, agents), 1)
    total = values_ref[...]
    for n, residual in enumerate(residuals):
        final = rms(residual + merged[n * rows : (n + 1) * rows])
        value = jnp.sum(final * weight_ref[...], axis=-1, keepdims=True)
        spot = lane == place + (turn * tile + n * group)
        total = total + jnp.sum(
            jnp.where(spot, value.reshape(steps, group, 1), 0.0), axis=1
        )
    values_ref[...] = total

    @pl.when(turn == pl.num_programs(0) - 1)
    def _():
        found = values_ref[...]
        boot = boot_ref[...]
        advantages = suffix(found, rewards_ref[...], done_ref[...], boot, jnp.zeros_like(boot))
        edge_ref[...] = jnp.concatenate([found[:1], advantages[0]], axis=0)


def time_stage(residuals, rims, offset, proj, merge, weight, done, rewards, boot):
    part_steps = [r.shape[0] for r in residuals]
    steps = sum(part_steps)
    _, agents, width = residuals[0].shape
    tile = 16
    whole = lambda i, o: (0, 0)

    def blocks(arrays):
        return [
            pl.BlockSpec((array.shape[0], tile, width), lambda i, o: (0, i, 0))
            for array in arrays
        ]

    rows = 16 * steps
    fixed = [proj, merge, weight, done, rewards, boot]
    return pl.pallas_call(
        functools.partial(time_kernel, len(residuals), steps, tile, width // HEADS),
        grid_spec=pltpu.PrefetchScalarGridSpec(
            num_scalar_prefetch=1,
            grid=(agents // tile,),
            in_specs=blocks(residuals)
            + blocks(rims)
            + [pl.BlockSpec(array.shape, whole) for array in fixed],
            out_specs=[
                pl.BlockSpec((steps, agents), whole),
                pl.BlockSpec((2, agents), whole),
            ],
            scratch_shapes=[pltpu.VMEM((rows, rows), f32)],
        ),
        out_shape=[
            jax.ShapeDtypeStruct((steps, agents), f32),
            jax.ShapeDtypeStruct((2, agents), f32),
        ],
        compiler_params=pltpu.CompilerParams(vmem_limit_bytes=VMEM_LIMIT),
        name="time_stage",
    )(offset, *residuals, *rims, *fixed)


def advantage_kernel(last_ref, values_ref, rewards_ref, done_ref, boot_ref, edge_ref, out_ref, mine_ref):
    last = last_ref[0] > 0
    arriving = edge_ref[...]
    boot = boot_ref[...]
    found = values_ref[...]
    next_value = jnp.where(last, boot, arriving[:1])
    next_advantage = jnp.where(last, 0.0, arriving[1:2])
    rows = suffix(found, rewards_ref[...], done_ref[...], next_value, next_advantage)
    out_ref[...] = jnp.concatenate(rows, axis=0)
    mine_ref[...] = jnp.concatenate([found[:1], rows[0]], axis=0)


def advantage_stage(last, values, rewards, done, boot, edge):
    return pl.pallas_call(
        advantage_kernel,
        in_specs=[pl.BlockSpec(memory_space=pltpu.SMEM)]
        + [pl.BlockSpec(memory_space=pltpu.VMEM)] * 5,
        out_specs=[pl.BlockSpec(memory_space=pltpu.VMEM)] * 2,
        out_shape=[
            jax.ShapeDtypeStruct(values.shape, f32),
            jax.ShapeDtypeStruct(edge.shape, f32),
        ],
        name="advantage_stage",
    )(last, values, rewards, done, boot, edge)


def exchange_slots(embedded, lists, capacity):
    steps, agents, width = embedded.shape
    blocks = lax.axis_size("agent")
    list_length = lists.shape[1]
    named = lists.reshape(-1)
    row_steps = jnp.arange(named.shape[0], dtype=jnp.int32) // list_length
    hits = (named[:, None] == jnp.arange(blocks, dtype=jnp.int32)[None, :]).astype(jnp.int32)
    slot = jnp.sum((jnp.cumsum(hits, axis=0) - hits) * hits, axis=1)
    slot_hits = (slot[:, None] == jnp.arange(capacity, dtype=jnp.int32)[None, :]).astype(jnp.int32)
    requests = jnp.sum(
        (hits * row_steps[:, None])[:, :, None] * slot_hits[:, None, :], axis=0
    )
    wanted = lax.all_to_all(requests, "agent", split_axis=0, concat_axis=0, tiled=True)
    outgoing = embedded[wanted.reshape(-1)].reshape(blocks, capacity, agents, width)
    arrived = lax.all_to_all(outgoing, "agent", split_axis=0, concat_axis=0, tiled=True)
    return arrived.reshape(blocks * capacity, agents, width), named * capacity + slot


def body(
    embedded,
    block_lists,
    done_flags,
    rewards,
    bootstrap,
    agent_proj,
    agent_merge,
    time_proj,
    time_merge,
    value_weight,
):
    steps, agents, width = embedded.shape
    list_length = block_lists.shape[2]
    blocks = lax.axis_size("agent")
    lists = block_lists[0]
    capacity = max(2, (2 * steps * list_length + blocks - 1) // blocks)
    residuals, normed = [], []
    if steps <= 2 * capacity:
        chunk = max(1, steps // 4)
        pools = [
            lax.all_gather(embedded[at : at + chunk], "agent", axis=0, tiled=True)
            for at in range(0, steps, chunk)
        ]
        for n, pool in enumerate(pools):
            mine = lists[n * chunk : (n + 1) * chunk]
            where = mine * chunk + jnp.arange(chunk, dtype=jnp.int32)[:, None]
            first, second = agent_stage(
                embedded, pool, where.reshape(-1), n * chunk, chunk, agent_proj, agent_merge
            )
            residuals.append(first)
            normed.append(second)
    else:
        pool, where = exchange_slots(embedded, lists, capacity)
        first, second = agent_stage(embedded, pool, where, 0, steps, agent_proj, agent_merge)
        residuals.append(first)
        normed.append(second)

    spans = lax.axis_size("tm")
    forward = [(i, i + 1) for i in range(spans - 1)]
    backward = [(i + 1, i) for i in range(spans - 1)]
    rims = [lax.ppermute(part, "tm", forward) for part in normed]
    index = lax.axis_index("tm")
    offset = (index * steps).astype(jnp.int32).reshape(1)
    boot = bootstrap.reshape(1, agents)
    values, edge = time_stage(
        residuals,
        rims,
        offset,
        time_proj,
        time_merge,
        value_weight.reshape(1, width),
        done_flags,
        rewards,
        boot,
    )
    last = (index == spans - 1).astype(jnp.int32).reshape(1)
    for _ in range(max(1, spans - 1)):
        arriving = lax.ppermute(edge, "tm", backward)
        advantages, edge = advantage_stage(last, values, rewards, done_flags, boot, arriving)
    return (values, advantages)


def solution(mesh):
    placed = (
        P(("groups", "tm"), "agent", None),
        P(("groups", "agent"), "tm", None),
        P(("groups", "tm"), "agent"),
        P(("groups", "tm"), "agent"),
        P(("groups", "agent")),
        P(),
        P(),
        P(),
        P(),
        P(),
    )
    return jax.shard_map(
        body,
        mesh=mesh,
        in_specs=placed,
        out_specs=(P(("groups", "tm"), "agent"), P(("groups", "tm"), "agent")),
        check_vma=False,
    )
```

```python
import functools

import jax
import jax.numpy as jnp
from jax import lax
from jax.experimental import pallas as pl
from jax.experimental.pallas import tpu as pltpu
from jax.sharding import PartitionSpec as P

HEADS = 8
WINDOW = 16
discount = 0.9997
trace_decay = 0.995
epsilon = 1e-06
bf16 = jnp.bfloat16
f32 = jnp.float32
VMEM_LIMIT = 48 * 1024 * 1024
SPAN = 1024
COLUMNS = 4
ROWS = 2


def rms(values):
    return values * lax.rsqrt(jnp.mean(values * values, axis=-1, keepdims=True) + epsilon)


def dot(a, b):
    return jnp.dot(a, b, preferred_element_type=f32)


def dot_t(a, b):
    return lax.dot_general(a, b, (((1,), (1,)), ((), ())), preferred_element_type=f32)


def attend(queries, keys, values, head_size, bias):
    rows, width = queries.shape
    scale = head_size ** (-0.5)
    pair = 2 * head_size
    lane = lax.broadcasted_iota(jnp.int32, (rows, pair), 1)
    first = lane < head_size
    ones = jnp.ones((keys.shape[0], pair), bf16)
    mixed = []
    for at in range(0, width, pair):
        both = queries[:, at : at + pair]
        none = jnp.zeros_like(both)
        stacked = jnp.concatenate(
            [jnp.where(first, both, none), jnp.where(first, none, both)], axis=0
        )
        scores = dot_t(stacked, keys[:, at : at + pair]) * scale
        if bias is not None:
            scores = scores + bias
        weights = jnp.exp(scores - jnp.max(scores, axis=-1, keepdims=True)).astype(bf16)
        summed = dot(weights, jnp.concatenate([values[:, at : at + pair], ones], axis=1))
        result = summed[:, :pair] / summed[:, pair:]
        mixed.append(jnp.where(first, result[:rows], result[rows:]).astype(bf16))
    return jnp.concatenate(mixed, axis=1)


def fetch(entry, arrays, target, sem):
    for code, ref in arrays.items():

        @pl.when(entry // SPAN == code)
        def _(ref=ref):
            pltpu.make_async_copy(ref.at[entry % SPAN], target, sem).start()


def agent_kernel(list_length, first_step, codes, head_size, table_ref, own_ref, *refs):
    arrays = dict(zip(codes, refs))
    proj_ref, merge_ref, residual_ref, normed_ref, held_ref, sems = refs[len(codes) :]
    width = own_ref.shape[-1]
    turn = pl.program_id(0)

    def begin(step):
        for j in range(list_length):
            slot = step % 2
            entry = table_ref[(first_step + step) * list_length + j]
            fetch(entry, arrays, held_ref.at[slot, j], sems.at[slot, j])

    @pl.when(turn == 0)
    def _():
        begin(turn)

    @pl.when(turn + 1 < pl.num_programs(0))
    def _():
        begin(turn + 1)

    own = own_ref[0].astype(f32)
    rows = [rms(own).astype(bf16)]
    queries = dot(rows[0], proj_ref[:, :width]).astype(bf16)
    slot = turn % 2
    for j in range(list_length):
        pltpu.make_async_copy(refs[0].at[0], held_ref.at[slot, j], sems.at[slot, j]).wait()
        rows.append(rms(held_ref[slot, j].astype(f32)).astype(bf16))
    keyvals = dot(jnp.concatenate(rows, axis=0), proj_ref[:, width:]).astype(bf16)
    mixed = attend(queries, keyvals[:, :width], keyvals[:, width:], head_size, None)
    residual = own + dot(mixed, merge_ref[...])
    residual_ref[0] = residual
    normed_ref[0] = rms(residual).astype(bf16)


def agent_stage(embedded, arrays, table, first_step, steps, list_length, proj, merge):
    _, agents, width = embedded.shape
    piece = (1, agents, width)
    whole = lambda i, w: (0, 0)
    flops = 2 * steps * agents * width * width * (4 + 2 * list_length + 2 * (1 + list_length))
    return pl.pallas_call(
        functools.partial(
            agent_kernel, list_length, first_step, tuple(arrays), width // HEADS
        ),
        grid_spec=pltpu.PrefetchScalarGridSpec(
            num_scalar_prefetch=1,
            grid=(steps,),
            in_specs=[pl.BlockSpec(piece, lambda i, w: (first_step + i, 0, 0))]
            + [pl.BlockSpec(memory_space=pl.ANY)] * len(arrays)
            + [pl.BlockSpec(proj.shape, whole), pl.BlockSpec(merge.shape, whole)],
            out_specs=[pl.BlockSpec(piece, lambda i, w: (i, 0, 0))] * 2,
            scratch_shapes=[
                pltpu.VMEM((2, list_length, agents, width), bf16),
                pltpu.SemaphoreType.DMA((2, list_length)),
            ],
        ),
        out_shape=[
            jax.ShapeDtypeStruct((steps, agents, width), f32),
            jax.ShapeDtypeStruct((steps, agents, width), bf16),
        ],
        compiler_params=pltpu.CompilerParams(vmem_limit_bytes=VMEM_LIMIT),
        cost_estimate=pl.CostEstimate(
            flops=5 * flops, bytes_accessed=steps * agents * width * 12, transcendentals=0
        ),
        name="agent_stage",
    )(table, embedded, *arrays.values(), proj, merge)


def pack_kernel(codes, parts, table_ref, *refs):
    arrays = dict(zip(codes, refs))
    outs, sems = refs[len(codes) : -1], refs[-1]
    slots = [
        (offset + n, out.at[n]) for out, (offset, count) in zip(outs, parts) for n in range(count)
    ]
    for n, (at, target) in enumerate(slots):
        fetch(table_ref[at], arrays, target, sems.at[n])
    for n, (at, target) in enumerate(slots):

        @pl.when(table_ref[at] >= 0)
        def _(n=n, target=target):
            pltpu.make_async_copy(refs[0].at[0], target, sems.at[n]).wait()


def pack(table, arrays, parts):
    piece = next(iter(arrays.values())).shape[1:]
    return pl.pallas_call(
        functools.partial(pack_kernel, tuple(arrays), parts),
        in_specs=[pl.BlockSpec(memory_space=pltpu.SMEM)]
        + [pl.BlockSpec(memory_space=pl.ANY)] * len(arrays),
        out_specs=[pl.BlockSpec(memory_space=pl.ANY)] * len(parts),
        out_shape=[jax.ShapeDtypeStruct((count,) + piece, bf16) for _, count in parts],
        scratch_shapes=[pltpu.SemaphoreType.DMA((sum(count for _, count in parts),))],
        cost_estimate=pl.CostEstimate(
            flops=0, bytes_accessed=4 * sum(c for _, c in parts) * piece[0] * piece[1], transcendentals=0
        ),
        name="pack",
    )(table, *arrays.values())


def suffix(values, rewards, done, next_value, next_advantage):
    steps = values.shape[0]
    living = 1.0 - done.astype(f32)
    running, following, rows = next_advantage, next_value, [None] * steps
    for step in range(steps - 1, -1, -1):
        alive = living[step : step + 1]
        value = values[step : step + 1]
        change = rewards[step : step + 1] + discount * alive * following - value
        running = change + discount * trace_decay * alive * running
        rows[step] = running
        following = value
    return rows


def time_kernel(parts, steps, tile, head_size, offset_ref, *refs):
    refs = list(refs)
    residual_refs = [refs.pop(0) for _ in range(parts)]
    rim_refs = [refs.pop(0) for _ in range(parts)]
    proj_ref, merge_ref, weight_ref, done_ref, rewards_ref, boot_ref = refs[:6]
    values_ref, edge_ref, bias_ref = refs[6:]
    width = proj_ref.shape[0]
    turn = pl.program_id(0)
    group = 8
    rows = steps * group
    agents = values_ref.shape[1]

    @pl.when(turn == 0)
    def _():
        r = lax.broadcasted_iota(jnp.int32, (2 * rows, 2 * rows), 0) % rows
        c = lax.broadcasted_iota(jnp.int32, (2 * rows, 2 * rows), 1)
        query_step = r // group
        key_step = c // group - steps
        allowed = (
            (r % group == c % group)
            & (key_step <= query_step)
            & (key_step > query_step - WINDOW)
            & (key_step + offset_ref[0] >= 0)
        )
        bias_ref[...] = jnp.where(allowed, 0.0, -1e30)
        values_ref[...] = jnp.zeros_like(values_ref)

    def pieces(part_refs):
        whole = jnp.concatenate([ref[...].astype(f32) for ref in part_refs], axis=0)
        return [
            whole[:, at : at + group].reshape(rows, width) for at in range(0, tile, group)
        ]

    residuals = pieces(residual_refs)
    current = jnp.concatenate([rms(r).astype(bf16) for r in residuals], axis=0)
    behind = jnp.concatenate([r.astype(bf16) for r in pieces(rim_refs)], axis=0)
    projected = dot(current, proj_ref[...]).astype(bf16)
    before = dot(behind, proj_ref[:, width:]).astype(bf16)
    bias = bias_ref[...]
    mixed = []
    for at in range(0, tile * steps, rows):
        mine, past = projected[at : at + rows], before[at : at + rows]
        keys = jnp.concatenate([past[:, :width], mine[:, width : 2 * width]], axis=0)
        held = jnp.concatenate([past[:, width:], mine[:, 2 * width :]], axis=0)
        mixed.append(attend(mine[:, :width], keys, held, head_size, bias))
    merged = dot(jnp.concatenate(mixed, axis=0), merge_ref[...])
    lane = lax.broadcasted_iota(jnp.int32, (steps, group, agents), 2)
    place = lax.broadcasted_iota(jnp.int32, (steps, group, agents), 1)
    total = values_ref[...]
    for n, residual in enumerate(residuals):
        final = rms(residual + merged[n * rows : (n + 1) * rows])
        value = jnp.sum(final * weight_ref[...], axis=-1, keepdims=True)
        spot = lane == place + (turn * tile + n * group)
        total = total + jnp.sum(
            jnp.where(spot, value.reshape(steps, group, 1), 0.0), axis=1
        )
    values_ref[...] = total

    @pl.when(turn == pl.num_programs(0) - 1)
    def _():
        found = values_ref[...]
        boot = boot_ref[...]
        advantages = suffix(found, rewards_ref[...], done_ref[...], boot, jnp.zeros_like(boot))
        edge_ref[...] = jnp.concatenate([found[:1], advantages[0]], axis=0)


def time_stage(residuals, rims, offset, proj, merge, weight, done, rewards, boot):
    part_steps = [r.shape[0] for r in residuals]
    steps = sum(part_steps)
    _, agents, width = residuals[0].shape
    tile = 16
    whole = lambda i, o: (0, 0)

    def blocks(arrays):
        return [
            pl.BlockSpec((array.shape[0], tile, width), lambda i, o: (0, i, 0))
            for array in arrays
        ]

    rows = 16 * steps
    fixed = [proj, merge, weight, done, rewards, boot]
    return pl.pallas_call(
        functools.partial(time_kernel, len(residuals), steps, tile, width // HEADS),
        grid_spec=pltpu.PrefetchScalarGridSpec(
            num_scalar_prefetch=1,
            grid=(agents // tile,),
            in_specs=blocks(residuals)
            + blocks(rims)
            + [pl.BlockSpec(array.shape, whole) for array in fixed],
            out_specs=[
                pl.BlockSpec((steps, agents), whole),
                pl.BlockSpec((2, agents), whole),
            ],
            scratch_shapes=[pltpu.VMEM((rows, rows), f32)],
        ),
        out_shape=[
            jax.ShapeDtypeStruct((steps, agents), f32),
            jax.ShapeDtypeStruct((2, agents), f32),
        ],
        compiler_params=pltpu.CompilerParams(vmem_limit_bytes=VMEM_LIMIT),
        name="time_stage",
    )(offset, *residuals, *rims, *fixed)


def advantage_kernel(last_ref, values_ref, rewards_ref, done_ref, boot_ref, edge_ref, out_ref, mine_ref):
    last = last_ref[0] > 0
    arriving = edge_ref[...]
    boot = boot_ref[...]
    found = values_ref[...]
    next_value = jnp.where(last, boot, arriving[:1])
    next_advantage = jnp.where(last, 0.0, arriving[1:2])
    rows = suffix(found, rewards_ref[...], done_ref[...], next_value, next_advantage)
    out_ref[...] = jnp.concatenate(rows, axis=0)
    mine_ref[...] = jnp.concatenate([found[:1], rows[0]], axis=0)


def advantage_stage(last, values, rewards, done, boot, edge):
    return pl.pallas_call(
        advantage_kernel,
        in_specs=[pl.BlockSpec(memory_space=pltpu.SMEM)]
        + [pl.BlockSpec(memory_space=pltpu.VMEM)] * 5,
        out_specs=[pl.BlockSpec(memory_space=pltpu.VMEM)] * 2,
        out_shape=[
            jax.ShapeDtypeStruct(values.shape, f32),
            jax.ShapeDtypeStruct(edge.shape, f32),
        ],
        name="advantage_stage",
    )(last, values, rewards, done, boot, edge)


def exchange_slots(embedded, lists, capacity):
    steps, agents, width = embedded.shape
    blocks = lax.axis_size("agent")
    list_length = lists.shape[1]
    named = lists.reshape(-1)
    row_steps = jnp.arange(named.shape[0], dtype=jnp.int32) // list_length
    hits = (named[:, None] == jnp.arange(blocks, dtype=jnp.int32)[None, :]).astype(jnp.int32)
    slot = jnp.sum((jnp.cumsum(hits, axis=0) - hits) * hits, axis=1)
    slot_hits = (slot[:, None] == jnp.arange(capacity, dtype=jnp.int32)[None, :]).astype(jnp.int32)
    requests = jnp.sum(
        (hits * row_steps[:, None])[:, :, None] * slot_hits[:, None, :], axis=0
    )
    wanted = lax.all_to_all(requests, "agent", split_axis=0, concat_axis=0, tiled=True)
    outgoing = embedded[wanted.reshape(-1)].reshape(blocks, capacity, agents, width)
    arrived = lax.all_to_all(outgoing, "agent", split_axis=0, concat_axis=0, tiled=True)
    return arrived.reshape(blocks * capacity, agents, width), named * capacity + slot


def relay_sizes(steps, capacity):
    chunk = steps // 4
    chunks = [chunk] * 4
    outward = [2 * chunk] * 3 + [chunk + 1] * 2
    across = [capacity] + [2 * chunk] * 3 + [chunk + 1, chunk]
    return chunks, outward, across


def relay_codes(chunks, outward, across):
    count = len(chunks)
    return {
        "own": 0,
        "outer": [1 + k for k in range(count)],
        "inner": [1 + count + k for k in range(count)],
        "far": [1 + 2 * count + k for k in range(count)],
        "outward": [1 + 3 * count + b for b in range(len(outward))],
        "across": [1 + 3 * count + len(outward) + b for b in range(len(across))],
    }


def relay_ready(count, k):
    return max(1, k), k + 1


def plan_kernel(steps, list_length, chunks, outward, across, place_ref, lists_ref, out_ref, in_ref, flag_ref, eloc, yloc, room):
    codes = relay_codes(chunks, outward, across)
    column, row = place_ref[0], place_ref[1]
    far_side = column >= COLUMNS // 2
    mirror = lambda u: jnp.where(far_side, COLUMNS - 1 - u, u)
    me = mirror(column)
    inner = me == 1
    starts = [sum(chunks[:k]) for k in range(len(chunks))]
    e_base = [sum(outward[:b]) for b in range(len(outward))]
    y_base = [sum(outward) + sum(across[:b]) for b in range(len(across))]
    block = lambda c, r: c * ROWS + r
    entry = lambda b, t, j: lists_ref[(b * steps + t) * list_length + j]

    def clear(n, _):
        out_ref[n] = -1
        return 0

    lax.fori_loop(0, sum(outward) + sum(across), clear, 0)

    def named(dest, t, source):
        hit = entry(dest, t, 0) == source
        for j in range(1, list_length):
            hit = hit | (entry(dest, t, j) == source)
        return hit

    def choose(sizes, ready):
        batch = jnp.int32(-1)
        for b in range(len(sizes) - 1, -1, -1):
            batch = jnp.where((room[b] < sizes[b]) & (b >= ready), b, batch)
        return batch

    def base_of(bases, batch):
        base = jnp.int32(0)
        for b, value in enumerate(bases):
            base = jnp.where(batch == b, value, base)
        return base

    def empty(sizes):
        for b in range(len(sizes)):
            room[b] = 0

    for turn in range(2):
        sender = row if turn == 0 else 1 - row
        empty(outward)
        for k, count in enumerate(chunks):
            ready = (0, 0) + relay_ready(len(chunks), k)
            held = (0, codes["own"] * SPAN + starts[k], codes["inner"][k] * SPAN, codes["far"][k] * SPAN)
            for u in (1, 2, 3):

                def outer_piece(n, _, u=u, k=k, ready=ready, held=held):
                    t = starts[k] + n
                    source = block(mirror(u), sender)
                    need = named(block(mirror(0), 0), t, source)
                    for r in range(1, ROWS):
                        need = need | named(block(mirror(0), r), t, source)
                    batch = choose(outward, ready[u])
                    eloc[(turn * COLUMNS + u) * steps + t] = -1

                    @pl.when(need & (batch >= 0))
                    def _():
                        slot = room[batch]
                        room[batch] = slot + 1
                        eloc[(turn * COLUMNS + u) * steps + t] = batch * SPAN + slot
                        if turn == 0:

                            @pl.when(inner)
                            def _():
                                out_ref[base_of(e_base, batch) + slot] = held[u] + n

                    return 0

                lax.fori_loop(0, count, outer_piece, 0)

    for turn in range(2):
        sender = row if turn == 0 else 1 - row
        empty(across)
        for k, count in enumerate(chunks):
            ready = relay_ready(len(chunks), k)
            ready = (ready[0], 0) + ready
            held = (codes["outer"][k] * SPAN, codes["own"] * SPAN + starts[k], codes["inner"][k] * SPAN, codes["far"][k] * SPAN)
            for u in range(COLUMNS):

                def row_piece(n, _, u=u, k=k, ready=ready, held=held):
                    t = starts[k] + n
                    need = named(block(column, 1 - sender), t, block(mirror(u), sender))
                    if u == 0:
                        lies = jnp.int32(codes["own"] * SPAN) + t
                        when = jnp.int32(0)
                    else:
                        where = eloc[(turn * COLUMNS + u) * steps + t]
                        lies = codes["outward"][0] * SPAN + where
                        when = jnp.where(where < 0, len(across), where // SPAN + 1)
                    when = jnp.where(inner, ready[u], when)
                    lies = jnp.where(inner, held[u] + n, lies)
                    batch = choose(across, when)
                    yloc[(turn * COLUMNS + u) * steps + t] = -1

                    @pl.when(need & (batch >= 0))
                    def _():
                        slot = room[batch]
                        room[batch] = slot + 1
                        yloc[(turn * COLUMNS + u) * steps + t] = batch * SPAN + slot
                        if turn == 0:
                            out_ref[base_of(y_base, batch) + slot] = lies

                    return 0

                lax.fori_loop(0, count, row_piece, 0)

    flag_ref[0] = 0
    for k, count in enumerate(chunks):

        def listed_piece(n, _, k=k):
            t = starts[k] + n // list_length
            source = entry(block(column, row), t, n % list_length)
            u = mirror(source // ROWS)
            same = source % ROWS == row
            e = eloc[u * steps + t]
            y = yloc[(COLUMNS + u) * steps + t]
            code = jnp.where(u == 0, codes["outer"][k], jnp.where(u == 2, codes["inner"][k], codes["far"][k]))
            direct = jnp.where(inner, code * SPAN + t - starts[k], codes["outward"][0] * SPAN + e)
            direct = jnp.where(u == me, codes["own"] * SPAN + t, direct)
            local = inner | (u == me)
            bad = jnp.where(
                same,
                jnp.logical_not(local) & ((e < 0) | (e // SPAN > min(k + 2, len(outward) - 1))),
                (y < 0) | (y // SPAN > k + 2),
            )
            place = jnp.where(same, direct, codes["across"][0] * SPAN + y)
            in_ref[t * list_length + n % list_length] = jnp.where(bad, codes["own"] * SPAN, place)

            @pl.when(bad)
            def _():
                flag_ref[0] = 1

            return 0

        lax.fori_loop(0, count * list_length, listed_piece, 0)


def plan(lists_all, place, steps, list_length, chunks, outward, across):
    smem = pl.BlockSpec(memory_space=pltpu.SMEM)
    slots = sum(outward) + sum(across)
    return pl.pallas_call(
        functools.partial(plan_kernel, steps, list_length, chunks, outward, across),
        in_specs=[smem, smem],
        out_specs=[smem] * 3,
        out_shape=[
            jax.ShapeDtypeStruct((slots,), jnp.int32),
            jax.ShapeDtypeStruct((steps * list_length,), jnp.int32),
            jax.ShapeDtypeStruct((1,), jnp.int32),
        ],
        scratch_shapes=[
            pltpu.SMEM((2 * COLUMNS * steps,), jnp.int32),
            pltpu.SMEM((2 * COLUMNS * steps,), jnp.int32),
            pltpu.SMEM((max(len(outward), len(across)),), jnp.int32),
        ],
        name="plan",
    )(place, lists_all)


def column_pairs(moves):
    return [(a * ROWS + r, b * ROWS + r) for a, b in moves for r in range(ROWS)]


def relay(embedded, lists, capacity):
    steps, agents, width = embedded.shape
    list_length = lists.shape[1]
    chunks, outward, across = relay_sizes(steps, capacity)
    codes = relay_codes(chunks, outward, across)
    starts = [sum(chunks[:k]) for k in range(len(chunks))]
    index = lax.axis_index("agent")
    place = jnp.stack([index // ROWS, index % ROWS]).astype(jnp.int32)
    send = lambda value, pairs: lax.ppermute(value, "agent", pairs)
    inward = column_pairs([(0, 1), (3, 2)])
    swap = column_pairs([(1, 2), (2, 1)])
    away = column_pairs([(1, 0), (2, 3)])
    over = [(c * ROWS + r, c * ROWS + 1 - r) for c in range(COLUMNS) for r in range(ROWS)]
    everyone = lax.all_gather(lists.reshape(-1), "agent", axis=0, tiled=True)
    out_table, in_table, flag = plan(
        everyone, place, steps, list_length, chunks, outward, across
    )
    arrays = {codes["own"]: embedded}

    def begin(k, part):
        arrays[codes["outer"][k]] = send(part, inward)
        arrays[codes["inner"][k]] = send(part, swap)
        arrays[codes["far"][k]] = send(arrays[codes["outer"][k]], swap)

    def own_part(k):
        return embedded[starts[k] : starts[k] + chunks[k]]

    for k in range(len(chunks)):
        begin(k, own_part(k))
    e_base = [sum(outward[:b]) for b in range(len(outward))]
    y_base = [sum(outward) + sum(across[:b]) for b in range(len(across))]
    for stage in range(len(across)):
        known = {codes["own"]: embedded}
        for k in range(len(chunks)):
            near, far = relay_ready(len(chunks), k)
            if near <= stage:
                known[codes["outer"][k]] = arrays[codes["outer"][k]]
                known[codes["inner"][k]] = arrays[codes["inner"][k]]
            if far <= stage:
                known[codes["far"][k]] = arrays[codes["far"][k]]
        for b in range(min(stage, len(outward))):
            known[codes["outward"][b]] = arrays[codes["outward"][b]]
        parts = [(e_base[stage], outward[stage])] if stage < len(outward) else []
        packed = pack(out_table, known, tuple(parts + [(y_base[stage], across[stage])]))
        if parts:
            arrays[codes["outward"][stage]] = send(packed[0], away)
        arrays[codes["across"][stage]] = send(packed[-1], over)
    work = []
    for k in range(len(chunks)):
        wanted = [codes["own"], codes["outer"][k], codes["inner"][k], codes["far"][k]]
        wanted += codes["outward"][: k + 3] + codes["across"][: k + 3]
        work.append((starts[k], chunks[k], {code: arrays[code] for code in wanted}))
    return work, in_table, flag


def body(
    embedded,
    block_lists,
    done_flags,
    rewards,
    bootstrap,
    agent_proj,
    agent_merge,
    time_proj,
    time_merge,
    value_weight,
):
    steps, agents, width = embedded.shape
    list_length = block_lists.shape[2]
    blocks = lax.axis_size("agent")
    lists = block_lists[0]
    capacity = max(2, (2 * steps * list_length + blocks - 1) // blocks)
    spans = lax.axis_size("tm")
    index = lax.axis_index("tm")
    offset = (index * steps).astype(jnp.int32).reshape(1)
    boot = bootstrap.reshape(1, agents)
    forward = [(i, i + 1) for i in range(spans - 1)]
    backward = [(i + 1, i) for i in range(spans - 1)]

    def finish(work, table):
        residuals, rims = [], []
        for first, count, arrays in work:
            residual, normed = agent_stage(
                embedded, arrays, table, first, count, list_length, agent_proj, agent_merge
            )
            residuals.append(residual)
            rims.append(lax.ppermute(normed, "tm", forward))
        values, edge = time_stage(
            residuals,
            rims,
            offset,
            time_proj,
            time_merge,
            value_weight.reshape(1, width),
            done_flags,
            rewards,
            boot,
        )
        last = (index == spans - 1).astype(jnp.int32).reshape(1)
        for _ in range(max(1, spans - 1)):
            arriving = lax.ppermute(edge, "tm", backward)
            advantages, edge = advantage_stage(last, values, rewards, done_flags, boot, arriving)
        return values, advantages

    def padded():
        pool, where = exchange_slots(embedded, lists, capacity)
        return finish([(0, steps, {1: pool})], where + SPAN)

    if blocks != COLUMNS * ROWS or steps % 4:
        return padded()
    work, table, flag = relay(embedded, lists, capacity)
    crowded = lax.pmax(flag[0], ("groups", "agent", "tm"))
    found = finish(work, table)
    return lax.cond(crowded > 0, padded, lambda: found)


def solution(mesh):
    placed = (
        P(("groups", "tm"), "agent", None),
        P(("groups", "agent"), "tm", None),
        P(("groups", "tm"), "agent"),
        P(("groups", "tm"), "agent"),
        P(("groups", "agent")),
        P(),
        P(),
        P(),
        P(),
        P(),
    )
    return jax.shard_map(
        body,
        mesh=mesh,
        in_specs=placed,
        out_specs=(P(("groups", "tm"), "agent"), P(("groups", "tm"), "agent")),
        check_vma=False,
    )
```

```python
import functools

import jax
import jax.numpy as jnp
from jax import lax
from jax.experimental import pallas as pl
from jax.experimental.pallas import tpu as pltpu
from jax.sharding import PartitionSpec as P

HEADS = 8
WINDOW = 16
discount = 0.9997
trace_decay = 0.995
epsilon = 1e-06
bf16 = jnp.bfloat16
f32 = jnp.float32
VMEM_LIMIT = 48 * 1024 * 1024
SPAN = 1024
COLUMNS = 4
ROWS = 2


def rms(values):
    return values * lax.rsqrt(jnp.mean(values * values, axis=-1, keepdims=True) + epsilon)


def dot(a, b):
    return jnp.dot(a, b, preferred_element_type=f32)


def dot_t(a, b):
    return lax.dot_general(a, b, (((1,), (1,)), ((), ())), preferred_element_type=f32)


def attend(queries, keys, values, head_size, bias):
    rows, width = queries.shape
    scale = head_size ** (-0.5)
    pair = 2 * head_size
    lane = lax.broadcasted_iota(jnp.int32, (rows, pair), 1)
    first = lane < head_size
    ones = jnp.ones((keys.shape[0], pair), bf16)
    mixed = []
    for at in range(0, width, pair):
        both = queries[:, at : at + pair]
        none = jnp.zeros_like(both)
        stacked = jnp.concatenate(
            [jnp.where(first, both, none), jnp.where(first, none, both)], axis=0
        )
        scores = dot_t(stacked, keys[:, at : at + pair]) * scale
        if bias is not None:
            scores = scores + bias
        weights = jnp.exp(scores - jnp.max(scores, axis=-1, keepdims=True)).astype(bf16)
        summed = dot(weights, jnp.concatenate([values[:, at : at + pair], ones], axis=1))
        result = summed[:, :pair] / summed[:, pair:]
        mixed.append(jnp.where(first, result[:rows], result[rows:]).astype(bf16))
    return jnp.concatenate(mixed, axis=1)


def fetch(entry, arrays, target, sem):
    for code, ref in arrays.items():

        @pl.when(entry // SPAN == code)
        def _(ref=ref):
            pltpu.make_async_copy(ref.at[entry % SPAN], target, sem).start()


def agent_kernel(list_length, first_step, codes, idle, head_size, table_ref, own_ref, *refs):
    arrays = dict(zip(codes, refs))
    proj_ref, merge_ref, residual_ref, normed_ref, held_ref, sems = refs[len(codes) + idle :]
    width = own_ref.shape[-1]
    turn = pl.program_id(0)

    def begin(step):
        for j in range(list_length):
            slot = step % 2
            entry = table_ref[(first_step + step) * list_length + j]
            fetch(entry, arrays, held_ref.at[slot, j], sems.at[slot, j])

    @pl.when(turn == 0)
    def _():
        begin(turn)

    @pl.when(turn + 1 < pl.num_programs(0))
    def _():
        begin(turn + 1)

    own = own_ref[0].astype(f32)
    rows = [rms(own).astype(bf16)]
    queries = dot(rows[0], proj_ref[:, :width]).astype(bf16)
    slot = turn % 2
    for j in range(list_length):
        pltpu.make_async_copy(refs[0].at[0], held_ref.at[slot, j], sems.at[slot, j]).wait()
        rows.append(rms(held_ref[slot, j].astype(f32)).astype(bf16))
    keyvals = dot(jnp.concatenate(rows, axis=0), proj_ref[:, width:]).astype(bf16)
    mixed = attend(queries, keyvals[:, :width], keyvals[:, width:], head_size, None)
    residual = own + dot(mixed, merge_ref[...])
    residual_ref[0] = residual
    normed_ref[0] = rms(residual).astype(bf16)


def agent_stage(embedded, arrays, table, first_step, steps, list_length, proj, merge, after=()):
    _, agents, width = embedded.shape
    piece = (1, agents, width)
    whole = lambda i, w: (0, 0)
    flops = 2 * steps * agents * width * width * (4 + 2 * list_length + 2 * (1 + list_length))
    return pl.pallas_call(
        functools.partial(
            agent_kernel, list_length, first_step, tuple(arrays), len(after), width // HEADS
        ),
        grid_spec=pltpu.PrefetchScalarGridSpec(
            num_scalar_prefetch=1,
            grid=(steps,),
            in_specs=[pl.BlockSpec(piece, lambda i, w: (first_step + i, 0, 0))]
            + [pl.BlockSpec(memory_space=pl.ANY)] * (len(arrays) + len(after))
            + [pl.BlockSpec(proj.shape, whole), pl.BlockSpec(merge.shape, whole)],
            out_specs=[pl.BlockSpec(piece, lambda i, w: (i, 0, 0))] * 2,
            scratch_shapes=[
                pltpu.VMEM((2, list_length, agents, width), bf16),
                pltpu.SemaphoreType.DMA((2, list_length)),
            ],
        ),
        out_shape=[
            jax.ShapeDtypeStruct((steps, agents, width), f32),
            jax.ShapeDtypeStruct((steps, agents, width), bf16),
        ],
        compiler_params=pltpu.CompilerParams(vmem_limit_bytes=VMEM_LIMIT),
        cost_estimate=pl.CostEstimate(
            flops=5 * flops, bytes_accessed=steps * agents * width * 12, transcendentals=0
        ),
        name="agent_stage",
    )(table, embedded, *arrays.values(), *after, proj, merge)


def pack_kernel(codes, parts, idle, table_ref, *refs):
    arrays = dict(zip(codes, refs))
    outs, (held_ref, in_sems, out_sems) = refs[len(codes) + idle : -3], refs[-3:]
    slots = []
    for out, (offset, count, first) in zip(outs, parts):
        slots += [(offset, first, n, out.at[n]) for n in range(count)]

    def guarded(offset, n, action):
        if offset is None:
            action()
        else:
            pl.when(table_ref[offset + n] >= 0)(action)

    for at, (offset, first, n, _) in enumerate(slots):
        if offset is None:
            own = arrays[0].at[first + n]
            pltpu.make_async_copy(own, held_ref.at[at], in_sems.at[at]).start()
        else:
            fetch(table_ref[offset + n], arrays, held_ref.at[at], in_sems.at[at])
    for at, (offset, first, n, target) in enumerate(slots):

        def pass_on(at=at, target=target):
            pltpu.make_async_copy(refs[0].at[0], held_ref.at[at], in_sems.at[at]).wait()
            pltpu.make_async_copy(held_ref.at[at], target, out_sems.at[at]).start()

        guarded(offset, n, pass_on)
    for at, (offset, first, n, target) in enumerate(slots):

        def finish(at=at, target=target):
            pltpu.make_async_copy(held_ref.at[at], target, out_sems.at[at]).wait()

        guarded(offset, n, finish)


def pack(table, arrays, parts, after=()):
    piece = next(iter(arrays.values())).shape[1:]
    slots = sum(count for _, count, _ in parts)
    return pl.pallas_call(
        functools.partial(pack_kernel, tuple(arrays), tuple(parts), len(after)),
        in_specs=[pl.BlockSpec(memory_space=pltpu.SMEM)]
        + [pl.BlockSpec(memory_space=pl.ANY)] * (len(arrays) + len(after)),
        out_specs=[pl.BlockSpec(memory_space=pl.ANY)] * len(parts),
        out_shape=[jax.ShapeDtypeStruct((count,) + piece, bf16) for _, count, _ in parts],
        scratch_shapes=[
            pltpu.VMEM((slots,) + piece, bf16),
            pltpu.SemaphoreType.DMA((slots,)),
            pltpu.SemaphoreType.DMA((slots,)),
        ],
        cost_estimate=pl.CostEstimate(
            flops=0, bytes_accessed=4 * slots * piece[0] * piece[1], transcendentals=0
        ),
        compiler_params=pltpu.CompilerParams(vmem_limit_bytes=VMEM_LIMIT),
        name="pack",
    )(table, *arrays.values(), *after)


def suffix(values, rewards, done, next_value, next_advantage):
    steps = values.shape[0]
    living = 1.0 - done.astype(f32)
    running, following, rows = next_advantage, next_value, [None] * steps
    for step in range(steps - 1, -1, -1):
        alive = living[step : step + 1]
        value = values[step : step + 1]
        change = rewards[step : step + 1] + discount * alive * following - value
        running = change + discount * trace_decay * alive * running
        rows[step] = running
        following = value
    return rows


def time_kernel(parts, steps, tile, head_size, offset_ref, *refs):
    refs = list(refs)
    residual_refs = [refs.pop(0) for _ in range(parts)]
    rim_refs = [refs.pop(0) for _ in range(parts)]
    proj_ref, merge_ref, weight_ref, done_ref, rewards_ref, boot_ref = refs[:6]
    values_ref, edge_ref, bias_ref = refs[6:]
    width = proj_ref.shape[0]
    turn = pl.program_id(0)
    group = 8
    rows = steps * group
    agents = values_ref.shape[1]

    @pl.when(turn == 0)
    def _():
        r = lax.broadcasted_iota(jnp.int32, (2 * rows, 2 * rows), 0) % rows
        c = lax.broadcasted_iota(jnp.int32, (2 * rows, 2 * rows), 1)
        query_step = r // group
        key_step = c // group - steps
        allowed = (
            (r % group == c % group)
            & (key_step <= query_step)
            & (key_step > query_step - WINDOW)
            & (key_step + offset_ref[0] >= 0)
        )
        bias_ref[...] = jnp.where(allowed, 0.0, -1e30)
        values_ref[...] = jnp.zeros_like(values_ref)

    def pieces(part_refs):
        whole = jnp.concatenate([ref[...].astype(f32) for ref in part_refs], axis=0)
        return [
            whole[:, at : at + group].reshape(rows, width) for at in range(0, tile, group)
        ]

    residuals = pieces(residual_refs)
    current = jnp.concatenate([rms(r).astype(bf16) for r in residuals], axis=0)
    behind = jnp.concatenate([r.astype(bf16) for r in pieces(rim_refs)], axis=0)
    projected = dot(current, proj_ref[...]).astype(bf16)
    before = dot(behind, proj_ref[:, width:]).astype(bf16)
    bias = bias_ref[...]
    mixed = []
    for at in range(0, tile * steps, rows):
        mine, past = projected[at : at + rows], before[at : at + rows]
        keys = jnp.concatenate([past[:, :width], mine[:, width : 2 * width]], axis=0)
        held = jnp.concatenate([past[:, width:], mine[:, 2 * width :]], axis=0)
        mixed.append(attend(mine[:, :width], keys, held, head_size, bias))
    merged = dot(jnp.concatenate(mixed, axis=0), merge_ref[...])
    lane = lax.broadcasted_iota(jnp.int32, (steps, group, agents), 2)
    place = lax.broadcasted_iota(jnp.int32, (steps, group, agents), 1)
    total = values_ref[...]
    for n, residual in enumerate(residuals):
        final = rms(residual + merged[n * rows : (n + 1) * rows])
        value = jnp.sum(final * weight_ref[...], axis=-1, keepdims=True)
        spot = lane == place + (turn * tile + n * group)
        total = total + jnp.sum(
            jnp.where(spot, value.reshape(steps, group, 1), 0.0), axis=1
        )
    values_ref[...] = total

    @pl.when(turn == pl.num_programs(0) - 1)
    def _():
        found = values_ref[...]
        boot = boot_ref[...]
        advantages = suffix(found, rewards_ref[...], done_ref[...], boot, jnp.zeros_like(boot))
        edge_ref[...] = jnp.concatenate([found[:1], advantages[0]], axis=0)


def time_stage(residuals, rims, offset, proj, merge, weight, done, rewards, boot):
    part_steps = [r.shape[0] for r in residuals]
    steps = sum(part_steps)
    _, agents, width = residuals[0].shape
    tile = 16
    whole = lambda i, o: (0, 0)

    def blocks(arrays):
        return [
            pl.BlockSpec((array.shape[0], tile, width), lambda i, o: (0, i, 0))
            for array in arrays
        ]

    rows = 16 * steps
    fixed = [proj, merge, weight, done, rewards, boot]
    return pl.pallas_call(
        functools.partial(time_kernel, len(residuals), steps, tile, width // HEADS),
        grid_spec=pltpu.PrefetchScalarGridSpec(
            num_scalar_prefetch=1,
            grid=(agents // tile,),
            in_specs=blocks(residuals)
            + blocks(rims)
            + [pl.BlockSpec(array.shape, whole) for array in fixed],
            out_specs=[
                pl.BlockSpec((steps, agents), whole),
                pl.BlockSpec((2, agents), whole),
            ],
            scratch_shapes=[pltpu.VMEM((rows, rows), f32)],
        ),
        out_shape=[
            jax.ShapeDtypeStruct((steps, agents), f32),
            jax.ShapeDtypeStruct((2, agents), f32),
        ],
        compiler_params=pltpu.CompilerParams(vmem_limit_bytes=VMEM_LIMIT),
        name="time_stage",
    )(offset, *residuals, *rims, *fixed)


def advantage_kernel(last_ref, values_ref, rewards_ref, done_ref, boot_ref, edge_ref, out_ref, mine_ref):
    last = last_ref[0] > 0
    arriving = edge_ref[...]
    boot = boot_ref[...]
    found = values_ref[...]
    next_value = jnp.where(last, boot, arriving[:1])
    next_advantage = jnp.where(last, 0.0, arriving[1:2])
    rows = suffix(found, rewards_ref[...], done_ref[...], next_value, next_advantage)
    out_ref[...] = jnp.concatenate(rows, axis=0)
    mine_ref[...] = jnp.concatenate([found[:1], rows[0]], axis=0)


def advantage_stage(last, values, rewards, done, boot, edge):
    return pl.pallas_call(
        advantage_kernel,
        in_specs=[pl.BlockSpec(memory_space=pltpu.SMEM)]
        + [pl.BlockSpec(memory_space=pltpu.VMEM)] * 5,
        out_specs=[pl.BlockSpec(memory_space=pltpu.VMEM)] * 2,
        out_shape=[
            jax.ShapeDtypeStruct(values.shape, f32),
            jax.ShapeDtypeStruct(edge.shape, f32),
        ],
        name="advantage_stage",
    )(last, values, rewards, done, boot, edge)


def exchange_slots(embedded, lists, capacity):
    steps, agents, width = embedded.shape
    blocks = lax.axis_size("agent")
    list_length = lists.shape[1]
    named = lists.reshape(-1)
    row_steps = jnp.arange(named.shape[0], dtype=jnp.int32) // list_length
    hits = (named[:, None] == jnp.arange(blocks, dtype=jnp.int32)[None, :]).astype(jnp.int32)
    slot = jnp.sum((jnp.cumsum(hits, axis=0) - hits) * hits, axis=1)
    slot_hits = (slot[:, None] == jnp.arange(capacity, dtype=jnp.int32)[None, :]).astype(jnp.int32)
    requests = jnp.sum(
        (hits * row_steps[:, None])[:, :, None] * slot_hits[:, None, :], axis=0
    )
    wanted = lax.all_to_all(requests, "agent", split_axis=0, concat_axis=0, tiled=True)
    outgoing = embedded[wanted.reshape(-1)].reshape(blocks, capacity, agents, width)
    arrived = lax.all_to_all(outgoing, "agent", split_axis=0, concat_axis=0, tiled=True)
    return arrived.reshape(blocks * capacity, agents, width), named * capacity + slot


OUTWARD_READY = {1: (0, 1), 2: (1, 3), 3: (2, 4)}
ACROSS_READY = {0: (1, 2), 1: (0, 0), 2: (1, 3), 3: (2, 4)}
OUTWARD_DUE = (3, 4)
ACROSS_DUE = (3, 5)


def relay_sizes(steps, capacity):
    half, quarter = steps // 2, steps // 4
    chunks = [half, half]
    outward = [half, half, half, half - 1, half]
    across = [capacity - 2, half - 1, half, half - 1, quarter + 2, half - 1]
    return chunks, outward, across


def relay_codes(chunks, outward, across):
    count = len(chunks)
    return {
        "own": 0,
        "outer": [1 + 3 * count + k for k in range(count)],
        "inner": [1 + count + k for k in range(count)],
        "far": [1 + 2 * count + k for k in range(count)],
        "outward": [1 + 3 * count + b for b in range(len(outward))],
        "across": [1 + 3 * count + len(outward) + b for b in range(len(across))],
    }


def plan_kernel(steps, list_length, chunks, outward, across, place_ref, lists_ref, out_ref, in_ref, flag_ref, eloc, yloc, room):
    codes = relay_codes(chunks, outward, across)
    column, row = place_ref[0], place_ref[1]
    far_side = column >= COLUMNS // 2
    mirror = lambda u: jnp.where(far_side, COLUMNS - 1 - u, u)
    me = mirror(column)
    inner = me == 1
    starts = [sum(chunks[:k]) for k in range(len(chunks))]
    e_base = [sum(outward[:b]) for b in range(len(outward))]
    y_base = [sum(outward) + sum(across[:b]) for b in range(len(across))]
    block = lambda c, r: c * ROWS + r
    entry = lambda b, t, j: lists_ref[(b * steps + t) * list_length + j]

    def clear(n, _):
        out_ref[n] = -1
        return 0

    lax.fori_loop(0, sum(outward) + sum(across), clear, 0)

    @pl.when(me == 0)
    def _():
        for n in range(chunks[1]):
            out_ref[e_base[1] + n] = codes["own"] * SPAN + starts[1] + n

    def named(dest, t, source):
        hit = entry(dest, t, 0) == source
        for j in range(1, list_length):
            hit = hit | (entry(dest, t, j) == source)
        return hit

    def choose(sizes, ready):
        batch = jnp.int32(-1)
        for b in range(len(sizes) - 1, -1, -1):
            batch = jnp.where((room[b] < sizes[b]) & (b >= ready), b, batch)
        return batch

    def base_of(bases, batch):
        base = jnp.int32(0)
        for b, value in enumerate(bases):
            base = jnp.where(batch == b, value, base)
        return base

    def empty(sizes):
        for b in range(len(sizes)):
            room[b] = 0

    for turn in range(2):
        sender = row if turn == 0 else 1 - row
        empty(outward)
        room[0] = outward[0]
        for k, count in enumerate(chunks):
            held = (0, codes["own"] * SPAN + starts[k], codes["inner"][k] * SPAN, codes["far"][k] * SPAN)
            for u in (1, 2, 3):

                def first_piece(n, _):
                    eloc[(turn * COLUMNS + 1) * steps + n] = n
                    return 0

                if u == 1 and k == 0:
                    lax.fori_loop(0, count, first_piece, 0)
                    continue

                def outer_piece(n, _, u=u, k=k, held=held):
                    t = starts[k] + n
                    source = block(mirror(u), sender)
                    need = named(block(mirror(0), 0), t, source)
                    for r in range(1, ROWS):
                        need = need | named(block(mirror(0), r), t, source)
                    batch = choose(outward, OUTWARD_READY[u][k])
                    eloc[(turn * COLUMNS + u) * steps + t] = -1

                    @pl.when(need & (batch >= 0))
                    def _():
                        slot = room[batch]
                        room[batch] = slot + 1
                        eloc[(turn * COLUMNS + u) * steps + t] = batch * SPAN + slot
                        if turn == 0:

                            @pl.when(inner)
                            def _():
                                out_ref[base_of(e_base, batch) + slot] = held[u] + n

                    return 0

                lax.fori_loop(0, count, outer_piece, 0)

    for turn in range(2):
        sender = row if turn == 0 else 1 - row
        empty(across)
        for k, count in enumerate(chunks):
            held = (codes["outer"][k] * SPAN, codes["own"] * SPAN + starts[k], codes["inner"][k] * SPAN, codes["far"][k] * SPAN)
            for u in range(COLUMNS):

                def row_piece(n, _, u=u, k=k, held=held):
                    t = starts[k] + n
                    need = named(block(column, 1 - sender), t, block(mirror(u), sender))
                    if u == 0:
                        lies = jnp.int32(codes["own"] * SPAN) + t
                        when = jnp.int32(0)
                    else:
                        where = eloc[(turn * COLUMNS + u) * steps + t]
                        lies = codes["outward"][0] * SPAN + where
                        when = jnp.where(where < 0, len(across), where // SPAN + 1)
                    when = jnp.where(inner, ACROSS_READY[u][k], when)
                    lies = jnp.where(inner, held[u] + n, lies)
                    batch = choose(across, when)
                    yloc[(turn * COLUMNS + u) * steps + t] = -1

                    @pl.when(need & (batch >= 0))
                    def _():
                        slot = room[batch]
                        room[batch] = slot + 1
                        yloc[(turn * COLUMNS + u) * steps + t] = batch * SPAN + slot
                        if turn == 0:
                            out_ref[base_of(y_base, batch) + slot] = lies

                    return 0

                lax.fori_loop(0, count, row_piece, 0)

    flag_ref[0] = 0
    for k, count in enumerate(chunks):

        def listed_piece(n, _, k=k):
            t = starts[k] + n // list_length
            source = entry(block(column, row), t, n % list_length)
            u = mirror(source // ROWS)
            same = source % ROWS == row
            e = eloc[u * steps + t]
            y = yloc[(COLUMNS + u) * steps + t]
            code = jnp.where(u == 0, codes["outer"][k], jnp.where(u == 2, codes["inner"][k], codes["far"][k]))
            direct = jnp.where(inner, code * SPAN + t - starts[k], codes["outward"][0] * SPAN + e)
            direct = jnp.where(u == me, codes["own"] * SPAN + t, direct)
            local = inner | (u == me)
            bad = jnp.where(
                same,
                jnp.logical_not(local) & ((e < 0) | (e // SPAN > OUTWARD_DUE[k])),
                (y < 0) | (y // SPAN > ACROSS_DUE[k]),
            )
            place = jnp.where(same, direct, codes["across"][0] * SPAN + y)
            in_ref[t * list_length + n % list_length] = jnp.where(bad, codes["own"] * SPAN, place)

            @pl.when(bad)
            def _():
                flag_ref[0] = 1

            return 0

        lax.fori_loop(0, count * list_length, listed_piece, 0)


def plan(lists_all, place, steps, list_length, chunks, outward, across):
    smem = pl.BlockSpec(memory_space=pltpu.SMEM)
    slots = sum(outward) + sum(across)
    return pl.pallas_call(
        functools.partial(plan_kernel, steps, list_length, chunks, outward, across),
        in_specs=[smem, smem],
        out_specs=[smem] * 3,
        out_shape=[
            jax.ShapeDtypeStruct((slots,), jnp.int32),
            jax.ShapeDtypeStruct((steps * list_length,), jnp.int32),
            jax.ShapeDtypeStruct((1,), jnp.int32),
        ],
        scratch_shapes=[
            pltpu.SMEM((2 * COLUMNS * steps,), jnp.int32),
            pltpu.SMEM((2 * COLUMNS * steps,), jnp.int32),
            pltpu.SMEM((max(len(outward), len(across)),), jnp.int32),
        ],
        name="plan",
    )(place, lists_all)


def shared(value, axes):
    count = lax.axis_size(axes)
    rows = jnp.broadcast_to(value[None], (count,) + value.shape)
    return lax.all_to_all(rows, axes, split_axis=0, concat_axis=0, tiled=True)


def column_pairs(moves):
    return [(a * ROWS + r, b * ROWS + r) for a, b in moves for r in range(ROWS)]


def relay(embedded, lists, capacity, attention):
    steps, agents, width = embedded.shape
    list_length = lists.shape[1]
    chunks, outward, across = relay_sizes(steps, capacity)
    codes = relay_codes(chunks, outward, across)
    starts = [sum(chunks[:k]) for k in range(len(chunks))]
    e_base = [sum(outward[:b]) for b in range(len(outward))]
    y_base = [sum(outward) + sum(across[:b]) for b in range(len(across))]
    index = lax.axis_index("agent")
    place = jnp.stack([index // ROWS, index % ROWS]).astype(jnp.int32)
    send = lambda value, pairs: lax.ppermute(value, "agent", pairs)
    edges = column_pairs([(0, 1), (1, 0), (2, 3), (3, 2)])
    swap = column_pairs([(1, 2), (2, 1)])
    over = [(c * ROWS + r, c * ROWS + 1 - r) for c in range(COLUMNS) for r in range(ROWS)]
    arrays = {codes["own"]: embedded}

    def pick(names):
        return {code: arrays[code] for code in names}

    def outward_part(stage):
        return (e_base[stage], outward[stage], None)

    def across_part(stage):
        return (y_base[stage], across[stage], None)

    reads = [[codes["own"]] for _ in across]
    for stage in range(1, len(across)):
        reads[stage] += codes["outward"][: min(stage, len(outward))]
        for name, u in (("inner", 2), ("far", 3)):
            for k in range(len(chunks)):
                if OUTWARD_READY[u][k] <= stage:
                    reads[stage].append(codes[name][k])

    settled = [(), (), (0, 1)] + [(stage - 1,) for stage in range(3, len(across))]
    first = embedded[: chunks[0]]
    arrays[codes["outward"][0]] = send(first, edges)
    arrays[codes["inner"][0]] = send(first, swap)
    everyone = shared(lists.reshape(-1), "agent").reshape(-1)
    out_table, in_table, flag = plan(
        everyone, place, steps, list_length, chunks, outward, across
    )
    (packed,) = pack(out_table, pick(reads[0]), [across_part(0)])
    arrays[codes["across"][0]] = send(packed, over)
    arrays[codes["far"][0]] = send(arrays[codes["outward"][0]], swap)
    done, after = [], ()
    for stage in range(1, len(across)):
        parts = [across_part(stage)]
        if stage < len(outward):
            parts.append(outward_part(stage))
        if stage == 1:
            parts.append((None, chunks[1], starts[1]))
        if stage == len(across) - 1:
            done.append(attention(0, chunks[0], due(arrays, codes, 0), in_table, after))
            after = (done[0][0],)
        else:
            after += tuple(arrays[codes["across"][b]] for b in settled[stage])
        packed = pack(out_table, pick(reads[stage]), parts, after)
        arrays[codes["across"][stage]] = send(packed[0], over)
        if stage < len(outward):
            arrays[codes["outward"][stage]] = send(packed[1], edges)
        if stage == 1:
            arrays[codes["inner"][1]] = send(packed[2], swap)
            arrays[codes["far"][1]] = send(arrays[codes["outward"][1]], swap)
            crowded = jnp.max(shared(flag, ("groups", "agent", "tm")))
        after = (crowded.reshape(1),) if stage == 2 else ()
    done.append(attention(starts[1], chunks[1], due(arrays, codes, 1), in_table, ()))
    return done, crowded


def due(arrays, codes, k):
    wanted = [codes["own"], codes["inner"][k], codes["far"][k]]
    wanted += codes["outward"][: OUTWARD_DUE[k] + 1] + codes["across"][: ACROSS_DUE[k] + 1]
    return {code: arrays[code] for code in wanted}


def body(
    embedded,
    block_lists,
    done_flags,
    rewards,
    bootstrap,
    agent_proj,
    agent_merge,
    time_proj,
    time_merge,
    value_weight,
):
    steps, agents, width = embedded.shape
    list_length = block_lists.shape[2]
    blocks = lax.axis_size("agent")
    lists = block_lists[0]
    capacity = max(2, (2 * steps * list_length + blocks - 1) // blocks)
    spans = lax.axis_size("tm")
    index = lax.axis_index("tm")
    offset = (index * steps).astype(jnp.int32).reshape(1)
    boot = bootstrap.reshape(1, agents)
    forward = [(i, i + 1) for i in range(spans - 1)]
    backward = [(i + 1, i) for i in range(spans - 1)]

    def attention(first, count, arrays, table, after=()):
        residual, normed = agent_stage(
            embedded, arrays, table, first, count, list_length, agent_proj, agent_merge, after
        )
        return residual, lax.ppermute(normed, "tm", forward)

    def finish(done):
        residuals, rims = [part[0] for part in done], [part[1] for part in done]
        values, edge = time_stage(
            residuals,
            rims,
            offset,
            time_proj,
            time_merge,
            value_weight.reshape(1, width),
            done_flags,
            rewards,
            boot,
        )
        last = (index == spans - 1).astype(jnp.int32).reshape(1)
        for _ in range(max(1, spans - 1)):
            arriving = lax.ppermute(edge, "tm", backward)
            advantages, edge = advantage_stage(last, values, rewards, done_flags, boot, arriving)
        return values, advantages

    def padded():
        pool, where = exchange_slots(embedded, lists, capacity)
        return finish([attention(0, steps, {1: pool}, where + SPAN)])

    if blocks != COLUMNS * ROWS or steps % 4:
        return padded()
    done, crowded = relay(embedded, lists, capacity, attention)
    found = finish(done)
    return lax.cond(crowded > 0, padded, lambda: found)


def solution(mesh):
    placed = (
        P(("groups", "tm"), "agent", None),
        P(("groups", "agent"), "tm", None),
        P(("groups", "tm"), "agent"),
        P(("groups", "tm"), "agent"),
        P(("groups", "agent")),
        P(),
        P(),
        P(),
        P(),
        P(),
    )
    return jax.shard_map(
        body,
        mesh=mesh,
        in_specs=placed,
        out_specs=(P(("groups", "tm"), "agent"), P(("groups", "tm"), "agent")),
        check_vma=False,
    )
```

```python
import functools

import jax
import jax.numpy as jnp
from jax import lax
from jax.experimental import pallas as pl
from jax.experimental.pallas import tpu as pltpu
from jax.sharding import PartitionSpec as P

HEADS = 8
WINDOW = 16
discount = 0.9997
trace_decay = 0.995
epsilon = 1e-06
bf16 = jnp.bfloat16
f32 = jnp.float32
VMEM_LIMIT = 48 * 1024 * 1024
SPAN = 1024
COLUMNS = 4
ROWS = 2


def rms(values):
    return values * lax.rsqrt(jnp.mean(values * values, axis=-1, keepdims=True) + epsilon)


def dot(a, b):
    return jnp.dot(a, b, preferred_element_type=f32)


def dot_t(a, b):
    return lax.dot_general(a, b, (((1,), (1,)), ((), ())), preferred_element_type=f32)


def attend(queries, keys, values, head_size, bias):
    rows, width = queries.shape
    scale = head_size ** (-0.5)
    pair = 2 * head_size
    lane = lax.broadcasted_iota(jnp.int32, (rows, pair), 1)
    first = lane < head_size
    ones = jnp.ones((keys.shape[0], pair), bf16)
    mixed = []
    for at in range(0, width, pair):
        both = queries[:, at : at + pair]
        none = jnp.zeros_like(both)
        stacked = jnp.concatenate(
            [jnp.where(first, both, none), jnp.where(first, none, both)], axis=0
        )
        scores = dot_t(stacked, keys[:, at : at + pair]) * scale
        if bias is not None:
            scores = scores + bias
        weights = jnp.exp(scores - jnp.max(scores, axis=-1, keepdims=True)).astype(bf16)
        summed = dot(weights, jnp.concatenate([values[:, at : at + pair], ones], axis=1))
        result = summed[:, :pair] / summed[:, pair:]
        mixed.append(jnp.where(first, result[:rows], result[rows:]).astype(bf16))
    return jnp.concatenate(mixed, axis=1)


def fetch(entry, arrays, target, sem):
    for code, ref in arrays.items():

        @pl.when(entry // SPAN == code)
        def _(ref=ref):
            pltpu.make_async_copy(ref.at[entry % SPAN], target, sem).start()


def agent_kernel(list_length, first_step, codes, idle, head_size, table_ref, own_ref, *refs):
    arrays = dict(zip(codes, refs))
    proj_ref, merge_ref, residual_ref, normed_ref, held_ref, sems = refs[len(codes) + idle :]
    width = own_ref.shape[-1]
    turn = pl.program_id(0)

    def begin(step):
        for j in range(list_length):
            slot = step % 2
            entry = table_ref[(first_step + step) * list_length + j]
            fetch(entry, arrays, held_ref.at[slot, j], sems.at[slot, j])

    @pl.when(turn == 0)
    def _():
        begin(turn)

    @pl.when(turn + 1 < pl.num_programs(0))
    def _():
        begin(turn + 1)

    own = own_ref[0].astype(f32)
    rows = [rms(own).astype(bf16)]
    queries = dot(rows[0], proj_ref[:, :width]).astype(bf16)
    slot = turn % 2
    for j in range(list_length):
        pltpu.make_async_copy(refs[0].at[0], held_ref.at[slot, j], sems.at[slot, j]).wait()
        rows.append(rms(held_ref[slot, j].astype(f32)).astype(bf16))
    keyvals = dot(jnp.concatenate(rows, axis=0), proj_ref[:, width:]).astype(bf16)
    mixed = attend(queries, keyvals[:, :width], keyvals[:, width:], head_size, None)
    residual = own + dot(mixed, merge_ref[...])
    residual_ref[0] = residual
    normed_ref[0] = rms(residual).astype(bf16)


def agent_stage(embedded, arrays, table, first_step, steps, list_length, proj, merge, after=()):
    _, agents, width = embedded.shape
    piece = (1, agents, width)
    whole = lambda i, w: (0, 0)
    flops = 2 * steps * agents * width * width * (4 + 2 * list_length + 2 * (1 + list_length))
    return pl.pallas_call(
        functools.partial(
            agent_kernel, list_length, first_step, tuple(arrays), len(after), width // HEADS
        ),
        grid_spec=pltpu.PrefetchScalarGridSpec(
            num_scalar_prefetch=1,
            grid=(steps,),
            in_specs=[pl.BlockSpec(piece, lambda i, w: (first_step + i, 0, 0))]
            + [pl.BlockSpec(memory_space=pl.ANY)] * (len(arrays) + len(after))
            + [pl.BlockSpec(proj.shape, whole), pl.BlockSpec(merge.shape, whole)],
            out_specs=[pl.BlockSpec(piece, lambda i, w: (i, 0, 0))] * 2,
            scratch_shapes=[
                pltpu.VMEM((2, list_length, agents, width), bf16),
                pltpu.SemaphoreType.DMA((2, list_length)),
            ],
        ),
        out_shape=[
            jax.ShapeDtypeStruct((steps, agents, width), f32),
            jax.ShapeDtypeStruct((steps, agents, width), bf16),
        ],
        compiler_params=pltpu.CompilerParams(vmem_limit_bytes=VMEM_LIMIT),
        cost_estimate=pl.CostEstimate(
            flops=5 * flops, bytes_accessed=steps * agents * width * 12, transcendentals=0
        ),
        name="agent_stage",
    )(table, embedded, *arrays.values(), *after, proj, merge)


def pack_kernel(codes, parts, idle, table_ref, *refs):
    arrays = dict(zip(codes, refs))
    outs, (held_ref, in_sems, out_sems) = refs[len(codes) + idle : -3], refs[-3:]
    slots = []
    for out, (offset, count, first) in zip(outs, parts):
        slots += [(offset, first, n, out.at[n]) for n in range(count)]

    def guarded(offset, n, action):
        if offset is None:
            action()
        else:
            pl.when(table_ref[offset + n] >= 0)(action)

    for at, (offset, first, n, _) in enumerate(slots):
        if offset is None:
            own = arrays[0].at[first + n]
            pltpu.make_async_copy(own, held_ref.at[at], in_sems.at[at]).start()
        else:
            fetch(table_ref[offset + n], arrays, held_ref.at[at], in_sems.at[at])
    for at, (offset, first, n, target) in enumerate(slots):

        def pass_on(at=at, target=target):
            pltpu.make_async_copy(refs[0].at[0], held_ref.at[at], in_sems.at[at]).wait()
            pltpu.make_async_copy(held_ref.at[at], target, out_sems.at[at]).start()

        guarded(offset, n, pass_on)
    for at, (offset, first, n, target) in enumerate(slots):

        def finish(at=at, target=target):
            pltpu.make_async_copy(held_ref.at[at], target, out_sems.at[at]).wait()

        guarded(offset, n, finish)


def pack(table, arrays, parts, after=()):
    piece = next(iter(arrays.values())).shape[1:]
    slots = sum(count for _, count, _ in parts)
    return pl.pallas_call(
        functools.partial(pack_kernel, tuple(arrays), tuple(parts), len(after)),
        in_specs=[pl.BlockSpec(memory_space=pltpu.SMEM)]
        + [pl.BlockSpec(memory_space=pl.ANY)] * (len(arrays) + len(after)),
        out_specs=[pl.BlockSpec(memory_space=pl.ANY)] * len(parts),
        out_shape=[jax.ShapeDtypeStruct((count,) + piece, bf16) for _, count, _ in parts],
        scratch_shapes=[
            pltpu.VMEM((slots,) + piece, bf16),
            pltpu.SemaphoreType.DMA((slots,)),
            pltpu.SemaphoreType.DMA((slots,)),
        ],
        cost_estimate=pl.CostEstimate(
            flops=0, bytes_accessed=4 * slots * piece[0] * piece[1], transcendentals=0
        ),
        compiler_params=pltpu.CompilerParams(vmem_limit_bytes=VMEM_LIMIT),
        name="pack",
    )(table, *arrays.values(), *after)


def suffix(values, rewards, done, next_value, next_advantage):
    steps = values.shape[0]
    living = 1.0 - done.astype(f32)
    running, following, rows = next_advantage, next_value, [None] * steps
    for step in range(steps - 1, -1, -1):
        alive = living[step : step + 1]
        value = values[step : step + 1]
        change = rewards[step : step + 1] + discount * alive * following - value
        running = change + discount * trace_decay * alive * running
        rows[step] = running
        following = value
    return rows


def time_kernel(parts, steps, tile, head_size, offset_ref, *refs):
    refs = list(refs)
    residual_refs = [refs.pop(0) for _ in range(parts)]
    rim_refs = [refs.pop(0) for _ in range(parts)]
    proj_ref, merge_ref, weight_ref, done_ref, rewards_ref, boot_ref = refs[:6]
    values_ref, edge_ref, bias_ref = refs[6:]
    width = proj_ref.shape[0]
    turn = pl.program_id(0)
    group = 8
    rows = steps * group
    agents = values_ref.shape[1]

    @pl.when(turn == 0)
    def _():
        r = lax.broadcasted_iota(jnp.int32, (2 * rows, 2 * rows), 0) % rows
        c = lax.broadcasted_iota(jnp.int32, (2 * rows, 2 * rows), 1)
        query_step = r // group
        key_step = c // group - steps
        allowed = (
            (r % group == c % group)
            & (key_step <= query_step)
            & (key_step > query_step - WINDOW)
            & (key_step + offset_ref[0] >= 0)
        )
        bias_ref[...] = jnp.where(allowed, 0.0, -1e30)
        values_ref[...] = jnp.zeros_like(values_ref)

    def pieces(part_refs):
        whole = jnp.concatenate([ref[...].astype(f32) for ref in part_refs], axis=0)
        return [
            whole[:, at : at + group].reshape(rows, width) for at in range(0, tile, group)
        ]

    residuals = pieces(residual_refs)
    current = jnp.concatenate([rms(r).astype(bf16) for r in residuals], axis=0)
    behind = jnp.concatenate([r.astype(bf16) for r in pieces(rim_refs)], axis=0)
    projected = dot(current, proj_ref[...]).astype(bf16)
    before = dot(behind, proj_ref[:, width:]).astype(bf16)
    bias = bias_ref[...]
    mixed = []
    for at in range(0, tile * steps, rows):
        mine, past = projected[at : at + rows], before[at : at + rows]
        keys = jnp.concatenate([past[:, :width], mine[:, width : 2 * width]], axis=0)
        held = jnp.concatenate([past[:, width:], mine[:, 2 * width :]], axis=0)
        mixed.append(attend(mine[:, :width], keys, held, head_size, bias))
    merged = dot(jnp.concatenate(mixed, axis=0), merge_ref[...])
    lane = lax.broadcasted_iota(jnp.int32, (steps, group, agents), 2)
    place = lax.broadcasted_iota(jnp.int32, (steps, group, agents), 1)
    total = values_ref[...]
    for n, residual in enumerate(residuals):
        final = rms(residual + merged[n * rows : (n + 1) * rows])
        value = jnp.sum(final * weight_ref[...], axis=-1, keepdims=True)
        spot = lane == place + (turn * tile + n * group)
        total = total + jnp.sum(
            jnp.where(spot, value.reshape(steps, group, 1), 0.0), axis=1
        )
    values_ref[...] = total

    @pl.when(turn == pl.num_programs(0) - 1)
    def _():
        found = values_ref[...]
        boot = boot_ref[...]
        advantages = suffix(found, rewards_ref[...], done_ref[...], boot, jnp.zeros_like(boot))
        edge_ref[...] = jnp.concatenate([found[:1], advantages[0]], axis=0)


def time_stage(residuals, rims, offset, proj, merge, weight, done, rewards, boot):
    part_steps = [r.shape[0] for r in residuals]
    steps = sum(part_steps)
    _, agents, width = residuals[0].shape
    tile = 16
    whole = lambda i, o: (0, 0)

    def blocks(arrays):
        return [
            pl.BlockSpec((array.shape[0], tile, width), lambda i, o: (0, i, 0))
            for array in arrays
        ]

    rows = 16 * steps
    fixed = [proj, merge, weight, done, rewards, boot]
    return pl.pallas_call(
        functools.partial(time_kernel, len(residuals), steps, tile, width // HEADS),
        grid_spec=pltpu.PrefetchScalarGridSpec(
            num_scalar_prefetch=1,
            grid=(agents // tile,),
            in_specs=blocks(residuals)
            + blocks(rims)
            + [pl.BlockSpec(array.shape, whole) for array in fixed],
            out_specs=[
                pl.BlockSpec((steps, agents), whole),
                pl.BlockSpec((2, agents), whole),
            ],
            scratch_shapes=[pltpu.VMEM((rows, rows), f32)],
        ),
        out_shape=[
            jax.ShapeDtypeStruct((steps, agents), f32),
            jax.ShapeDtypeStruct((2, agents), f32),
        ],
        compiler_params=pltpu.CompilerParams(vmem_limit_bytes=VMEM_LIMIT),
        name="time_stage",
    )(offset, *residuals, *rims, *fixed)


def advantage_kernel(last_ref, values_ref, rewards_ref, done_ref, boot_ref, edge_ref, out_ref, mine_ref):
    last = last_ref[0] > 0
    arriving = edge_ref[...]
    boot = boot_ref[...]
    found = values_ref[...]
    next_value = jnp.where(last, boot, arriving[:1])
    next_advantage = jnp.where(last, 0.0, arriving[1:2])
    rows = suffix(found, rewards_ref[...], done_ref[...], next_value, next_advantage)
    out_ref[...] = jnp.concatenate(rows, axis=0)
    mine_ref[...] = jnp.concatenate([found[:1], rows[0]], axis=0)


def advantage_stage(last, values, rewards, done, boot, edge):
    return pl.pallas_call(
        advantage_kernel,
        in_specs=[pl.BlockSpec(memory_space=pltpu.SMEM)]
        + [pl.BlockSpec(memory_space=pltpu.VMEM)] * 5,
        out_specs=[pl.BlockSpec(memory_space=pltpu.VMEM)] * 2,
        out_shape=[
            jax.ShapeDtypeStruct(values.shape, f32),
            jax.ShapeDtypeStruct(edge.shape, f32),
        ],
        name="advantage_stage",
    )(last, values, rewards, done, boot, edge)


def exchange_slots(embedded, lists, capacity):
    steps, agents, width = embedded.shape
    blocks = lax.axis_size("agent")
    list_length = lists.shape[1]
    named = lists.reshape(-1)
    row_steps = jnp.arange(named.shape[0], dtype=jnp.int32) // list_length
    hits = (named[:, None] == jnp.arange(blocks, dtype=jnp.int32)[None, :]).astype(jnp.int32)
    slot = jnp.sum((jnp.cumsum(hits, axis=0) - hits) * hits, axis=1)
    slot_hits = (slot[:, None] == jnp.arange(capacity, dtype=jnp.int32)[None, :]).astype(jnp.int32)
    requests = jnp.sum(
        (hits * row_steps[:, None])[:, :, None] * slot_hits[:, None, :], axis=0
    )
    wanted = lax.all_to_all(requests, "agent", split_axis=0, concat_axis=0, tiled=True)
    outgoing = embedded[wanted.reshape(-1)].reshape(blocks, capacity, agents, width)
    arrived = lax.all_to_all(outgoing, "agent", split_axis=0, concat_axis=0, tiled=True)
    return arrived.reshape(blocks * capacity, agents, width), named * capacity + slot


OUTWARD_READY = {1: (0, 2, 2), 2: (1, 3, 3), 3: (2, 3, 4)}
ACROSS_READY = {0: (0, 1, 1), 1: (0, 0, 0), 2: (0, 2, 2), 3: (1, 2, 3)}
OUTWARD_DUE = (3, 4, 4)
ACROSS_DUE = (2, 3, 4)


def relay_sizes(steps, capacity):
    half, quarter = steps // 2, steps // 4
    chunks = [half, quarter, quarter]
    outward = [half, half, half + 1, half + 1, quarter + 2]
    across = [capacity + 1, half, half, half - 1, quarter + 2]
    return chunks, outward, across


def relay_codes(outward, across):
    names = {}
    code = 1
    for name, count in (("edge", len(outward)), ("swap", 2), ("far", 3), ("across", len(across))):
        names[name] = [code + n for n in range(count)]
        code += count
    names["own"] = 0
    return names


def inner_place(codes, starts, u, k):
    behind = starts[k] - starts[min(k, 1)]
    if u == 0:
        return codes["edge"][min(k, 1)] * SPAN + behind
    if u == 1:
        return codes["own"] * SPAN + starts[k]
    if u == 2:
        return codes["swap"][min(k, 1)] * SPAN + behind
    return codes["far"][k] * SPAN


def plan_kernel(steps, list_length, chunks, outward, across, place_ref, lists_ref, out_ref, in_ref, flag_ref, eloc, yloc, room):
    codes = relay_codes(outward, across)
    column, row = place_ref[0], place_ref[1]
    far_side = column >= COLUMNS // 2
    mirror = lambda u: jnp.where(far_side, COLUMNS - 1 - u, u)
    me = mirror(column)
    inner = me == 1
    starts = [sum(chunks[:k]) for k in range(len(chunks))]
    e_base = [sum(outward[:b]) for b in range(len(outward))]
    y_base = [sum(outward) + sum(across[:b]) for b in range(len(across))]
    block = lambda c, r: c * ROWS + r
    entry = lambda b, t, j: lists_ref[(b * steps + t) * list_length + j]

    def clear(n, _):
        out_ref[n] = -1
        return 0

    lax.fori_loop(0, sum(outward) + sum(across), clear, 0)

    def named(dest, t, source):
        hit = entry(dest, t, 0) == source
        for j in range(1, list_length):
            hit = hit | (entry(dest, t, j) == source)
        return hit

    def choose(sizes, ready):
        batch = jnp.int32(-1)
        for b in range(len(sizes) - 1, -1, -1):
            batch = jnp.where((room[b] < sizes[b]) & (b >= ready), b, batch)
        return batch

    def base_of(bases, batch):
        base = jnp.int32(0)
        for b, value in enumerate(bases):
            base = jnp.where(batch == b, value, base)
        return base

    def empty(sizes):
        for b in range(len(sizes)):
            room[b] = 0

    for turn in range(2):
        sender = row if turn == 0 else 1 - row
        empty(outward)
        room[0], room[1] = outward[0], outward[1]
        for k, count in enumerate(chunks):
            for u in (1, 2, 3):

                def first_piece(n, _, u=u):
                    eloc[(turn * COLUMNS + u) * steps + n] = (u - 1) * SPAN + n
                    return 0

                if u in (1, 2) and k == 0:
                    lax.fori_loop(0, count, first_piece, 0)
                    continue

                def outer_piece(n, _, u=u, k=k):
                    t = starts[k] + n
                    source = block(mirror(u), sender)
                    need = named(block(mirror(0), 0), t, source)
                    for r in range(1, ROWS):
                        need = need | named(block(mirror(0), r), t, source)
                    batch = choose(outward, OUTWARD_READY[u][k])
                    eloc[(turn * COLUMNS + u) * steps + t] = -1

                    @pl.when(need & (batch >= 0))
                    def _():
                        slot = room[batch]
                        room[batch] = slot + 1
                        eloc[(turn * COLUMNS + u) * steps + t] = batch * SPAN + slot
                        if turn == 0:

                            @pl.when(inner)
                            def _():
                                out_ref[base_of(e_base, batch) + slot] = inner_place(codes, starts, u, k) + n

                    return 0

                lax.fori_loop(0, count, outer_piece, 0)

    for turn in range(2):
        sender = row if turn == 0 else 1 - row
        empty(across)
        for k, count in enumerate(chunks):
            for u in range(COLUMNS):

                def row_piece(n, _, u=u, k=k):
                    t = starts[k] + n
                    need = named(block(column, 1 - sender), t, block(mirror(u), sender))
                    if u == 0:
                        lies = jnp.int32(codes["own"] * SPAN) + t
                        when = jnp.int32(0)
                    else:
                        where = eloc[(turn * COLUMNS + u) * steps + t]
                        lies = codes["edge"][0] * SPAN + where
                        when = jnp.where(where < 0, len(across), where // SPAN)
                    when = jnp.where(inner, ACROSS_READY[u][k], when)
                    lies = jnp.where(inner, inner_place(codes, starts, u, k) + n, lies)
                    batch = choose(across, when)
                    yloc[(turn * COLUMNS + u) * steps + t] = -1

                    @pl.when(need & (batch >= 0))
                    def _():
                        slot = room[batch]
                        room[batch] = slot + 1
                        yloc[(turn * COLUMNS + u) * steps + t] = batch * SPAN + slot
                        if turn == 0:
                            out_ref[base_of(y_base, batch) + slot] = lies

                    return 0

                lax.fori_loop(0, count, row_piece, 0)

    flag_ref[0] = 0
    for k, count in enumerate(chunks):

        def listed_piece(n, _, k=k):
            t = starts[k] + n // list_length
            source = entry(block(column, row), t, n % list_length)
            u = mirror(source // ROWS)
            same = source % ROWS == row
            e = eloc[u * steps + t]
            y = yloc[(COLUMNS + u) * steps + t]
            first = jnp.int32(0)
            for w in (0, 2, 3):
                first = jnp.where(u == w, inner_place(codes, starts, w, k), first)
            direct = jnp.where(inner, first + t - starts[k], codes["edge"][0] * SPAN + e)
            direct = jnp.where(u == me, codes["own"] * SPAN + t, direct)
            local = inner | (u == me)
            bad = jnp.where(
                same,
                jnp.logical_not(local) & ((e < 0) | (e // SPAN > OUTWARD_DUE[k])),
                (y < 0) | (y // SPAN > ACROSS_DUE[k]),
            )
            place = jnp.where(same, direct, codes["across"][0] * SPAN + y)
            in_ref[t * list_length + n % list_length] = jnp.where(bad, codes["own"] * SPAN, place)

            @pl.when(bad)
            def _():
                flag_ref[0] = 1

            return 0

        lax.fori_loop(0, count * list_length, listed_piece, 0)


def plan(lists_all, place, steps, list_length, chunks, outward, across):
    smem = pl.BlockSpec(memory_space=pltpu.SMEM)
    slots = sum(outward) + sum(across)
    return pl.pallas_call(
        functools.partial(plan_kernel, steps, list_length, chunks, outward, across),
        in_specs=[smem, smem],
        out_specs=[smem] * 3,
        out_shape=[
            jax.ShapeDtypeStruct((slots,), jnp.int32),
            jax.ShapeDtypeStruct((steps * list_length,), jnp.int32),
            jax.ShapeDtypeStruct((1,), jnp.int32),
        ],
        scratch_shapes=[
            pltpu.SMEM((2 * COLUMNS * steps,), jnp.int32),
            pltpu.SMEM((2 * COLUMNS * steps,), jnp.int32),
            pltpu.SMEM((max(len(outward), len(across)),), jnp.int32),
        ],
        name="plan",
    )(place, lists_all)


def shared(value, axes):
    count = lax.axis_size(axes)
    rows = jnp.broadcast_to(value[None], (count,) + value.shape)
    return lax.all_to_all(rows, axes, split_axis=0, concat_axis=0, tiled=True)


def column_pairs(moves):
    return [(a * ROWS + r, b * ROWS + r) for a, b in moves for r in range(ROWS)]


def relay(embedded, lists, capacity, attention):
    steps, agents, width = embedded.shape
    list_length = lists.shape[1]
    chunks, outward, across = relay_sizes(steps, capacity)
    codes = relay_codes(outward, across)
    starts = [sum(chunks[:k]) for k in range(len(chunks))]
    e_base = [sum(outward[:b]) for b in range(len(outward))]
    y_base = [sum(outward) + sum(across[:b]) for b in range(len(across))]
    index = lax.axis_index("agent")
    place = jnp.stack([index // ROWS, index % ROWS]).astype(jnp.int32)
    send = lambda value, pairs: lax.ppermute(value, "agent", pairs)
    edges = column_pairs([(0, 1), (1, 0), (2, 3), (3, 2)])
    swap = column_pairs([(1, 2), (2, 1)])
    over = [(c * ROWS + r, c * ROWS + 1 - r) for c in range(COLUMNS) for r in range(ROWS)]
    own, edge, swapped, far, rows = (codes[n] for n in ("own", "edge", "swap", "far", "across"))
    arrays = {own: embedded}

    def pick(names):
        return {code: arrays[code] for code in names}

    first = embedded[: chunks[0]]
    arrays[edge[0]] = send(first, edges)
    arrays[swapped[0]] = send(first, swap)
    everyone = shared(lists.reshape(-1), "agent").reshape(-1)
    out_table, in_table, flag = plan(
        everyone, place, steps, list_length, chunks, outward, across
    )
    arrays[far[0]] = send(arrays[edge[0]], swap)
    column = index // ROWS
    outer = (column == 0) | (column == COLUMNS - 1)
    slots = jnp.arange(outward[1], dtype=jnp.int32)
    table = jnp.where(outer, own * SPAN + starts[1] + slots, swapped[0] * SPAN + slots)
    packed = pack(table, pick([own, swapped[0]]), [(0, outward[1], None), (None, outward[1], starts[1])])
    arrays[edge[1]] = send(packed[0], edges)
    arrays[swapped[1]] = send(packed[1], swap)
    (packed,) = pack(out_table, pick([own, edge[0], swapped[0]]), [(y_base[0], across[0], None)], packed[:1])
    arrays[rows[0]] = send(packed, over)
    for k in (1, 2):
        at = starts[k] - starts[1]
        arrays[far[k]] = send(arrays[edge[1]][at : at + chunks[k]], swap)

    def stage(n, reads, settled, after=()):
        parts = [(y_base[n - 1], across[n - 1], None)]
        if n < len(outward):
            parts.append((e_base[n], outward[n], None))
        after = tuple(arrays[rows[b]] for b in settled) + tuple(after)
        packed = pack(out_table, pick([own] + reads), parts, after)
        if n < len(outward):
            arrays[edge[n]] = send(packed[1], edges)
        arrays[rows[n - 1]] = send(packed[0], over)
        return packed[0]

    reads = edge[:2] + swapped[:1] + far[:1]
    token = stage(2, reads, (), (packed,))
    crowded = jnp.max(shared(flag, ("groups", "agent", "tm")))
    reads = reads + edge[2:3] + swapped[1:] + far[1:2]
    token = stage(3, reads, (0, 1), (token, crowded.reshape(1)))
    reads = reads + edge[3:4] + far[2:3]
    token = stage(4, reads, (2,), (token,))
    done = [attention(0, chunks[0], due(arrays, codes, starts, 0), in_table, (token,))]
    reads = reads + edge[4:5]
    token = stage(5, reads, (3,), (done[0][0],))
    for k in (1, 2):
        done.append(
            attention(starts[k], chunks[k], due(arrays, codes, starts, k), in_table, (token, done[-1][0]))
        )
    return done, crowded


def due(arrays, codes, starts, k):
    wanted = {codes["own"], *codes["edge"][: OUTWARD_DUE[k] + 1]}
    wanted |= {inner_place(codes, starts, u, k) // SPAN for u in (0, 2, 3)}
    wanted |= set(codes["across"][: ACROSS_DUE[k] + 1])
    return {code: arrays[code] for code in sorted(wanted)}


def body(
    embedded,
    block_lists,
    done_flags,
    rewards,
    bootstrap,
    agent_proj,
    agent_merge,
    time_proj,
    time_merge,
    value_weight,
):
    steps, agents, width = embedded.shape
    list_length = block_lists.shape[2]
    blocks = lax.axis_size("agent")
    lists = block_lists[0]
    capacity = max(2, (2 * steps * list_length + blocks - 1) // blocks)
    spans = lax.axis_size("tm")
    index = lax.axis_index("tm")
    offset = (index * steps).astype(jnp.int32).reshape(1)
    boot = bootstrap.reshape(1, agents)
    forward = [(i, i + 1) for i in range(spans - 1)]
    backward = [(i + 1, i) for i in range(spans - 1)]

    def attention(first, count, arrays, table, after=()):
        residual, normed = agent_stage(
            embedded, arrays, table, first, count, list_length, agent_proj, agent_merge, after
        )
        return residual, lax.ppermute(normed, "tm", forward)

    def finish(done):
        residuals, rims = [part[0] for part in done], [part[1] for part in done]
        values, edge = time_stage(
            residuals,
            rims,
            offset,
            time_proj,
            time_merge,
            value_weight.reshape(1, width),
            done_flags,
            rewards,
            boot,
        )
        last = (index == spans - 1).astype(jnp.int32).reshape(1)
        for _ in range(max(1, spans - 1)):
            arriving = lax.ppermute(edge, "tm", backward)
            advantages, edge = advantage_stage(last, values, rewards, done_flags, boot, arriving)
        return values, advantages

    def padded():
        pool, where = exchange_slots(embedded, lists, capacity)
        return finish([attention(0, steps, {1: pool}, where + SPAN)])

    if blocks != COLUMNS * ROWS or steps % 4:
        return padded()
    done, crowded = relay(embedded, lists, capacity, attention)
    found = finish(done)
    return lax.cond(crowded > 0, padded, lambda: found)


def solution(mesh):
    placed = (
        P(("groups", "tm"), "agent", None),
        P(("groups", "agent"), "tm", None),
        P(("groups", "tm"), "agent"),
        P(("groups", "tm"), "agent"),
        P(("groups", "agent")),
        P(),
        P(),
        P(),
        P(),
        P(),
    )
    return jax.shard_map(
        body,
        mesh=mesh,
        in_specs=placed,
        out_specs=(P(("groups", "tm"), "agent"), P(("groups", "tm"), "agent")),
        check_vma=False,
    )
```

```python
import functools

import jax
import jax.numpy as jnp
from jax import lax
from jax.experimental import pallas as pl
from jax.experimental.pallas import tpu as pltpu
from jax.sharding import PartitionSpec as P

HEADS = 8
WINDOW = 16
discount = 0.9997
trace_decay = 0.995
epsilon = 1e-06
bf16 = jnp.bfloat16
f32 = jnp.float32
VMEM_LIMIT = 48 * 1024 * 1024
SPAN = 1024
COLUMNS = 4
ROWS = 2


def rms(values):
    return values * lax.rsqrt(jnp.mean(values * values, axis=-1, keepdims=True) + epsilon)


def dot(a, b):
    return jnp.dot(a, b, preferred_element_type=f32)


def dot_t(a, b):
    return lax.dot_general(a, b, (((1,), (1,)), ((), ())), preferred_element_type=f32)


def attend(queries, keys, values, head_size, bias):
    rows, width = queries.shape
    scale = head_size ** (-0.5)
    pair = 2 * head_size
    lane = lax.broadcasted_iota(jnp.int32, (rows, pair), 1)
    first = lane < head_size
    ones = jnp.ones((keys.shape[0], pair), bf16)
    mixed = []
    for at in range(0, width, pair):
        both = queries[:, at : at + pair]
        none = jnp.zeros_like(both)
        stacked = jnp.concatenate(
            [jnp.where(first, both, none), jnp.where(first, none, both)], axis=0
        )
        scores = dot_t(stacked, keys[:, at : at + pair]) * scale
        if bias is not None:
            scores = scores + bias
        weights = jnp.exp(scores - jnp.max(scores, axis=-1, keepdims=True)).astype(bf16)
        summed = dot(weights, jnp.concatenate([values[:, at : at + pair], ones], axis=1))
        result = summed[:, :pair] / summed[:, pair:]
        mixed.append(jnp.where(first, result[:rows], result[rows:]).astype(bf16))
    return jnp.concatenate(mixed, axis=1)


def fetch(entry, arrays, target, sem):
    for code, ref in arrays.items():

        @pl.when(entry // SPAN == code)
        def _(ref=ref):
            pltpu.make_async_copy(ref.at[entry % SPAN], target, sem).start()


def agent_kernel(list_length, first_step, codes, idle, head_size, table_ref, own_ref, *refs):
    arrays = dict(zip(codes, refs))
    proj_ref, merge_ref, residual_ref, normed_ref, held_ref, sems = refs[len(codes) + idle :]
    width = own_ref.shape[-1]
    turn = pl.program_id(0)

    def begin(step):
        for j in range(list_length):
            slot = step % 2
            entry = table_ref[(first_step + step) * list_length + j]
            fetch(entry, arrays, held_ref.at[slot, j], sems.at[slot, j])

    @pl.when(turn == 0)
    def _():
        begin(turn)

    @pl.when(turn + 1 < pl.num_programs(0))
    def _():
        begin(turn + 1)

    own = own_ref[0].astype(f32)
    rows = [rms(own).astype(bf16)]
    queries = dot(rows[0], proj_ref[:, :width]).astype(bf16)
    slot = turn % 2
    for j in range(list_length):
        pltpu.make_async_copy(refs[0].at[0], held_ref.at[slot, j], sems.at[slot, j]).wait()
        rows.append(rms(held_ref[slot, j].astype(f32)).astype(bf16))
    keyvals = dot(jnp.concatenate(rows, axis=0), proj_ref[:, width:]).astype(bf16)
    mixed = attend(queries, keyvals[:, :width], keyvals[:, width:], head_size, None)
    residual = own + dot(mixed, merge_ref[...])
    residual_ref[0] = residual
    normed_ref[0] = rms(residual).astype(bf16)


def agent_stage(embedded, arrays, table, first_step, steps, list_length, proj, merge, after=()):
    _, agents, width = embedded.shape
    piece = (1, agents, width)
    whole = lambda i, w: (0, 0)
    flops = 2 * steps * agents * width * width * (4 + 2 * list_length + 2 * (1 + list_length))
    return pl.pallas_call(
        functools.partial(
            agent_kernel, list_length, first_step, tuple(arrays), len(after), width // HEADS
        ),
        grid_spec=pltpu.PrefetchScalarGridSpec(
            num_scalar_prefetch=1,
            grid=(steps,),
            in_specs=[pl.BlockSpec(piece, lambda i, w: (first_step + i, 0, 0))]
            + [pl.BlockSpec(memory_space=pl.ANY)] * (len(arrays) + len(after))
            + [pl.BlockSpec(proj.shape, whole), pl.BlockSpec(merge.shape, whole)],
            out_specs=[pl.BlockSpec(piece, lambda i, w: (i, 0, 0))] * 2,
            scratch_shapes=[
                pltpu.VMEM((2, list_length, agents, width), bf16),
                pltpu.SemaphoreType.DMA((2, list_length)),
            ],
        ),
        out_shape=[
            jax.ShapeDtypeStruct((steps, agents, width), f32),
            jax.ShapeDtypeStruct((steps, agents, width), bf16),
        ],
        compiler_params=pltpu.CompilerParams(vmem_limit_bytes=VMEM_LIMIT),
        cost_estimate=pl.CostEstimate(
            flops=5 * flops, bytes_accessed=steps * agents * width * 12, transcendentals=0
        ),
        name="agent_stage",
    )(table, embedded, *arrays.values(), *after, proj, merge)


def pack_kernel(codes, parts, idle, table_ref, *refs):
    arrays = dict(zip(codes, refs))
    outs, (held_ref, in_sems, out_sems) = refs[len(codes) + idle : -3], refs[-3:]
    slots = []
    for out, (offset, count, first) in zip(outs, parts):
        slots += [(offset, first, n, out.at[n]) for n in range(count)]

    def guarded(offset, n, action):
        if offset is None:
            action()
        else:
            pl.when(table_ref[offset + n] >= 0)(action)

    for at, (offset, first, n, _) in enumerate(slots):
        if offset is None:
            own = arrays[0].at[first + n]
            pltpu.make_async_copy(own, held_ref.at[at], in_sems.at[at]).start()
        else:
            fetch(table_ref[offset + n], arrays, held_ref.at[at], in_sems.at[at])
    for at, (offset, first, n, target) in enumerate(slots):

        def pass_on(at=at, target=target):
            pltpu.make_async_copy(refs[0].at[0], held_ref.at[at], in_sems.at[at]).wait()
            pltpu.make_async_copy(held_ref.at[at], target, out_sems.at[at]).start()

        guarded(offset, n, pass_on)
    for at, (offset, first, n, target) in enumerate(slots):

        def finish(at=at, target=target):
            pltpu.make_async_copy(held_ref.at[at], target, out_sems.at[at]).wait()

        guarded(offset, n, finish)


def pack(table, arrays, parts, after=()):
    piece = next(iter(arrays.values())).shape[1:]
    slots = sum(count for _, count, _ in parts)
    return pl.pallas_call(
        functools.partial(pack_kernel, tuple(arrays), tuple(parts), len(after)),
        in_specs=[pl.BlockSpec(memory_space=pltpu.SMEM)]
        + [pl.BlockSpec(memory_space=pl.ANY)] * (len(arrays) + len(after)),
        out_specs=[pl.BlockSpec(memory_space=pl.ANY)] * len(parts),
        out_shape=[jax.ShapeDtypeStruct((count,) + piece, bf16) for _, count, _ in parts],
        scratch_shapes=[
            pltpu.VMEM((slots,) + piece, bf16),
            pltpu.SemaphoreType.DMA((slots,)),
            pltpu.SemaphoreType.DMA((slots,)),
        ],
        cost_estimate=pl.CostEstimate(
            flops=0, bytes_accessed=piece[0] * piece[1], transcendentals=0
        ),
        compiler_params=pltpu.CompilerParams(vmem_limit_bytes=VMEM_LIMIT),
        name="pack",
    )(table, *arrays.values(), *after)


def suffix(values, rewards, done, next_value, next_advantage):
    steps = values.shape[0]
    living = 1.0 - done.astype(f32)
    running, following, rows = next_advantage, next_value, [None] * steps
    for step in range(steps - 1, -1, -1):
        alive = living[step : step + 1]
        value = values[step : step + 1]
        change = rewards[step : step + 1] + discount * alive * following - value
        running = change + discount * trace_decay * alive * running
        rows[step] = running
        following = value
    return rows


def time_kernel(parts, steps, tile, head_size, offset_ref, *refs):
    refs = list(refs)
    residual_refs = [refs.pop(0) for _ in range(parts)]
    rim_refs = [refs.pop(0) for _ in range(parts)]
    proj_ref, merge_ref, weight_ref, done_ref, rewards_ref, boot_ref = refs[:6]
    values_ref, edge_ref, bias_ref = refs[6:]
    width = proj_ref.shape[0]
    turn = pl.program_id(0)
    group = 8
    rows = steps * group
    agents = values_ref.shape[1]

    @pl.when(turn == 0)
    def _():
        r = lax.broadcasted_iota(jnp.int32, (2 * rows, 2 * rows), 0) % rows
        c = lax.broadcasted_iota(jnp.int32, (2 * rows, 2 * rows), 1)
        query_step = r // group
        key_step = c // group - steps
        allowed = (
            (r % group == c % group)
            & (key_step <= query_step)
            & (key_step > query_step - WINDOW)
            & (key_step + offset_ref[0] >= 0)
        )
        bias_ref[...] = jnp.where(allowed, 0.0, -1e30)
        values_ref[...] = jnp.zeros_like(values_ref)

    def pieces(part_refs):
        whole = jnp.concatenate([ref[...].astype(f32) for ref in part_refs], axis=0)
        return [
            whole[:, at : at + group].reshape(rows, width) for at in range(0, tile, group)
        ]

    residuals = pieces(residual_refs)
    current = jnp.concatenate([rms(r).astype(bf16) for r in residuals], axis=0)
    behind = jnp.concatenate([r.astype(bf16) for r in pieces(rim_refs)], axis=0)
    projected = dot(current, proj_ref[...]).astype(bf16)
    before = dot(behind, proj_ref[:, width:]).astype(bf16)
    bias = bias_ref[...]
    mixed = []
    for at in range(0, tile * steps, rows):
        mine, past = projected[at : at + rows], before[at : at + rows]
        keys = jnp.concatenate([past[:, :width], mine[:, width : 2 * width]], axis=0)
        held = jnp.concatenate([past[:, width:], mine[:, 2 * width :]], axis=0)
        mixed.append(attend(mine[:, :width], keys, held, head_size, bias))
    merged = dot(jnp.concatenate(mixed, axis=0), merge_ref[...])
    lane = lax.broadcasted_iota(jnp.int32, (steps, group, agents), 2)
    place = lax.broadcasted_iota(jnp.int32, (steps, group, agents), 1)
    total = values_ref[...]
    for n, residual in enumerate(residuals):
        final = rms(residual + merged[n * rows : (n + 1) * rows])
        value = jnp.sum(final * weight_ref[...], axis=-1, keepdims=True)
        spot = lane == place + (turn * tile + n * group)
        total = total + jnp.sum(
            jnp.where(spot, value.reshape(steps, group, 1), 0.0), axis=1
        )
    values_ref[...] = total

    @pl.when(turn == pl.num_programs(0) - 1)
    def _():
        found = values_ref[...]
        boot = boot_ref[...]
        advantages = suffix(found, rewards_ref[...], done_ref[...], boot, jnp.zeros_like(boot))
        edge_ref[...] = jnp.concatenate([found[:1], advantages[0]], axis=0)


def time_stage(residuals, rims, offset, proj, merge, weight, done, rewards, boot):
    part_steps = [r.shape[0] for r in residuals]
    steps = sum(part_steps)
    _, agents, width = residuals[0].shape
    tile = 16
    whole = lambda i, o: (0, 0)

    def blocks(arrays):
        return [
            pl.BlockSpec((array.shape[0], tile, width), lambda i, o: (0, i, 0))
            for array in arrays
        ]

    rows = 16 * steps
    fixed = [proj, merge, weight, done, rewards, boot]
    return pl.pallas_call(
        functools.partial(time_kernel, len(residuals), steps, tile, width // HEADS),
        grid_spec=pltpu.PrefetchScalarGridSpec(
            num_scalar_prefetch=1,
            grid=(agents // tile,),
            in_specs=blocks(residuals)
            + blocks(rims)
            + [pl.BlockSpec(array.shape, whole) for array in fixed],
            out_specs=[
                pl.BlockSpec((steps, agents), whole),
                pl.BlockSpec((2, agents), whole),
            ],
            scratch_shapes=[pltpu.VMEM((rows, rows), f32)],
        ),
        out_shape=[
            jax.ShapeDtypeStruct((steps, agents), f32),
            jax.ShapeDtypeStruct((2, agents), f32),
        ],
        compiler_params=pltpu.CompilerParams(vmem_limit_bytes=VMEM_LIMIT),
        name="time_stage",
    )(offset, *residuals, *rims, *fixed)


def advantage_kernel(last_ref, values_ref, rewards_ref, done_ref, boot_ref, edge_ref, out_ref, mine_ref):
    last = last_ref[0] > 0
    arriving = edge_ref[...]
    boot = boot_ref[...]
    found = values_ref[...]
    next_value = jnp.where(last, boot, arriving[:1])
    next_advantage = jnp.where(last, 0.0, arriving[1:2])
    rows = suffix(found, rewards_ref[...], done_ref[...], next_value, next_advantage)
    out_ref[...] = jnp.concatenate(rows, axis=0)
    mine_ref[...] = jnp.concatenate([found[:1], rows[0]], axis=0)


def advantage_stage(last, values, rewards, done, boot, edge):
    return pl.pallas_call(
        advantage_kernel,
        in_specs=[pl.BlockSpec(memory_space=pltpu.SMEM)]
        + [pl.BlockSpec(memory_space=pltpu.VMEM)] * 5,
        out_specs=[pl.BlockSpec(memory_space=pltpu.VMEM)] * 2,
        out_shape=[
            jax.ShapeDtypeStruct(values.shape, f32),
            jax.ShapeDtypeStruct(edge.shape, f32),
        ],
        name="advantage_stage",
    )(last, values, rewards, done, boot, edge)


def exchange_slots(embedded, lists, capacity):
    steps, agents, width = embedded.shape
    blocks = lax.axis_size("agent")
    list_length = lists.shape[1]
    named = lists.reshape(-1)
    row_steps = jnp.arange(named.shape[0], dtype=jnp.int32) // list_length
    hits = (named[:, None] == jnp.arange(blocks, dtype=jnp.int32)[None, :]).astype(jnp.int32)
    slot = jnp.sum((jnp.cumsum(hits, axis=0) - hits) * hits, axis=1)
    slot_hits = (slot[:, None] == jnp.arange(capacity, dtype=jnp.int32)[None, :]).astype(jnp.int32)
    requests = jnp.sum(
        (hits * row_steps[:, None])[:, :, None] * slot_hits[:, None, :], axis=0
    )
    wanted = lax.all_to_all(requests, "agent", split_axis=0, concat_axis=0, tiled=True)
    outgoing = embedded[wanted.reshape(-1)].reshape(blocks, capacity, agents, width)
    arrived = lax.all_to_all(outgoing, "agent", split_axis=0, concat_axis=0, tiled=True)
    return arrived.reshape(blocks * capacity, agents, width), named * capacity + slot


OUTWARD_READY = {1: (0, 1, 1), 2: (1, 3, 3), 3: (2, 3, 4)}
ACROSS_READY = {0: (1, 2, 2), 1: (0, 0, 0), 2: (1, 3, 3), 3: (2, 3, 4)}
OUTWARD_DUE = (3, 4, 4)
ACROSS_DUE = (3, 4, 5)


def relay_sizes(steps, capacity):
    half, quarter = steps // 2, steps // 4
    chunks = [half, quarter, quarter]
    outward = [half, half, half, half, quarter + 2]
    across = [quarter, half, half, half - 1, quarter + 2, quarter + 2]
    return chunks, outward, across


def relay_codes(outward, across):
    names = {}
    code = 1
    for name, count in (("edge", len(outward)), ("swap", 2), ("far", 3), ("across", len(across))):
        names[name] = [code + n for n in range(count)]
        code += count
    names["own"] = 0
    return names


def inner_place(codes, starts, u, k):
    behind = starts[k] - starts[min(k, 1)]
    if u == 0:
        return codes["edge"][min(k, 1)] * SPAN + behind
    if u == 1:
        return codes["own"] * SPAN + starts[k]
    if u == 2:
        return codes["swap"][min(k, 1)] * SPAN + behind
    return codes["far"][k] * SPAN


def plan_kernel(steps, list_length, chunks, outward, across, place_ref, lists_ref, out_ref, in_ref, flag_ref, eloc, yloc, room):
    codes = relay_codes(outward, across)
    column, row = place_ref[0], place_ref[1]
    far_side = column >= COLUMNS // 2
    mirror = lambda u: jnp.where(far_side, COLUMNS - 1 - u, u)
    me = mirror(column)
    inner = me == 1
    starts = [sum(chunks[:k]) for k in range(len(chunks))]
    e_base = [sum(outward[:b]) for b in range(len(outward))]
    y_base = [sum(outward) + sum(across[:b]) for b in range(len(across))]
    block = lambda c, r: c * ROWS + r
    entry = lambda b, t, j: lists_ref[(b * steps + t) * list_length + j]

    def clear(n, _):
        out_ref[n] = -1
        return 0

    lax.fori_loop(0, sum(outward) + sum(across), clear, 0)

    @pl.when(me == 0)
    def _():
        for n in range(outward[1]):
            out_ref[e_base[1] + n] = codes["own"] * SPAN + starts[1] + n

    def named(dest, t, source):
        hit = entry(dest, t, 0) == source
        for j in range(1, list_length):
            hit = hit | (entry(dest, t, j) == source)
        return hit

    def choose(sizes, ready):
        batch = jnp.int32(-1)
        for b in range(len(sizes) - 1, -1, -1):
            batch = jnp.where((room[b] < sizes[b]) & (b >= ready), b, batch)
        return batch

    def base_of(bases, batch):
        base = jnp.int32(0)
        for b, value in enumerate(bases):
            base = jnp.where(batch == b, value, base)
        return base

    def empty(sizes):
        for b in range(len(sizes)):
            room[b] = 0

    for turn in range(2):
        sender = row if turn == 0 else 1 - row
        empty(outward)
        room[0] = outward[0]
        for k, count in enumerate(chunks):
            for u in (1, 2, 3):

                def first_piece(n, _):
                    eloc[(turn * COLUMNS + 1) * steps + n] = n
                    return 0

                if u == 1 and k == 0:
                    lax.fori_loop(0, count, first_piece, 0)
                    continue

                def outer_piece(n, _, u=u, k=k):
                    t = starts[k] + n
                    source = block(mirror(u), sender)
                    need = named(block(mirror(0), 0), t, source)
                    for r in range(1, ROWS):
                        need = need | named(block(mirror(0), r), t, source)
                    batch = choose(outward, OUTWARD_READY[u][k])
                    eloc[(turn * COLUMNS + u) * steps + t] = -1

                    @pl.when(need & (batch >= 0))
                    def _():
                        slot = room[batch]
                        room[batch] = slot + 1
                        eloc[(turn * COLUMNS + u) * steps + t] = batch * SPAN + slot
                        if turn == 0:

                            @pl.when(inner)
                            def _():
                                out_ref[base_of(e_base, batch) + slot] = inner_place(codes, starts, u, k) + n

                    return 0

                lax.fori_loop(0, count, outer_piece, 0)

    for turn in range(2):
        sender = row if turn == 0 else 1 - row
        empty(across)
        for k, count in enumerate(chunks):
            for u in range(COLUMNS):

                def row_piece(n, _, u=u, k=k):
                    t = starts[k] + n
                    need = named(block(column, 1 - sender), t, block(mirror(u), sender))
                    if u == 0:
                        lies = jnp.int32(codes["own"] * SPAN) + t
                        when = jnp.int32(0)
                    else:
                        where = eloc[(turn * COLUMNS + u) * steps + t]
                        lies = codes["edge"][0] * SPAN + where
                        when = jnp.where(where < 0, len(across), where // SPAN + 1)
                    when = jnp.where(inner, ACROSS_READY[u][k], when)
                    lies = jnp.where(inner, inner_place(codes, starts, u, k) + n, lies)
                    batch = choose(across, when)
                    yloc[(turn * COLUMNS + u) * steps + t] = -1

                    @pl.when(need & (batch >= 0))
                    def _():
                        slot = room[batch]
                        room[batch] = slot + 1
                        yloc[(turn * COLUMNS + u) * steps + t] = batch * SPAN + slot
                        if turn == 0:
                            out_ref[base_of(y_base, batch) + slot] = lies

                    return 0

                lax.fori_loop(0, count, row_piece, 0)

    flag_ref[0] = 0
    for k, count in enumerate(chunks):

        def listed_piece(n, _, k=k):
            t = starts[k] + n // list_length
            source = entry(block(column, row), t, n % list_length)
            u = mirror(source // ROWS)
            same = source % ROWS == row
            e = eloc[u * steps + t]
            y = yloc[(COLUMNS + u) * steps + t]
            first = jnp.int32(0)
            for w in (0, 2, 3):
                first = jnp.where(u == w, inner_place(codes, starts, w, k), first)
            direct = jnp.where(inner, first + t - starts[k], codes["edge"][0] * SPAN + e)
            direct = jnp.where(u == me, codes["own"] * SPAN + t, direct)
            local = inner | (u == me)
            bad = jnp.where(
                same,
                jnp.logical_not(local) & ((e < 0) | (e // SPAN > OUTWARD_DUE[k])),
                (y < 0) | (y // SPAN > ACROSS_DUE[k]),
            )
            place = jnp.where(same, direct, codes["across"][0] * SPAN + y)
            in_ref[t * list_length + n % list_length] = jnp.where(bad, codes["own"] * SPAN, place)

            @pl.when(bad)
            def _():
                flag_ref[0] = 1

            return 0

        lax.fori_loop(0, count * list_length, listed_piece, 0)


def plan(lists_all, place, steps, list_length, chunks, outward, across):
    smem = pl.BlockSpec(memory_space=pltpu.SMEM)
    slots = sum(outward) + sum(across)
    return pl.pallas_call(
        functools.partial(plan_kernel, steps, list_length, chunks, outward, across),
        in_specs=[smem, smem],
        out_specs=[smem] * 3,
        out_shape=[
            jax.ShapeDtypeStruct((slots,), jnp.int32),
            jax.ShapeDtypeStruct((steps * list_length,), jnp.int32),
            jax.ShapeDtypeStruct((1,), jnp.int32),
        ],
        scratch_shapes=[
            pltpu.SMEM((2 * COLUMNS * steps,), jnp.int32),
            pltpu.SMEM((2 * COLUMNS * steps,), jnp.int32),
            pltpu.SMEM((max(len(outward), len(across)),), jnp.int32),
        ],
        name="plan",
    )(place, lists_all)


def shared(value, axes):
    count = lax.axis_size(axes)
    rows = jnp.broadcast_to(value[None], (count,) + value.shape)
    return lax.all_to_all(rows, axes, split_axis=0, concat_axis=0, tiled=True)


def column_pairs(moves):
    return [(a * ROWS + r, b * ROWS + r) for a, b in moves for r in range(ROWS)]


def relay(embedded, lists, capacity, attention):
    steps, agents, width = embedded.shape
    list_length = lists.shape[1]
    chunks, outward, across = relay_sizes(steps, capacity)
    codes = relay_codes(outward, across)
    starts = [sum(chunks[:k]) for k in range(len(chunks))]
    e_base = [sum(outward[:b]) for b in range(len(outward))]
    y_base = [sum(outward) + sum(across[:b]) for b in range(len(across))]
    index = lax.axis_index("agent")
    place = jnp.stack([index // ROWS, index % ROWS]).astype(jnp.int32)
    send = lambda value, pairs: lax.ppermute(value, "agent", pairs)
    edges = column_pairs([(0, 1), (1, 0), (2, 3), (3, 2)])
    swap = column_pairs([(1, 2), (2, 1)])
    over = [(c * ROWS + r, c * ROWS + 1 - r) for c in range(COLUMNS) for r in range(ROWS)]
    own, edge, swapped, far, rows = (codes[n] for n in ("own", "edge", "swap", "far", "across"))
    arrays = {own: embedded}

    def pick(names):
        return {code: arrays[code] for code in names}

    def across_part(n):
        return (y_base[n], across[n], None)

    def stage(n, reads, settled, after=()):
        parts = [across_part(n)]
        if n < len(outward):
            parts.append((e_base[n], outward[n], None))
        if n == 1:
            parts.append((None, outward[1], starts[1]))
        after = tuple(arrays[rows[b]] for b in settled) + tuple(after)
        packed = pack(out_table, pick([own] + reads), parts, after)
        if n < len(outward):
            arrays[edge[n]] = send(packed[1], edges)
        arrays[rows[n]] = send(packed[0], over)
        return packed

    everyone = shared(lists.reshape(-1), "agent").reshape(-1)
    begin = jnp.minimum(everyone[0], 0)
    first = lax.dynamic_slice_in_dim(embedded, begin, chunks[0], 0)
    arrays[edge[0]] = send(first, edges)
    arrays[swapped[0]] = send(first, swap)
    out_table, in_table, flag = plan(
        everyone, place, steps, list_length, chunks, outward, across
    )
    (token,) = pack(out_table, pick([own]), [across_part(0)])
    arrays[rows[0]] = send(token, over)
    crowded = jnp.max(shared(flag, ("groups", "agent", "tm")))
    arrays[far[0]] = send(arrays[edge[0]], swap)
    reads = edge[:1] + swapped[:1]
    packed = stage(1, reads, (0,), (token, crowded.reshape(1)))
    arrays[swapped[1]] = send(packed[2], swap)
    for k in (1, 2):
        at = starts[k] - starts[1]
        arrays[far[k]] = send(arrays[edge[1]][at : at + chunks[k]], swap)
    reads = reads + edge[1:2] + far[:1]
    packed = stage(2, reads, (1,), packed[:1])
    reads = reads + edge[2:3] + swapped[1:] + far[1:2]
    packed = stage(3, reads, (2,), packed[:1])
    reads = reads + edge[3:4] + far[2:3]
    packed = stage(4, reads, (3,), packed[:1])
    done = [attention(0, chunks[0], due(arrays, codes, starts, 0), in_table, packed[:1])]
    reads = reads + edge[4:5]
    packed = stage(5, reads, (4,), (done[0][0],))
    for k in (1, 2):
        done.append(
            attention(starts[k], chunks[k], due(arrays, codes, starts, k), in_table, (packed[0], done[-1][0]))
        )
    return done, crowded


def due(arrays, codes, starts, k):
    wanted = {codes["own"], *codes["edge"][: OUTWARD_DUE[k] + 1]}
    wanted |= {inner_place(codes, starts, u, k) // SPAN for u in (0, 2, 3)}
    wanted |= set(codes["across"][: ACROSS_DUE[k] + 1])
    return {code: arrays[code] for code in sorted(wanted)}


def body(
    embedded,
    block_lists,
    done_flags,
    rewards,
    bootstrap,
    agent_proj,
    agent_merge,
    time_proj,
    time_merge,
    value_weight,
):
    steps, agents, width = embedded.shape
    list_length = block_lists.shape[2]
    blocks = lax.axis_size("agent")
    lists = block_lists[0]
    capacity = max(2, (2 * steps * list_length + blocks - 1) // blocks)
    spans = lax.axis_size("tm")
    index = lax.axis_index("tm")
    offset = (index * steps).astype(jnp.int32).reshape(1)
    boot = bootstrap.reshape(1, agents)
    forward = [(i, i + 1) for i in range(spans - 1)]
    backward = [(i + 1, i) for i in range(spans - 1)]

    def attention(first, count, arrays, table, after=()):
        residual, normed = agent_stage(
            embedded, arrays, table, first, count, list_length, agent_proj, agent_merge, after
        )
        return residual, lax.ppermute(normed, "tm", forward)

    def finish(done):
        residuals, rims = [part[0] for part in done], [part[1] for part in done]
        values, edge = time_stage(
            residuals,
            rims,
            offset,
            time_proj,
            time_merge,
            value_weight.reshape(1, width),
            done_flags,
            rewards,
            boot,
        )
        last = (index == spans - 1).astype(jnp.int32).reshape(1)
        for _ in range(max(1, spans - 1)):
            arriving = lax.ppermute(edge, "tm", backward)
            advantages, edge = advantage_stage(last, values, rewards, done_flags, boot, arriving)
        return values, advantages

    def padded():
        pool, where = exchange_slots(embedded, lists, capacity)
        return finish([attention(0, steps, {1: pool}, where + SPAN)])

    if blocks != COLUMNS * ROWS or steps % 4:
        return padded()
    done, crowded = relay(embedded, lists, capacity, attention)
    found = finish(done)
    return lax.cond(crowded > 0, padded, lambda: found)


def solution(mesh):
    placed = (
        P(("groups", "tm"), "agent", None),
        P(("groups", "agent"), "tm", None),
        P(("groups", "tm"), "agent"),
        P(("groups", "tm"), "agent"),
        P(("groups", "agent")),
        P(),
        P(),
        P(),
        P(),
        P(),
    )
    return jax.shard_map(
        body,
        mesh=mesh,
        in_specs=placed,
        out_specs=(P(("groups", "tm"), "agent"), P(("groups", "tm"), "agent")),
        check_vma=False,
    )
```

```python
import functools
import math

import jax
import jax.numpy as jnp
from jax import lax
from jax.experimental import pallas as pl
from jax.experimental.pallas import tpu as pltpu
from jax.sharding import PartitionSpec as P

HEADS = 8
WINDOW = 16
discount = 0.9997
trace_decay = 0.995
epsilon = 1e-06
bf16 = jnp.bfloat16
f32 = jnp.float32
VMEM_LIMIT = 48 * 1024 * 1024
SPAN = 1024
COLUMNS = 4
ROWS = 2


def rms(values):
    return values * lax.rsqrt(jnp.mean(values * values, axis=-1, keepdims=True) + epsilon)


def dot(a, b):
    return jnp.dot(a, b, preferred_element_type=f32)


def dot_t(a, b):
    return lax.dot_general(a, b, (((1,), (1,)), ((), ())), preferred_element_type=f32)


def attend(queries, keys, values, head_size, bias):
    rows, width = queries.shape
    scale = head_size ** (-0.5) * math.log2(math.e)
    pair = 2 * head_size
    lane = lax.broadcasted_iota(jnp.int32, (rows, pair), 1)
    first = lane < head_size
    ones = jnp.ones((keys.shape[0], pair), bf16)
    mixed = []
    for at in range(0, width, pair):
        both = queries[:, at : at + pair]
        none = jnp.zeros_like(both)
        stacked = jnp.concatenate(
            [jnp.where(first, both, none), jnp.where(first, none, both)], axis=0
        )
        scores = dot_t(stacked, keys[:, at : at + pair])
        if bias is not None:
            scores = scores + bias
        weights = jnp.exp2((scores - jnp.max(scores, axis=-1, keepdims=True)) * scale).astype(bf16)
        summed = dot(weights, jnp.concatenate([values[:, at : at + pair], ones], axis=1))
        result = summed[:, :pair] / summed[:, pair:]
        mixed.append(jnp.where(first, result[:rows], result[rows:]).astype(bf16))
    return jnp.concatenate(mixed, axis=1)


def fetch(entry, arrays, target, sem):
    for code, ref in arrays.items():

        @pl.when(entry // SPAN == code)
        def _(ref=ref):
            pltpu.make_async_copy(ref.at[entry % SPAN], target, sem).start()


def agent_kernel(
    list_length, first_step, codes, idle, head_size, table_ref, own_ref, *refs
):
    arrays = dict(zip(codes, refs))
    proj_ref, merge_ref, residual_ref, normed_ref, held_ref, sems = refs[len(codes) + idle :]
    together, agents, width = own_ref.shape
    turn = pl.program_id(0)
    pieces = [(s, j) for s in range(together) for j in range(list_length)]

    def begin(turn):
        slot = turn % 2
        for n, (s, j) in enumerate(pieces):
            entry = table_ref[(first_step + turn * together + s) * list_length + j]
            fetch(entry, arrays, held_ref.at[slot, n], sems.at[slot, n])

    @pl.when(turn == 0)
    def _():
        begin(turn)

    @pl.when(turn + 1 < pl.num_programs(0))
    def _():
        begin(turn + 1)

    slot = turn % 2
    for n in range(len(pieces)):
        pltpu.make_async_copy(refs[0].at[0], held_ref.at[slot, n], sems.at[slot, n]).wait()
    own = own_ref[...].astype(f32).reshape(together * agents, width)
    listed = held_ref[slot].astype(f32).reshape(len(pieces) * agents, width)
    mine = rms(own).astype(bf16)
    theirs = rms(listed).astype(bf16)
    queries = dot(mine, proj_ref[:, :width]).astype(bf16)
    near = dot(mine, proj_ref[:, width:]).astype(bf16)
    away = dot(theirs, proj_ref[:, width:]).astype(bf16)
    mixed = []
    for s in range(together):
        here = slice(s * agents, (s + 1) * agents)
        there = slice(s * list_length * agents, (s + 1) * list_length * agents)
        keyvals = jnp.concatenate([near[here], away[there]], axis=0)
        mixed.append(
            attend(queries[here], keyvals[:, :width], keyvals[:, width:], head_size, None)
        )
    residual = own + dot(jnp.concatenate(mixed, axis=0), merge_ref[...])
    residual_ref[...] = residual.reshape(together, agents, width)
    normed_ref[...] = rms(residual).astype(bf16).reshape(together, agents, width)


def agent_stage(embedded, arrays, table, first_step, steps, list_length, proj, merge, after=()):
    _, agents, width = embedded.shape
    together = math.gcd(steps, math.gcd(first_step, 2))
    piece = (together, agents, width)
    whole = lambda i, w: (0, 0)
    flops = 2 * steps * agents * width * width * (4 + 2 * list_length + 2 * (1 + list_length))
    return pl.pallas_call(
        functools.partial(
            agent_kernel, list_length, first_step, tuple(arrays), len(after), width // HEADS
        ),
        grid_spec=pltpu.PrefetchScalarGridSpec(
            num_scalar_prefetch=1,
            grid=(steps // together,),
            in_specs=[pl.BlockSpec(piece, lambda i, w: (first_step // together + i, 0, 0))]
            + [pl.BlockSpec(memory_space=pltpu.HBM)] * (len(arrays) + len(after))
            + [pl.BlockSpec(proj.shape, whole), pl.BlockSpec(merge.shape, whole)],
            out_specs=[pl.BlockSpec(piece, lambda i, w: (i, 0, 0))] * 2,
            scratch_shapes=[
                pltpu.VMEM((2, together * list_length, agents, width), bf16),
                pltpu.SemaphoreType.DMA((2, together * list_length)),
            ],
        ),
        out_shape=[
            jax.ShapeDtypeStruct((steps, agents, width), f32),
            jax.ShapeDtypeStruct((steps, agents, width), bf16),
        ],
        compiler_params=pltpu.CompilerParams(vmem_limit_bytes=VMEM_LIMIT),
        cost_estimate=pl.CostEstimate(
            flops=5 * flops, bytes_accessed=steps * agents * width * 12, transcendentals=0
        ),
        name="agent_stage",
    )(table, embedded, *arrays.values(), *after, proj, merge)


def pack_kernel(codes, parts, idle, table_ref, *refs):
    arrays = dict(zip(codes, refs))
    outs, (held_ref, in_sems, out_sems) = refs[len(codes) + idle : -3], refs[-3:]
    slots = []
    for out, (offset, count, first) in zip(outs, parts):
        slots += [(offset, first, n, out.at[n]) for n in range(count)]

    def guarded(offset, n, action):
        if offset is None:
            action()
        else:
            pl.when(table_ref[offset + n] >= 0)(action)

    for at, (offset, first, n, _) in enumerate(slots):
        if offset is None:
            own = arrays[0].at[first + n]
            pltpu.make_async_copy(own, held_ref.at[at], in_sems.at[at]).start()
        else:
            fetch(table_ref[offset + n], arrays, held_ref.at[at], in_sems.at[at])
    for at, (offset, first, n, target) in enumerate(slots):

        def pass_on(at=at, target=target):
            pltpu.make_async_copy(refs[0].at[0], held_ref.at[at], in_sems.at[at]).wait()
            pltpu.make_async_copy(held_ref.at[at], target, out_sems.at[at]).start()

        guarded(offset, n, pass_on)
    for at, (offset, first, n, target) in enumerate(slots):

        def finish(at=at, target=target):
            pltpu.make_async_copy(held_ref.at[at], target, out_sems.at[at]).wait()

        guarded(offset, n, finish)


def pack(table, arrays, parts, after=()):
    piece = next(iter(arrays.values())).shape[1:]
    slots = sum(count for _, count, _ in parts)
    return pl.pallas_call(
        functools.partial(pack_kernel, tuple(arrays), tuple(parts), len(after)),
        in_specs=[pl.BlockSpec(memory_space=pltpu.SMEM)]
        + [pl.BlockSpec(memory_space=pltpu.HBM)] * (len(arrays) + len(after)),
        out_specs=[pl.BlockSpec(memory_space=pltpu.HBM)] * len(parts),
        out_shape=[jax.ShapeDtypeStruct((count,) + piece, bf16) for _, count, _ in parts],
        scratch_shapes=[
            pltpu.VMEM((slots,) + piece, bf16),
            pltpu.SemaphoreType.DMA((slots,)),
            pltpu.SemaphoreType.DMA((slots,)),
        ],
        cost_estimate=pl.CostEstimate(
            flops=0, bytes_accessed=piece[0] * piece[1], transcendentals=0
        ),
        compiler_params=pltpu.CompilerParams(vmem_limit_bytes=VMEM_LIMIT),
        name="pack",
    )(table, *arrays.values(), *after)


def suffix(values, rewards, done, next_value, next_advantage):
    steps = values.shape[0]
    living = 1.0 - done.astype(f32)
    running, following, rows = next_advantage, next_value, [None] * steps
    for step in range(steps - 1, -1, -1):
        alive = living[step : step + 1]
        value = values[step : step + 1]
        change = rewards[step : step + 1] + discount * alive * following - value
        running = change + discount * trace_decay * alive * running
        rows[step] = running
        following = value
    return rows


def time_kernel(parts, steps, tile, head_size, offset_ref, *refs):
    refs = list(refs)
    residual_refs = [refs.pop(0) for _ in range(parts)]
    rim_refs = [refs.pop(0) for _ in range(parts)]
    proj_ref, merge_ref, weight_ref, done_ref, rewards_ref, boot_ref = refs[:6]
    values_ref, edge_ref, bias_ref = refs[6:]
    width = proj_ref.shape[0]
    turn = pl.program_id(0)
    group = 8
    rows = steps * group
    agents = values_ref.shape[1]

    @pl.when(turn == 0)
    def _():
        r = lax.broadcasted_iota(jnp.int32, (2 * rows, 2 * rows), 0) % rows
        c = lax.broadcasted_iota(jnp.int32, (2 * rows, 2 * rows), 1)
        query_step = r // group
        key_step = c // group - steps
        allowed = (
            (r % group == c % group)
            & (key_step <= query_step)
            & (key_step > query_step - WINDOW)
            & (key_step + offset_ref[0] >= 0)
        )
        bias_ref[...] = jnp.where(allowed, 0.0, -1e30)
        values_ref[...] = jnp.zeros_like(values_ref)

    def pieces(part_refs):
        whole = jnp.concatenate([ref[...].astype(f32) for ref in part_refs], axis=0)
        return [
            whole[:, at : at + group].reshape(rows, width) for at in range(0, tile, group)
        ]

    residuals = pieces(residual_refs)
    current = jnp.concatenate([rms(r).astype(bf16) for r in residuals], axis=0)
    behind = jnp.concatenate([r.astype(bf16) for r in pieces(rim_refs)], axis=0)
    projected = dot(current, proj_ref[...]).astype(bf16)
    before = dot(behind, proj_ref[:, width:]).astype(bf16)
    bias = bias_ref[...]
    mixed = []
    for at in range(0, tile * steps, rows):
        mine, past = projected[at : at + rows], before[at : at + rows]
        keys = jnp.concatenate([past[:, :width], mine[:, width : 2 * width]], axis=0)
        held = jnp.concatenate([past[:, width:], mine[:, 2 * width :]], axis=0)
        mixed.append(attend(mine[:, :width], keys, held, head_size, bias))
    merged = dot(jnp.concatenate(mixed, axis=0), merge_ref[...])
    lane = lax.broadcasted_iota(jnp.int32, (steps, group, agents), 2)
    place = lax.broadcasted_iota(jnp.int32, (steps, group, agents), 1)
    total = values_ref[...]
    for n, residual in enumerate(residuals):
        final = rms(residual + merged[n * rows : (n + 1) * rows])
        value = jnp.sum(final * weight_ref[...], axis=-1, keepdims=True)
        spot = lane == place + (turn * tile + n * group)
        total = total + jnp.sum(
            jnp.where(spot, value.reshape(steps, group, 1), 0.0), axis=1
        )
    values_ref[...] = total

    @pl.when(turn == pl.num_programs(0) - 1)
    def _():
        found = values_ref[...]
        boot = boot_ref[...]
        advantages = suffix(found, rewards_ref[...], done_ref[...], boot, jnp.zeros_like(boot))
        edge_ref[...] = jnp.concatenate([found[:1], advantages[0]], axis=0)


def time_stage(residuals, rims, offset, proj, merge, weight, done, rewards, boot):
    part_steps = [r.shape[0] for r in residuals]
    steps = sum(part_steps)
    _, agents, width = residuals[0].shape
    tile = 16
    whole = lambda i, o: (0, 0)

    def blocks(arrays):
        return [
            pl.BlockSpec((array.shape[0], tile, width), lambda i, o: (0, i, 0))
            for array in arrays
        ]

    rows = 16 * steps
    fixed = [proj, merge, weight, done, rewards, boot]
    return pl.pallas_call(
        functools.partial(time_kernel, len(residuals), steps, tile, width // HEADS),
        grid_spec=pltpu.PrefetchScalarGridSpec(
            num_scalar_prefetch=1,
            grid=(agents // tile,),
            in_specs=blocks(residuals)
            + blocks(rims)
            + [pl.BlockSpec(array.shape, whole) for array in fixed],
            out_specs=[
                pl.BlockSpec((steps, agents), whole),
                pl.BlockSpec((2, agents), whole),
            ],
            scratch_shapes=[pltpu.VMEM((rows, rows), f32)],
        ),
        out_shape=[
            jax.ShapeDtypeStruct((steps, agents), f32),
            jax.ShapeDtypeStruct((2, agents), f32),
        ],
        compiler_params=pltpu.CompilerParams(vmem_limit_bytes=VMEM_LIMIT),
        name="time_stage",
    )(offset, *residuals, *rims, *fixed)


def advantage_kernel(last_ref, values_ref, rewards_ref, done_ref, boot_ref, edge_ref, out_ref, mine_ref):
    last = last_ref[0] > 0
    arriving = edge_ref[...]
    boot = boot_ref[...]
    found = values_ref[...]
    next_value = jnp.where(last, boot, arriving[:1])
    next_advantage = jnp.where(last, 0.0, arriving[1:2])
    rows = suffix(found, rewards_ref[...], done_ref[...], next_value, next_advantage)
    out_ref[...] = jnp.concatenate(rows, axis=0)
    mine_ref[...] = jnp.concatenate([found[:1], rows[0]], axis=0)


def advantage_stage(last, values, rewards, done, boot, edge):
    return pl.pallas_call(
        advantage_kernel,
        in_specs=[pl.BlockSpec(memory_space=pltpu.SMEM)]
        + [pl.BlockSpec(memory_space=pltpu.VMEM)] * 5,
        out_specs=[pl.BlockSpec(memory_space=pltpu.VMEM)] * 2,
        out_shape=[
            jax.ShapeDtypeStruct(values.shape, f32),
            jax.ShapeDtypeStruct(edge.shape, f32),
        ],
        name="advantage_stage",
    )(last, values, rewards, done, boot, edge)


def exchange_slots(embedded, lists, capacity):
    steps, agents, width = embedded.shape
    blocks = lax.axis_size("agent")
    list_length = lists.shape[1]
    named = lists.reshape(-1)
    row_steps = jnp.arange(named.shape[0], dtype=jnp.int32) // list_length
    hits = (named[:, None] == jnp.arange(blocks, dtype=jnp.int32)[None, :]).astype(jnp.int32)
    slot = jnp.sum((jnp.cumsum(hits, axis=0) - hits) * hits, axis=1)
    slot_hits = (slot[:, None] == jnp.arange(capacity, dtype=jnp.int32)[None, :]).astype(jnp.int32)
    requests = jnp.sum(
        (hits * row_steps[:, None])[:, :, None] * slot_hits[:, None, :], axis=0
    )
    wanted = lax.all_to_all(requests, "agent", split_axis=0, concat_axis=0, tiled=True)
    outgoing = embedded[wanted.reshape(-1)].reshape(blocks, capacity, agents, width)
    arrived = lax.all_to_all(outgoing, "agent", split_axis=0, concat_axis=0, tiled=True)
    return arrived.reshape(blocks * capacity, agents, width), named * capacity + slot


OUTWARD_READY = {1: (0, 1, 1), 2: (1, 3, 3), 3: (2, 3, 4)}
ACROSS_READY = {0: (1, 2, 2), 1: (0, 0, 0), 2: (1, 3, 3), 3: (2, 3, 4)}
OUTWARD_DUE = (3, 4, 4)
ACROSS_DUE = (3, 4, 5)


def relay_sizes(steps, capacity):
    half, quarter = steps // 2, steps // 4
    chunks = [half, quarter, quarter]
    outward = [half, half, half, half, quarter + 2]
    across = [quarter, half, half, half - 1, quarter + 2, quarter + 2]
    return chunks, outward, across


def relay_codes(outward, across):
    names = {}
    code = 1
    for name, count in (("edge", len(outward)), ("swap", 2), ("far", 3), ("across", len(across))):
        names[name] = [code + n for n in range(count)]
        code += count
    names["own"] = 0
    return names


def inner_place(codes, starts, u, k):
    behind = starts[k] - starts[min(k, 1)]
    if u == 0:
        return codes["edge"][min(k, 1)] * SPAN + behind
    if u == 1:
        return codes["own"] * SPAN + starts[k]
    if u == 2:
        return codes["swap"][min(k, 1)] * SPAN + behind
    return codes["far"][k] * SPAN


def plan_kernel(steps, list_length, chunks, outward, across, place_ref, lists_ref, out_ref, in_ref, flag_ref, eloc, yloc, room):
    codes = relay_codes(outward, across)
    column, row = place_ref[0], place_ref[1]
    far_side = column >= COLUMNS // 2
    mirror = lambda u: jnp.where(far_side, COLUMNS - 1 - u, u)
    me = mirror(column)
    inner = me == 1
    starts = [sum(chunks[:k]) for k in range(len(chunks))]
    e_base = [sum(outward[:b]) for b in range(len(outward))]
    y_base = [sum(outward) + sum(across[:b]) for b in range(len(across))]
    block = lambda c, r: c * ROWS + r
    entry = lambda c, r, t, j: lists_ref[((c * ROWS + r) * steps + t) * list_length + j]

    def clear(n, _):
        out_ref[n] = -1
        return 0

    lax.fori_loop(0, sum(outward) + sum(across), clear, 0)

    @pl.when(me == 0)
    def _():
        for n in range(outward[1]):
            out_ref[e_base[1] + n] = codes["own"] * SPAN + starts[1] + n

    def named(place, r, t, source):
        hit = entry(place, r, t, 0) == source
        for j in range(1, list_length):
            hit = hit | (entry(place, r, t, j) == source)
        return hit

    def choose(sizes, ready):
        batch = jnp.int32(-1)
        for b in range(len(sizes) - 1, -1, -1):
            batch = jnp.where((room[b] < sizes[b]) & (b >= ready), b, batch)
        return batch

    def base_of(bases, batch):
        base = jnp.int32(0)
        for b, value in enumerate(bases):
            base = jnp.where(batch == b, value, base)
        return base

    def empty(sizes):
        for b in range(len(sizes)):
            room[b] = 0

    for turn in range(2):
        sender = row if turn == 0 else 1 - row
        empty(outward)
        room[0] = outward[0]
        for k, count in enumerate(chunks):
            for u in (1, 2, 3):

                def first_piece(n, _):
                    eloc[(turn * COLUMNS + 1) * steps + n] = n
                    return 0

                if u == 1 and k == 0:
                    lax.fori_loop(0, count, first_piece, 0)
                    continue

                def outer_piece(n, _, u=u, k=k):
                    t = starts[k] + n
                    source = block(mirror(u), sender)
                    need = named(0, 0, t, source)
                    for r in range(1, ROWS):
                        need = need | named(0, r, t, source)
                    batch = choose(outward, OUTWARD_READY[u][k])
                    eloc[(turn * COLUMNS + u) * steps + t] = -1

                    @pl.when(need & (batch >= 0))
                    def _():
                        slot = room[batch]
                        room[batch] = slot + 1
                        eloc[(turn * COLUMNS + u) * steps + t] = batch * SPAN + slot
                        if turn == 0:

                            @pl.when(inner)
                            def _():
                                out_ref[base_of(e_base, batch) + slot] = inner_place(codes, starts, u, k) + n

                    return 0

                lax.fori_loop(0, count, outer_piece, 0)

    for turn in range(2):
        sender = row if turn == 0 else 1 - row
        empty(across)
        for k, count in enumerate(chunks):
            for u in range(COLUMNS):

                def row_piece(n, _, u=u, k=k):
                    t = starts[k] + n
                    need = named(me, 1 - sender, t, block(mirror(u), sender))
                    if u == 0:
                        lies = jnp.int32(codes["own"] * SPAN) + t
                        when = jnp.int32(0)
                    else:
                        where = eloc[(turn * COLUMNS + u) * steps + t]
                        lies = codes["edge"][0] * SPAN + where
                        when = jnp.where(where < 0, len(across), where // SPAN + 1)
                    when = jnp.where(inner, ACROSS_READY[u][k], when)
                    lies = jnp.where(inner, inner_place(codes, starts, u, k) + n, lies)
                    batch = choose(across, when)
                    yloc[(turn * COLUMNS + u) * steps + t] = -1

                    @pl.when(need & (batch >= 0))
                    def _():
                        slot = room[batch]
                        room[batch] = slot + 1
                        yloc[(turn * COLUMNS + u) * steps + t] = batch * SPAN + slot
                        if turn == 0:
                            out_ref[base_of(y_base, batch) + slot] = lies

                    return 0

                lax.fori_loop(0, count, row_piece, 0)

    flag_ref[0] = 0
    for k, count in enumerate(chunks):

        def listed_piece(n, _, k=k):
            t = starts[k] + n // list_length
            source = entry(me, row, t, n % list_length)
            u = mirror(source // ROWS)
            same = source % ROWS == row
            e = eloc[u * steps + t]
            y = yloc[(COLUMNS + u) * steps + t]
            first = jnp.int32(0)
            for w in (0, 2, 3):
                first = jnp.where(u == w, inner_place(codes, starts, w, k), first)
            direct = jnp.where(inner, first + t - starts[k], codes["edge"][0] * SPAN + e)
            direct = jnp.where(u == me, codes["own"] * SPAN + t, direct)
            local = inner | (u == me)
            bad = jnp.where(
                same,
                jnp.logical_not(local) & ((e < 0) | (e // SPAN > OUTWARD_DUE[k])),
                (y < 0) | (y // SPAN > ACROSS_DUE[k]),
            )
            place = jnp.where(same, direct, codes["across"][0] * SPAN + y)
            in_ref[t * list_length + n % list_length] = jnp.where(bad, codes["own"] * SPAN, place)

            @pl.when(bad)
            def _():
                flag_ref[0] = 1

            return 0

        lax.fori_loop(0, count * list_length, listed_piece, 0)


def plan(lists_near, place, steps, list_length, chunks, outward, across):
    smem = pl.BlockSpec(memory_space=pltpu.SMEM)
    slots = sum(outward) + sum(across)
    return pl.pallas_call(
        functools.partial(plan_kernel, steps, list_length, chunks, outward, across),
        in_specs=[smem, smem],
        out_specs=[smem] * 3,
        out_shape=[
            jax.ShapeDtypeStruct((slots,), jnp.int32),
            jax.ShapeDtypeStruct((steps * list_length,), jnp.int32),
            jax.ShapeDtypeStruct((1,), jnp.int32),
        ],
        scratch_shapes=[
            pltpu.SMEM((2 * COLUMNS * steps,), jnp.int32),
            pltpu.SMEM((2 * COLUMNS * steps,), jnp.int32),
            pltpu.SMEM((max(len(outward), len(across)),), jnp.int32),
        ],
        name="plan",
    )(place, lists_near)


def shared(value, axes):
    count = lax.axis_size(axes)
    rows = jnp.broadcast_to(value[None], (count,) + value.shape)
    return lax.all_to_all(rows, axes, split_axis=0, concat_axis=0, tiled=True)


def column_pairs(moves):
    return [(a * ROWS + r, b * ROWS + r) for a, b in moves for r in range(ROWS)]


def relay(embedded, lists, capacity, attention):
    steps, agents, width = embedded.shape
    list_length = lists.shape[1]
    chunks, outward, across = relay_sizes(steps, capacity)
    codes = relay_codes(outward, across)
    starts = [sum(chunks[:k]) for k in range(len(chunks))]
    e_base = [sum(outward[:b]) for b in range(len(outward))]
    y_base = [sum(outward) + sum(across[:b]) for b in range(len(across))]
    index = lax.axis_index("agent")
    place = jnp.stack([index // ROWS, index % ROWS]).astype(jnp.int32)
    send = lambda value, pairs: lax.ppermute(value, "agent", pairs)
    edges = column_pairs([(0, 1), (1, 0), (2, 3), (3, 2)])
    swap = column_pairs([(1, 2), (2, 1)])
    over = [(c * ROWS + r, c * ROWS + 1 - r) for c in range(COLUMNS) for r in range(ROWS)]
    own, edge, swapped, far, rows = (codes[n] for n in ("own", "edge", "swap", "far", "across"))
    arrays = {own: embedded}

    def pick(names):
        return {code: arrays[code] for code in names}

    def across_part(n):
        return (y_base[n], across[n], None)

    def stage(n, reads, settled, after=()):
        parts = [across_part(n)]
        if n < len(outward):
            parts.append((e_base[n], outward[n], None))
        if n == 1:
            parts.append((None, outward[1], starts[1]))
        after = tuple(arrays[rows[b]] for b in settled) + tuple(after)
        packed = pack(out_table, pick([own] + reads), parts, after)
        if n < len(outward):
            arrays[edge[n]] = send(packed[1], edges)
        arrays[rows[n]] = send(packed[0], over)
        return packed

    mine = lists.reshape(-1)
    beside = send(mine, over)
    pair = jnp.stack([jnp.where(index % ROWS == r, mine, beside) for r in range(ROWS)])
    inward = column_pairs([(0, 1), (COLUMNS - 1, COLUMNS - 2)])
    outer_pair = send(pair, inward)
    column = index // ROWS
    outer = (column == 0) | (column == COLUMNS - 1)
    near = jnp.concatenate([jnp.where(outer, pair, outer_pair), pair], axis=0).reshape(-1)
    begin = jnp.minimum(near[0], 0)
    first = lax.dynamic_slice_in_dim(embedded, begin, chunks[0], 0)
    arrays[edge[0]] = send(first, edges)
    arrays[swapped[0]] = send(first, swap)
    out_table, in_table, flag = plan(
        near, place, steps, list_length, chunks, outward, across
    )
    (token,) = pack(out_table, pick([own]), [across_part(0)])
    arrays[rows[0]] = send(token, over)
    crowded = jnp.max(shared(flag, ("groups", "agent", "tm")))
    arrays[far[0]] = send(arrays[edge[0]], swap)
    reads = edge[:1] + swapped[:1]
    packed = stage(1, reads, (0,), (token, crowded.reshape(1)))
    arrays[swapped[1]] = send(packed[2], swap)
    for k in (1, 2):
        at = starts[k] - starts[1]
        arrays[far[k]] = send(arrays[edge[1]][at : at + chunks[k]], swap)
    reads = reads + edge[1:2] + far[:1]
    packed = stage(2, reads, (1,), packed[:1])
    reads = reads + edge[2:3] + swapped[1:] + far[1:2]
    packed = stage(3, reads, (2,), packed[:1])
    reads = reads + edge[3:4] + far[2:3]
    packed = stage(4, reads, (3,), packed[:1])
    done = [attention(0, chunks[0], due(arrays, codes, starts, 0), in_table, packed[:1])]
    reads = reads + edge[4:5]
    packed = stage(5, reads, (4,), (done[0][0],))
    for k in (1, 2):
        done.append(
            attention(starts[k], chunks[k], due(arrays, codes, starts, k), in_table, (packed[0], done[-1][0]))
        )
    return done, crowded


def due(arrays, codes, starts, k):
    wanted = {codes["own"], *codes["edge"][: OUTWARD_DUE[k] + 1]}
    wanted |= {inner_place(codes, starts, u, k) // SPAN for u in (0, 2, 3)}
    wanted |= set(codes["across"][: ACROSS_DUE[k] + 1])
    return {code: arrays[code] for code in sorted(wanted)}


def body(
    embedded,
    block_lists,
    done_flags,
    rewards,
    bootstrap,
    agent_proj,
    agent_merge,
    time_proj,
    time_merge,
    value_weight,
):
    steps, agents, width = embedded.shape
    list_length = block_lists.shape[2]
    blocks = lax.axis_size("agent")
    lists = block_lists[0]
    capacity = max(2, (2 * steps * list_length + blocks - 1) // blocks)
    spans = lax.axis_size("tm")
    index = lax.axis_index("tm")
    offset = (index * steps).astype(jnp.int32).reshape(1)
    boot = bootstrap.reshape(1, agents)
    forward = [(i, i + 1) for i in range(spans - 1)]
    backward = [(i + 1, i) for i in range(spans - 1)]

    def attention(first, count, arrays, table, after=()):
        residual, normed = agent_stage(
            embedded, arrays, table, first, count, list_length, agent_proj, agent_merge, after
        )
        return residual, lax.ppermute(normed, "tm", forward)

    def finish(done):
        residuals, rims = [part[0] for part in done], [part[1] for part in done]
        values, edge = time_stage(
            residuals,
            rims,
            offset,
            time_proj,
            time_merge,
            value_weight.reshape(1, width),
            done_flags,
            rewards,
            boot,
        )
        last = (index == spans - 1).astype(jnp.int32).reshape(1)
        for _ in range(max(1, spans - 1)):
            arriving = lax.ppermute(edge, "tm", backward)
            advantages, edge = advantage_stage(last, values, rewards, done_flags, boot, arriving)
        return values, advantages

    def padded():
        pool, where = exchange_slots(embedded, lists, capacity)
        return finish([attention(0, steps, {1: pool}, where + SPAN)])

    if blocks != COLUMNS * ROWS or steps % 4:
        return padded()
    done, crowded = relay(embedded, lists, capacity, attention)
    found = finish(done)
    return lax.cond(crowded > 0, padded, lambda: found)


def solution(mesh):
    placed = (
        P(("groups", "tm"), "agent", None),
        P(("groups", "agent"), "tm", None),
        P(("groups", "tm"), "agent"),
        P(("groups", "tm"), "agent"),
        P(("groups", "agent")),
        P(),
        P(),
        P(),
        P(),
        P(),
    )
    return jax.shard_map(
        body,
        mesh=mesh,
        in_specs=placed,
        out_specs=(P(("groups", "tm"), "agent"), P(("groups", "tm"), "agent")),
        check_vma=False,
    )
```

```python
import functools
import math

import jax
import jax.numpy as jnp
from jax import lax
from jax.experimental import pallas as pl
from jax.experimental.pallas import tpu as pltpu
from jax.sharding import PartitionSpec as P

HEADS = 8
WINDOW = 16
discount = 0.9997
trace_decay = 0.995
epsilon = 1e-06
bf16 = jnp.bfloat16
f32 = jnp.float32
VMEM_LIMIT = 48 * 1024 * 1024
SPAN = 1024
COLUMNS = 4
ROWS = 2


def rms(values):
    return values * lax.rsqrt(jnp.mean(values * values, axis=-1, keepdims=True) + epsilon)


def dot(a, b):
    return jnp.dot(a, b, preferred_element_type=f32)


def dot_t(a, b):
    return lax.dot_general(a, b, (((1,), (1,)), ((), ())), preferred_element_type=f32)


def attend(queries, keys, values, head_size, bias):
    rows, width = queries.shape
    scale = head_size ** (-0.5) * math.log2(math.e)
    pair = 2 * head_size
    lane = lax.broadcasted_iota(jnp.int32, (rows, pair), 1)
    first = lane < head_size
    ones = jnp.ones((keys.shape[0], pair), bf16)
    mixed = []
    for at in range(0, width, pair):
        both = queries[:, at : at + pair]
        none = jnp.zeros_like(both)
        stacked = jnp.concatenate(
            [jnp.where(first, both, none), jnp.where(first, none, both)], axis=0
        )
        scores = dot_t(stacked, keys[:, at : at + pair])
        if bias is not None:
            scores = scores + bias
        weights = jnp.exp2((scores - jnp.max(scores, axis=-1, keepdims=True)) * scale).astype(bf16)
        summed = dot(weights, jnp.concatenate([values[:, at : at + pair], ones], axis=1))
        result = summed[:, :pair] / summed[:, pair:]
        mixed.append(jnp.where(first, result[:rows], result[rows:]).astype(bf16))
    return jnp.concatenate(mixed, axis=1)


def fetch(entry, arrays, target, sem):
    for code, ref in arrays.items():

        @pl.when(entry // SPAN == code)
        def _(ref=ref):
            pltpu.make_async_copy(ref.at[entry % SPAN], target, sem).start()


def own_kernel(idle, own_ref, proj_ref, *refs):
    projected_ref = refs[idle]
    together, agents, width = own_ref.shape
    mine = rms(own_ref[...].astype(f32).reshape(together * agents, width)).astype(bf16)
    projected = dot(mine, proj_ref[...]).astype(bf16)
    projected_ref[...] = projected.reshape(together, agents, proj_ref.shape[1])


def own_stage(embedded, proj, after=()):
    steps, agents, width = embedded.shape
    together = math.gcd(steps, 4)
    return pl.pallas_call(
        functools.partial(own_kernel, len(after)),
        grid=(steps // together,),
        in_specs=[
            pl.BlockSpec((together, agents, width), lambda i: (i, 0, 0)),
            pl.BlockSpec(proj.shape, lambda i: (0, 0)),
        ]
        + [pl.BlockSpec(memory_space=pltpu.HBM)] * len(after),
        out_specs=pl.BlockSpec((together, agents, proj.shape[1]), lambda i: (i, 0, 0)),
        out_shape=jax.ShapeDtypeStruct((steps, agents, proj.shape[1]), bf16),
        compiler_params=pltpu.CompilerParams(vmem_limit_bytes=VMEM_LIMIT),
        name="own_stage",
    )(embedded, proj, *after)


def agent_kernel(
    list_length, first_step, codes, idle, head_size, table_ref, own_ref, projected_ref, *refs
):
    arrays = dict(zip(codes, refs))
    proj_ref, merge_ref, residual_ref, normed_ref, held_ref, sems = refs[len(codes) + idle :]
    together, agents, width = own_ref.shape
    turn = pl.program_id(0)
    pieces = [(s, j) for s in range(together) for j in range(list_length)]

    def begin(turn):
        slot = turn % 2
        for n, (s, j) in enumerate(pieces):
            entry = table_ref[(first_step + turn * together + s) * list_length + j]
            fetch(entry, arrays, held_ref.at[slot, n], sems.at[slot, n])

    @pl.when(turn == 0)
    def _():
        begin(turn)

    @pl.when(turn + 1 < pl.num_programs(0))
    def _():
        begin(turn + 1)

    slot = turn % 2
    for n in range(len(pieces)):
        pltpu.make_async_copy(refs[0].at[0], held_ref.at[slot, n], sems.at[slot, n]).wait()
    own = own_ref[...].astype(f32).reshape(together * agents, width)
    listed = held_ref[slot].astype(f32).reshape(len(pieces) * agents, width)
    theirs = rms(listed).astype(bf16)
    projected = projected_ref[...].reshape(together * agents, 3 * width)
    queries, near = projected[:, :width], projected[:, width:]
    away = dot(theirs, proj_ref[:, width:]).astype(bf16)
    mixed = []
    for s in range(together):
        here = slice(s * agents, (s + 1) * agents)
        there = slice(s * list_length * agents, (s + 1) * list_length * agents)
        keyvals = jnp.concatenate([near[here], away[there]], axis=0)
        mixed.append(
            attend(queries[here], keyvals[:, :width], keyvals[:, width:], head_size, None)
        )
    residual = own + dot(jnp.concatenate(mixed, axis=0), merge_ref[...])
    residual_ref[...] = residual.reshape(together, agents, width)
    normed_ref[...] = rms(residual).astype(bf16).reshape(together, agents, width)


def agent_stage(
    embedded, projected, arrays, table, first_step, steps, list_length, proj, merge, after=()
):
    _, agents, width = embedded.shape
    together = math.gcd(steps, math.gcd(first_step, 4))
    piece = (together, agents, width)
    whole = lambda i, w: (0, 0)
    flops = 2 * steps * agents * width * width * (4 + 2 * list_length + 2 * (1 + list_length))
    return pl.pallas_call(
        functools.partial(
            agent_kernel, list_length, first_step, tuple(arrays), len(after), width // HEADS
        ),
        grid_spec=pltpu.PrefetchScalarGridSpec(
            num_scalar_prefetch=1,
            grid=(steps // together,),
            in_specs=[
                pl.BlockSpec((together, agents, cols), lambda i, w: (first_step // together + i, 0, 0))
                for cols in (width, 3 * width)
            ]
            + [pl.BlockSpec(memory_space=pltpu.HBM)] * (len(arrays) + len(after))
            + [pl.BlockSpec(proj.shape, whole), pl.BlockSpec(merge.shape, whole)],
            out_specs=[pl.BlockSpec(piece, lambda i, w: (i, 0, 0))] * 2,
            scratch_shapes=[
                pltpu.VMEM((2, together * list_length, agents, width), bf16),
                pltpu.SemaphoreType.DMA((2, together * list_length)),
            ],
        ),
        out_shape=[
            jax.ShapeDtypeStruct((steps, agents, width), f32),
            jax.ShapeDtypeStruct((steps, agents, width), bf16),
        ],
        compiler_params=pltpu.CompilerParams(vmem_limit_bytes=VMEM_LIMIT),
        cost_estimate=pl.CostEstimate(
            flops=5 * flops, bytes_accessed=steps * agents * width * 12, transcendentals=0
        ),
        name="agent_stage",
    )(table, embedded, projected, *arrays.values(), *after, proj, merge)


def pack_kernel(codes, parts, idle, table_ref, *refs):
    arrays = dict(zip(codes, refs))
    outs, (held_ref, in_sems, out_sems) = refs[len(codes) + idle : -3], refs[-3:]
    slots = []
    for out, (offset, count, first) in zip(outs, parts):
        slots += [(offset, first, n, out.at[n]) for n in range(count)]

    def guarded(offset, n, action):
        if offset is None:
            action()
        else:
            pl.when(table_ref[offset + n] >= 0)(action)

    for at, (offset, first, n, _) in enumerate(slots):
        if offset is None:
            own = arrays[0].at[first + n]
            pltpu.make_async_copy(own, held_ref.at[at], in_sems.at[at]).start()
        else:
            fetch(table_ref[offset + n], arrays, held_ref.at[at], in_sems.at[at])
    for at, (offset, first, n, target) in enumerate(slots):

        def pass_on(at=at, target=target):
            pltpu.make_async_copy(refs[0].at[0], held_ref.at[at], in_sems.at[at]).wait()
            pltpu.make_async_copy(held_ref.at[at], target, out_sems.at[at]).start()

        guarded(offset, n, pass_on)
    for at, (offset, first, n, target) in enumerate(slots):

        def finish(at=at, target=target):
            pltpu.make_async_copy(held_ref.at[at], target, out_sems.at[at]).wait()

        guarded(offset, n, finish)


def pack(table, arrays, parts, after=()):
    piece = next(iter(arrays.values())).shape[1:]
    slots = sum(count for _, count, _ in parts)
    return pl.pallas_call(
        functools.partial(pack_kernel, tuple(arrays), tuple(parts), len(after)),
        in_specs=[pl.BlockSpec(memory_space=pltpu.SMEM)]
        + [pl.BlockSpec(memory_space=pltpu.HBM)] * (len(arrays) + len(after)),
        out_specs=[pl.BlockSpec(memory_space=pltpu.HBM)] * len(parts),
        out_shape=[jax.ShapeDtypeStruct((count,) + piece, bf16) for _, count, _ in parts],
        scratch_shapes=[
            pltpu.VMEM((slots,) + piece, bf16),
            pltpu.SemaphoreType.DMA((slots,)),
            pltpu.SemaphoreType.DMA((slots,)),
        ],
        cost_estimate=pl.CostEstimate(
            flops=0, bytes_accessed=piece[0] * piece[1], transcendentals=0
        ),
        compiler_params=pltpu.CompilerParams(vmem_limit_bytes=VMEM_LIMIT),
        name="pack",
    )(table, *arrays.values(), *after)


def suffix(values, rewards, done, next_value, next_advantage):
    steps = values.shape[0]
    living = 1.0 - done.astype(f32)
    running, following, rows = next_advantage, next_value, [None] * steps
    for step in range(steps - 1, -1, -1):
        alive = living[step : step + 1]
        value = values[step : step + 1]
        change = rewards[step : step + 1] + discount * alive * following - value
        running = change + discount * trace_decay * alive * running
        rows[step] = running
        following = value
    return rows


def time_kernel(parts, steps, tile, head_size, offset_ref, *refs):
    refs = list(refs)
    residual_refs = [refs.pop(0) for _ in range(parts)]
    rim_refs = [refs.pop(0) for _ in range(parts)]
    proj_ref, merge_ref, weight_ref, done_ref, rewards_ref, boot_ref = refs[:6]
    values_ref, edge_ref, bias_ref = refs[6:]
    width = proj_ref.shape[0]
    turn = pl.program_id(0)
    group = 8
    rows = steps * group
    agents = values_ref.shape[1]

    @pl.when(turn == 0)
    def _():
        r = lax.broadcasted_iota(jnp.int32, (2 * rows, 2 * rows), 0) % rows
        c = lax.broadcasted_iota(jnp.int32, (2 * rows, 2 * rows), 1)
        query_step = r // group
        key_step = c // group - steps
        allowed = (
            (r % group == c % group)
            & (key_step <= query_step)
            & (key_step > query_step - WINDOW)
            & (key_step + offset_ref[0] >= 0)
        )
        bias_ref[...] = jnp.where(allowed, 0.0, -1e30)
        values_ref[...] = jnp.zeros_like(values_ref)

    def pieces(part_refs):
        whole = jnp.concatenate([ref[...].astype(f32) for ref in part_refs], axis=0)
        return [
            whole[:, at : at + group].reshape(rows, width) for at in range(0, tile, group)
        ]

    residuals = pieces(residual_refs)
    current = jnp.concatenate([rms(r).astype(bf16) for r in residuals], axis=0)
    behind = jnp.concatenate([r.astype(bf16) for r in pieces(rim_refs)], axis=0)
    projected = dot(current, proj_ref[...]).astype(bf16)
    before = dot(behind, proj_ref[:, width:]).astype(bf16)
    bias = bias_ref[...]
    mixed = []
    for at in range(0, tile * steps, rows):
        mine, past = projected[at : at + rows], before[at : at + rows]
        keys = jnp.concatenate([past[:, :width], mine[:, width : 2 * width]], axis=0)
        held = jnp.concatenate([past[:, width:], mine[:, 2 * width :]], axis=0)
        mixed.append(attend(mine[:, :width], keys, held, head_size, bias))
    merged = dot(jnp.concatenate(mixed, axis=0), merge_ref[...])
    lane = lax.broadcasted_iota(jnp.int32, (steps, group, agents), 2)
    place = lax.broadcasted_iota(jnp.int32, (steps, group, agents), 1)
    total = values_ref[...]
    for n, residual in enumerate(residuals):
        final = rms(residual + merged[n * rows : (n + 1) * rows])
        value = jnp.sum(final * weight_ref[...], axis=-1, keepdims=True)
        spot = lane == place + (turn * tile + n * group)
        total = total + jnp.sum(
            jnp.where(spot, value.reshape(steps, group, 1), 0.0), axis=1
        )
    values_ref[...] = total

    @pl.when(turn == pl.num_programs(0) - 1)
    def _():
        found = values_ref[...]
        boot = boot_ref[...]
        advantages = suffix(found, rewards_ref[...], done_ref[...], boot, jnp.zeros_like(boot))
        edge_ref[...] = jnp.concatenate([found[:1], advantages[0]], axis=0)


def time_stage(residuals, rims, offset, proj, merge, weight, done, rewards, boot):
    part_steps = [r.shape[0] for r in residuals]
    steps = sum(part_steps)
    _, agents, width = residuals[0].shape
    tile = math.gcd(agents, 32)
    whole = lambda i, o: (0, 0)

    def blocks(arrays):
        return [
            pl.BlockSpec((array.shape[0], tile, width), lambda i, o: (0, i, 0))
            for array in arrays
        ]

    rows = 16 * steps
    fixed = [proj, merge, weight, done, rewards, boot]
    return pl.pallas_call(
        functools.partial(time_kernel, len(residuals), steps, tile, width // HEADS),
        grid_spec=pltpu.PrefetchScalarGridSpec(
            num_scalar_prefetch=1,
            grid=(agents // tile,),
            in_specs=blocks(residuals)
            + blocks(rims)
            + [pl.BlockSpec(array.shape, whole) for array in fixed],
            out_specs=[
                pl.BlockSpec((steps, agents), whole),
                pl.BlockSpec((2, agents), whole),
            ],
            scratch_shapes=[pltpu.VMEM((rows, rows), f32)],
        ),
        out_shape=[
            jax.ShapeDtypeStruct((steps, agents), f32),
            jax.ShapeDtypeStruct((2, agents), f32),
        ],
        compiler_params=pltpu.CompilerParams(vmem_limit_bytes=VMEM_LIMIT),
        name="time_stage",
    )(offset, *residuals, *rims, *fixed)


def advantage_kernel(last_ref, values_ref, rewards_ref, done_ref, boot_ref, edge_ref, out_ref, mine_ref):
    last = last_ref[0] > 0
    arriving = edge_ref[...]
    boot = boot_ref[...]
    found = values_ref[...]
    next_value = jnp.where(last, boot, arriving[:1])
    next_advantage = jnp.where(last, 0.0, arriving[1:2])
    rows = suffix(found, rewards_ref[...], done_ref[...], next_value, next_advantage)
    out_ref[...] = jnp.concatenate(rows, axis=0)
    mine_ref[...] = jnp.concatenate([found[:1], rows[0]], axis=0)


def advantage_stage(last, values, rewards, done, boot, edge):
    return pl.pallas_call(
        advantage_kernel,
        in_specs=[pl.BlockSpec(memory_space=pltpu.SMEM)]
        + [pl.BlockSpec(memory_space=pltpu.VMEM)] * 5,
        out_specs=[pl.BlockSpec(memory_space=pltpu.VMEM)] * 2,
        out_shape=[
            jax.ShapeDtypeStruct(values.shape, f32),
            jax.ShapeDtypeStruct(edge.shape, f32),
        ],
        name="advantage_stage",
    )(last, values, rewards, done, boot, edge)


def exchange_slots(embedded, lists, capacity):
    steps, agents, width = embedded.shape
    blocks = lax.axis_size("agent")
    list_length = lists.shape[1]
    named = lists.reshape(-1)
    row_steps = jnp.arange(named.shape[0], dtype=jnp.int32) // list_length
    hits = (named[:, None] == jnp.arange(blocks, dtype=jnp.int32)[None, :]).astype(jnp.int32)
    slot = jnp.sum((jnp.cumsum(hits, axis=0) - hits) * hits, axis=1)
    slot_hits = (slot[:, None] == jnp.arange(capacity, dtype=jnp.int32)[None, :]).astype(jnp.int32)
    requests = jnp.sum(
        (hits * row_steps[:, None])[:, :, None] * slot_hits[:, None, :], axis=0
    )
    wanted = lax.all_to_all(requests, "agent", split_axis=0, concat_axis=0, tiled=True)
    outgoing = embedded[wanted.reshape(-1)].reshape(blocks, capacity, agents, width)
    arrived = lax.all_to_all(outgoing, "agent", split_axis=0, concat_axis=0, tiled=True)
    return arrived.reshape(blocks * capacity, agents, width), named * capacity + slot


OUTWARD_READY = {1: (0, 1, 1), 2: (1, 3, 3), 3: (2, 3, 4)}
ACROSS_READY = {0: (1, 2, 2), 1: (0, 0, 0), 2: (1, 3, 3), 3: (2, 3, 4)}
OUTWARD_DUE = (3, 4, 4)
ACROSS_DUE = (3, 4, 5)


def relay_sizes(steps, capacity):
    half, quarter = steps // 2, steps // 4
    chunks = [half, quarter, quarter]
    outward = [half, half, half, half, quarter + 2]
    across = [quarter, half, half, half - 1, quarter + 2, quarter + 2]
    return chunks, outward, across


def relay_codes(outward, across):
    names = {}
    code = 1
    for name, count in (("edge", len(outward)), ("swap", 2), ("far", 3), ("across", len(across))):
        names[name] = [code + n for n in range(count)]
        code += count
    names["own"] = 0
    return names


def inner_place(codes, starts, u, k):
    behind = starts[k] - starts[min(k, 1)]
    if u == 0:
        return codes["edge"][min(k, 1)] * SPAN + behind
    if u == 1:
        return codes["own"] * SPAN + starts[k]
    if u == 2:
        return codes["swap"][min(k, 1)] * SPAN + behind
    return codes["far"][k] * SPAN


def plan_kernel(steps, list_length, chunks, outward, across, place_ref, lists_ref, out_ref, in_ref, flag_ref, eloc, yloc, room):
    codes = relay_codes(outward, across)
    column, row = place_ref[0], place_ref[1]
    far_side = column >= COLUMNS // 2
    mirror = lambda u: jnp.where(far_side, COLUMNS - 1 - u, u)
    me = mirror(column)
    inner = me == 1
    starts = [sum(chunks[:k]) for k in range(len(chunks))]
    e_base = [sum(outward[:b]) for b in range(len(outward))]
    y_base = [sum(outward) + sum(across[:b]) for b in range(len(across))]
    block = lambda c, r: c * ROWS + r
    entry = lambda c, r, t, j: lists_ref[((c * ROWS + r) * steps + t) * list_length + j]

    def clear(n, _):
        out_ref[n] = -1
        return 0

    lax.fori_loop(0, sum(outward) + sum(across), clear, 0)

    @pl.when(me == 0)
    def _():
        for n in range(outward[1]):
            out_ref[e_base[1] + n] = codes["own"] * SPAN + starts[1] + n

    def named(place, r, t, source):
        hit = entry(place, r, t, 0) == source
        for j in range(1, list_length):
            hit = hit | (entry(place, r, t, j) == source)
        return hit

    def choose(sizes, ready):
        batch = jnp.int32(-1)
        for b in range(len(sizes) - 1, -1, -1):
            batch = jnp.where((room[b] < sizes[b]) & (b >= ready), b, batch)
        return batch

    def base_of(bases, batch):
        base = jnp.int32(0)
        for b, value in enumerate(bases):
            base = jnp.where(batch == b, value, base)
        return base

    def empty(sizes):
        for b in range(len(sizes)):
            room[b] = 0

    for turn in range(2):
        sender = row if turn == 0 else 1 - row
        empty(outward)
        room[0] = outward[0]
        for k, count in enumerate(chunks):
            for u in (1, 2, 3):

                def first_piece(n, _):
                    eloc[(turn * COLUMNS + 1) * steps + n] = n
                    return 0

                if u == 1 and k == 0:
                    lax.fori_loop(0, count, first_piece, 0)
                    continue

                def outer_piece(n, _, u=u, k=k):
                    t = starts[k] + n
                    source = block(mirror(u), sender)
                    need = named(0, 0, t, source)
                    for r in range(1, ROWS):
                        need = need | named(0, r, t, source)
                    batch = choose(outward, OUTWARD_READY[u][k])
                    eloc[(turn * COLUMNS + u) * steps + t] = -1

                    @pl.when(need & (batch >= 0))
                    def _():
                        slot = room[batch]
                        room[batch] = slot + 1
                        eloc[(turn * COLUMNS + u) * steps + t] = batch * SPAN + slot
                        if turn == 0:

                            @pl.when(inner)
                            def _():
                                out_ref[base_of(e_base, batch) + slot] = inner_place(codes, starts, u, k) + n

                    return 0

                lax.fori_loop(0, count, outer_piece, 0)

    for turn in range(2):
        sender = row if turn == 0 else 1 - row
        empty(across)
        for k, count in enumerate(chunks):
            for u in range(COLUMNS):

                def row_piece(n, _, u=u, k=k):
                    t = starts[k] + n
                    need = named(me, 1 - sender, t, block(mirror(u), sender))
                    if u == 0:
                        lies = jnp.int32(codes["own"] * SPAN) + t
                        when = jnp.int32(0)
                    else:
                        where = eloc[(turn * COLUMNS + u) * steps + t]
                        lies = codes["edge"][0] * SPAN + where
                        when = jnp.where(where < 0, len(across), where // SPAN + 1)
                    when = jnp.where(inner, ACROSS_READY[u][k], when)
                    lies = jnp.where(inner, inner_place(codes, starts, u, k) + n, lies)
                    batch = choose(across, when)
                    yloc[(turn * COLUMNS + u) * steps + t] = -1

                    @pl.when(need & (batch >= 0))
                    def _():
                        slot = room[batch]
                        room[batch] = slot + 1
                        yloc[(turn * COLUMNS + u) * steps + t] = batch * SPAN + slot
                        if turn == 0:
                            out_ref[base_of(y_base, batch) + slot] = lies

                    return 0

                lax.fori_loop(0, count, row_piece, 0)

    flag_ref[0] = 0
    for k, count in enumerate(chunks):

        def listed_piece(n, _, k=k):
            t = starts[k] + n // list_length
            source = entry(me, row, t, n % list_length)
            u = mirror(source // ROWS)
            same = source % ROWS == row
            e = eloc[u * steps + t]
            y = yloc[(COLUMNS + u) * steps + t]
            first = jnp.int32(0)
            for w in (0, 2, 3):
                first = jnp.where(u == w, inner_place(codes, starts, w, k), first)
            direct = jnp.where(inner, first + t - starts[k], codes["edge"][0] * SPAN + e)
            direct = jnp.where(u == me, codes["own"] * SPAN + t, direct)
            local = inner | (u == me)
            bad = jnp.where(
                same,
                jnp.logical_not(local) & ((e < 0) | (e // SPAN > OUTWARD_DUE[k])),
                (y < 0) | (y // SPAN > ACROSS_DUE[k]),
            )
            place = jnp.where(same, direct, codes["across"][0] * SPAN + y)
            in_ref[t * list_length + n % list_length] = jnp.where(bad, codes["own"] * SPAN, place)

            @pl.when(bad)
            def _():
                flag_ref[0] = 1

            return 0

        lax.fori_loop(0, count * list_length, listed_piece, 0)


def plan(lists_near, place, steps, list_length, chunks, outward, across):
    smem = pl.BlockSpec(memory_space=pltpu.SMEM)
    slots = sum(outward) + sum(across)
    return pl.pallas_call(
        functools.partial(plan_kernel, steps, list_length, chunks, outward, across),
        in_specs=[smem, smem],
        out_specs=[smem] * 3,
        out_shape=[
            jax.ShapeDtypeStruct((slots,), jnp.int32),
            jax.ShapeDtypeStruct((steps * list_length,), jnp.int32),
            jax.ShapeDtypeStruct((1,), jnp.int32),
        ],
        scratch_shapes=[
            pltpu.SMEM((2 * COLUMNS * steps,), jnp.int32),
            pltpu.SMEM((2 * COLUMNS * steps,), jnp.int32),
            pltpu.SMEM((max(len(outward), len(across)),), jnp.int32),
        ],
        name="plan",
    )(place, lists_near)


def shared(value, axes):
    count = lax.axis_size(axes)
    rows = jnp.broadcast_to(value[None], (count,) + value.shape)
    return lax.all_to_all(rows, axes, split_axis=0, concat_axis=0, tiled=True)


def column_pairs(moves):
    return [(a * ROWS + r, b * ROWS + r) for a, b in moves for r in range(ROWS)]


def relay(embedded, lists, capacity, attention, own_projection):
    steps, agents, width = embedded.shape
    list_length = lists.shape[1]
    chunks, outward, across = relay_sizes(steps, capacity)
    codes = relay_codes(outward, across)
    starts = [sum(chunks[:k]) for k in range(len(chunks))]
    e_base = [sum(outward[:b]) for b in range(len(outward))]
    y_base = [sum(outward) + sum(across[:b]) for b in range(len(across))]
    index = lax.axis_index("agent")
    place = jnp.stack([index // ROWS, index % ROWS]).astype(jnp.int32)
    send = lambda value, pairs: lax.ppermute(value, "agent", pairs)
    edges = column_pairs([(0, 1), (1, 0), (2, 3), (3, 2)])
    swap = column_pairs([(1, 2), (2, 1)])
    over = [(c * ROWS + r, c * ROWS + 1 - r) for c in range(COLUMNS) for r in range(ROWS)]
    own, edge, swapped, far, rows = (codes[n] for n in ("own", "edge", "swap", "far", "across"))
    arrays = {own: embedded}

    def pick(names):
        return {code: arrays[code] for code in names}

    def across_part(n):
        return (y_base[n], across[n], None)

    def stage(n, reads, settled, after=()):
        parts = [across_part(n)]
        if n < len(outward):
            parts.append((e_base[n], outward[n], None))
        if n == 1:
            parts.append((None, outward[1], starts[1]))
        after = tuple(arrays[rows[b]] for b in settled) + tuple(after)
        packed = pack(out_table, pick([own] + reads), parts, after)
        if n < len(outward):
            arrays[edge[n]] = send(packed[1], edges)
        arrays[rows[n]] = send(packed[0], over)
        return packed

    mine = lists.reshape(-1)
    beside = send(mine, over)
    pair = jnp.stack([jnp.where(index % ROWS == r, mine, beside) for r in range(ROWS)])
    inward = column_pairs([(0, 1), (COLUMNS - 1, COLUMNS - 2)])
    outer_pair = send(pair, inward)
    column = index // ROWS
    outer = (column == 0) | (column == COLUMNS - 1)
    near = jnp.concatenate([jnp.where(outer, pair, outer_pair), pair], axis=0).reshape(-1)
    begin = jnp.minimum(near[0], 0)
    first = lax.dynamic_slice_in_dim(embedded, begin, chunks[0], 0)
    arrays[edge[0]] = send(first, edges)
    arrays[swapped[0]] = send(first, swap)
    out_table, in_table, flag = plan(
        near, place, steps, list_length, chunks, outward, across
    )
    (token,) = pack(out_table, pick([own]), [across_part(0)])
    arrays[rows[0]] = send(token, over)
    arrays[far[0]] = send(arrays[edge[0]], swap)
    reads = edge[:1] + swapped[:1]
    packed = stage(1, reads, (0,), (token,))
    arrays[swapped[1]] = send(packed[2], swap)
    for k in (1, 2):
        at = starts[k] - starts[1]
        arrays[far[k]] = send(arrays[edge[1]][at : at + chunks[k]], swap)
    reads = reads + edge[1:2] + far[:1]
    projected = own_projection(packed[:1])
    packed = stage(2, reads, (1,), (projected,))
    reads = reads + edge[2:3] + swapped[1:] + far[1:2]
    packed = stage(3, reads, (2,), packed[:1])
    reads = reads + edge[3:4] + far[2:3]
    packed = stage(4, reads, (3,), packed[:1])

    def attend_chunk(k, after):
        return attention(
            starts[k], chunks[k], due(arrays, codes, starts, k), in_table, projected, after
        )

    done = [attend_chunk(0, packed[:1])]
    reads = reads + edge[4:5]
    packed = stage(5, reads, (4,), (done[0][0],))
    done.append(attend_chunk(1, packed[:1]))
    sample = done[1][0][0, 0, :1]
    flag = jnp.maximum(flag, (sample != sample).astype(jnp.int32))
    crowded = jnp.max(shared(flag, ("groups", "agent", "tm")))
    done.append(attend_chunk(2, (done[1][0], crowded.reshape(1))))
    return done, crowded


def due(arrays, codes, starts, k):
    wanted = {codes["own"], *codes["edge"][: OUTWARD_DUE[k] + 1]}
    wanted |= {inner_place(codes, starts, u, k) // SPAN for u in (0, 2, 3)}
    wanted |= set(codes["across"][: ACROSS_DUE[k] + 1])
    return {code: arrays[code] for code in sorted(wanted)}


def body(
    embedded,
    block_lists,
    done_flags,
    rewards,
    bootstrap,
    agent_proj,
    agent_merge,
    time_proj,
    time_merge,
    value_weight,
):
    steps, agents, width = embedded.shape
    list_length = block_lists.shape[2]
    blocks = lax.axis_size("agent")
    lists = block_lists[0]
    capacity = max(2, (2 * steps * list_length + blocks - 1) // blocks)
    spans = lax.axis_size("tm")
    index = lax.axis_index("tm")
    offset = (index * steps).astype(jnp.int32).reshape(1)
    boot = bootstrap.reshape(1, agents)
    forward = [(i, i + 1) for i in range(spans - 1)]
    backward = [(i + 1, i) for i in range(spans - 1)]

    def own_projection(after=()):
        return own_stage(embedded, agent_proj, after)

    def attention(first, count, arrays, table, projected, after=()):
        residual, normed = agent_stage(
            embedded,
            projected,
            arrays,
            table,
            first,
            count,
            list_length,
            agent_proj,
            agent_merge,
            after,
        )
        return residual, lax.ppermute(normed, "tm", forward)

    def finish(done):
        residuals, rims = [part[0] for part in done], [part[1] for part in done]
        values, edge = time_stage(
            residuals,
            rims,
            offset,
            time_proj,
            time_merge,
            value_weight.reshape(1, width),
            done_flags,
            rewards,
            boot,
        )
        last = (index == spans - 1).astype(jnp.int32).reshape(1)
        for _ in range(max(1, spans - 1)):
            arriving = lax.ppermute(edge, "tm", backward)
            advantages, edge = advantage_stage(last, values, rewards, done_flags, boot, arriving)
        return values, advantages

    def padded():
        pool, where = exchange_slots(embedded, lists, capacity)
        return finish([attention(0, steps, {1: pool}, where + SPAN, own_projection())])

    if blocks != COLUMNS * ROWS or steps % 4:
        return padded()
    done, crowded = relay(embedded, lists, capacity, attention, own_projection)
    found = finish(done)
    return lax.cond(crowded > 0, padded, lambda: found)


def solution(mesh):
    placed = (
        P(("groups", "tm"), "agent", None),
        P(("groups", "agent"), "tm", None),
        P(("groups", "tm"), "agent"),
        P(("groups", "tm"), "agent"),
        P(("groups", "agent")),
        P(),
        P(),
        P(),
        P(),
        P(),
    )
    return jax.shard_map(
        body,
        mesh=mesh,
        in_specs=placed,
        out_specs=(P(("groups", "tm"), "agent"), P(("groups", "tm"), "agent")),
        check_vma=False,
    )
```

```python
import functools
import math

import jax
import jax.numpy as jnp
from jax import lax
from jax.experimental import pallas as pl
from jax.experimental.pallas import tpu as pltpu
from jax.sharding import PartitionSpec as P

HEADS = 8
WINDOW = 16
discount = 0.9997
trace_decay = 0.995
epsilon = 1e-06
bf16 = jnp.bfloat16
f32 = jnp.float32
MIB = 1024 * 1024
SPAN = 1024
COLUMNS = 4
ROWS = 2


def rms(values):
    return values * lax.rsqrt(jnp.mean(values * values, axis=-1, keepdims=True) + epsilon)


def dot(a, b):
    return jnp.dot(a, b, preferred_element_type=f32)


def dot_t(a, b):
    return lax.dot_general(a, b, (((1,), (1,)), ((), ())), preferred_element_type=f32)


def attend(queries, keys, values, head_size, bias):
    rows, width = queries.shape
    scale = head_size ** (-0.5) * math.log2(math.e)
    pair = 2 * head_size
    lane = lax.broadcasted_iota(jnp.int32, (rows, pair), 1)
    first = lane < head_size
    ones = jnp.ones((keys.shape[0], pair), bf16)
    mixed = []
    for at in range(0, width, pair):
        both = queries[:, at : at + pair]
        none = jnp.zeros_like(both)
        stacked = jnp.concatenate(
            [jnp.where(first, both, none), jnp.where(first, none, both)], axis=0
        )
        scores = dot_t(stacked, keys[:, at : at + pair])
        if bias is not None:
            scores = scores + bias
        weights = jnp.exp2((scores - jnp.max(scores, axis=-1, keepdims=True)) * scale).astype(bf16)
        summed = dot(weights, jnp.concatenate([values[:, at : at + pair], ones], axis=1))
        result = summed[:, :pair] / summed[:, pair:]
        mixed.append(jnp.where(first, result[:rows], result[rows:]).astype(bf16))
    return jnp.concatenate(mixed, axis=1)


def fetch(entry, arrays, target, sem):
    for code, ref in arrays.items():

        @pl.when(entry // SPAN == code)
        def _(ref=ref):
            pltpu.make_async_copy(ref.at[entry % SPAN], target, sem).start()


def own_kernel(idle, own_ref, proj_ref, *refs):
    projected_ref = refs[idle]
    together, agents, width = own_ref.shape
    mine = rms(own_ref[...].astype(f32).reshape(together * agents, width)).astype(bf16)
    projected = dot(mine, proj_ref[...]).astype(bf16)
    projected_ref[...] = projected.reshape(together, agents, proj_ref.shape[1])


def own_stage(embedded, proj, after=()):
    steps, agents, width = embedded.shape
    together = math.gcd(steps, 4)
    return pl.pallas_call(
        functools.partial(own_kernel, len(after)),
        grid=(steps // together,),
        in_specs=[
            pl.BlockSpec((together, agents, width), lambda i: (i, 0, 0)),
            pl.BlockSpec(proj.shape, lambda i: (0, 0)),
        ]
        + [pl.BlockSpec(memory_space=pltpu.HBM)] * len(after),
        out_specs=pl.BlockSpec((together, agents, proj.shape[1]), lambda i: (i, 0, 0)),
        out_shape=jax.ShapeDtypeStruct((steps, agents, proj.shape[1]), bf16),
        compiler_params=pltpu.CompilerParams(vmem_limit_bytes=20 * MIB),
        name="own_stage",
    )(embedded, proj, *after)


def agent_kernel(
    list_length, first_step, codes, idle, head_size, table_ref, own_ref, projected_ref, *refs
):
    arrays = dict(zip(codes, refs))
    proj_ref, merge_ref, residual_ref, normed_ref, held_ref, sems = refs[len(codes) + idle :]
    together, agents, width = own_ref.shape
    turn = pl.program_id(0)
    pieces = [(s, j) for s in range(together) for j in range(list_length)]

    def begin(turn):
        slot = turn % 2
        for n, (s, j) in enumerate(pieces):
            entry = table_ref[(first_step + turn * together + s) * list_length + j]
            fetch(entry, arrays, held_ref.at[slot, n], sems.at[slot, n])

    @pl.when(turn == 0)
    def _():
        begin(turn)

    @pl.when(turn + 1 < pl.num_programs(0))
    def _():
        begin(turn + 1)

    slot = turn % 2
    for n in range(len(pieces)):
        pltpu.make_async_copy(refs[0].at[0], held_ref.at[slot, n], sems.at[slot, n]).wait()
    own = own_ref[...].astype(f32).reshape(together * agents, width)
    listed = held_ref[slot].astype(f32).reshape(len(pieces) * agents, width)
    theirs = rms(listed).astype(bf16)
    projected = projected_ref[...].reshape(together * agents, 3 * width)
    queries, near = projected[:, :width], projected[:, width:]
    away = dot(theirs, proj_ref[:, width:]).astype(bf16)
    mixed = []
    for s in range(together):
        here = slice(s * agents, (s + 1) * agents)
        there = slice(s * list_length * agents, (s + 1) * list_length * agents)
        keyvals = jnp.concatenate([near[here], away[there]], axis=0)
        mixed.append(
            attend(queries[here], keyvals[:, :width], keyvals[:, width:], head_size, None)
        )
    residual = own + dot(jnp.concatenate(mixed, axis=0), merge_ref[...])
    residual_ref[...] = residual.reshape(together, agents, width)
    normed_ref[...] = rms(residual).astype(bf16).reshape(together, agents, width)


def agent_stage(
    embedded, projected, arrays, table, first_step, steps, list_length, proj, merge, after=()
):
    _, agents, width = embedded.shape
    together = math.gcd(steps, math.gcd(first_step, 2))
    piece = (together, agents, width)
    whole = lambda i, w: (0, 0)
    flops = 2 * steps * agents * width * width * (4 + 2 * list_length + 2 * (1 + list_length))
    return pl.pallas_call(
        functools.partial(
            agent_kernel, list_length, first_step, tuple(arrays), len(after), width // HEADS
        ),
        grid_spec=pltpu.PrefetchScalarGridSpec(
            num_scalar_prefetch=1,
            grid=(steps // together,),
            in_specs=[
                pl.BlockSpec((together, agents, cols), lambda i, w: (first_step // together + i, 0, 0))
                for cols in (width, 3 * width)
            ]
            + [pl.BlockSpec(memory_space=pltpu.HBM)] * (len(arrays) + len(after))
            + [pl.BlockSpec(proj.shape, whole), pl.BlockSpec(merge.shape, whole)],
            out_specs=[pl.BlockSpec(piece, lambda i, w: (i, 0, 0))] * 2,
            scratch_shapes=[
                pltpu.VMEM((2, together * list_length, agents, width), bf16),
                pltpu.SemaphoreType.DMA((2, together * list_length)),
            ],
        ),
        out_shape=[
            jax.ShapeDtypeStruct((steps, agents, width), f32),
            jax.ShapeDtypeStruct((steps, agents, width), bf16),
        ],
        compiler_params=pltpu.CompilerParams(vmem_limit_bytes=24 * MIB),
        cost_estimate=pl.CostEstimate(
            flops=5 * flops, bytes_accessed=steps * agents * width * 12, transcendentals=0
        ),
        name="agent_stage",
    )(table, embedded, projected, *arrays.values(), *after, proj, merge)


def pack_kernel(codes, parts, idle, flagged, table_ref, *refs):
    arrays = dict(zip(codes, refs))
    outs, (held_ref, in_sems, out_sems) = refs[len(codes) + idle : -3], refs[-3:]
    if flagged:
        outs[-1][...] = jnp.full(outs[-1].shape, outs[0][0], jnp.int32)
        outs = outs[1:-1]
    slots = []
    for out, (offset, count, first) in zip(outs, parts):
        slots += [(offset, first, n, out.at[n]) for n in range(count)]

    def guarded(offset, n, action):
        if offset is None:
            action()
        else:
            pl.when(table_ref[offset + n] >= 0)(action)

    for at, (offset, first, n, _) in enumerate(slots):
        if offset is None:
            own = arrays[0].at[first + n]
            pltpu.make_async_copy(own, held_ref.at[at], in_sems.at[at]).start()
        else:
            fetch(table_ref[offset + n], arrays, held_ref.at[at], in_sems.at[at])
    for at, (offset, first, n, target) in enumerate(slots):

        def pass_on(at=at, target=target):
            pltpu.make_async_copy(refs[0].at[0], held_ref.at[at], in_sems.at[at]).wait()
            pltpu.make_async_copy(held_ref.at[at], target, out_sems.at[at]).start()

        guarded(offset, n, pass_on)
    for at, (offset, first, n, target) in enumerate(slots):

        def finish(at=at, target=target):
            pltpu.make_async_copy(held_ref.at[at], target, out_sems.at[at]).wait()

        guarded(offset, n, finish)


def pack(table, arrays, parts, after=(), flag=None):
    piece = next(iter(arrays.values())).shape[1:]
    slots = sum(count for _, count, _ in parts)
    smem = pl.BlockSpec(memory_space=pltpu.SMEM)
    hbm = pl.BlockSpec(memory_space=pltpu.HBM)
    flags = () if flag is None else (flag,)
    out_specs = [hbm] * len(parts)
    out_shape = [jax.ShapeDtypeStruct((count,) + piece, bf16) for _, count, _ in parts]
    if flags:
        out_specs.append(pl.BlockSpec(memory_space=pltpu.VMEM))
        out_shape.append(jax.ShapeDtypeStruct((8, 128), jnp.int32))
    return pl.pallas_call(
        functools.partial(pack_kernel, tuple(arrays), tuple(parts), len(after), len(flags)),
        in_specs=[smem] + [hbm] * (len(arrays) + len(after)) + [smem] * len(flags),
        out_specs=out_specs,
        out_shape=out_shape,
        scratch_shapes=[
            pltpu.VMEM((slots,) + piece, bf16),
            pltpu.SemaphoreType.DMA((slots,)),
            pltpu.SemaphoreType.DMA((slots,)),
        ],
        cost_estimate=pl.CostEstimate(
            flops=0, bytes_accessed=piece[0] * piece[1], transcendentals=0
        ),
        compiler_params=pltpu.CompilerParams(
            vmem_limit_bytes=slots * piece[0] * piece[1] * 2 + 2 * MIB
        ),
        name="pack",
    )(table, *arrays.values(), *after, *flags)


def suffix(values, rewards, done, next_value, next_advantage):
    steps = values.shape[0]
    living = 1.0 - done.astype(f32)
    running, following, rows = next_advantage, next_value, [None] * steps
    for step in range(steps - 1, -1, -1):
        alive = living[step : step + 1]
        value = values[step : step + 1]
        change = rewards[step : step + 1] + discount * alive * following - value
        running = change + discount * trace_decay * alive * running
        rows[step] = running
        following = value
    return rows


def time_kernel(parts, steps, tile, head_size, offset_ref, *refs):
    refs = list(refs)
    residual_refs = [refs.pop(0) for _ in range(parts)]
    rim_refs = [refs.pop(0) for _ in range(parts)]
    proj_ref, merge_ref, weight_ref, done_ref, rewards_ref, boot_ref = refs[:6]
    values_ref, edge_ref, bias_ref = refs[6:]
    width = proj_ref.shape[0]
    turn = pl.program_id(0)
    group = 8
    rows = steps * group
    agents = values_ref.shape[1]

    @pl.when(turn == 0)
    def _():
        r = lax.broadcasted_iota(jnp.int32, (2 * rows, 2 * rows), 0) % rows
        c = lax.broadcasted_iota(jnp.int32, (2 * rows, 2 * rows), 1)
        query_step = r // group
        key_step = c // group - steps
        allowed = (
            (r % group == c % group)
            & (key_step <= query_step)
            & (key_step > query_step - WINDOW)
            & (key_step + offset_ref[0] >= 0)
        )
        bias_ref[...] = jnp.where(allowed, 0.0, -1e30)
        values_ref[...] = jnp.zeros_like(values_ref)

    def pieces(part_refs):
        whole = jnp.concatenate([ref[...].astype(f32) for ref in part_refs], axis=0)
        return [
            whole[:, at : at + group].reshape(rows, width) for at in range(0, tile, group)
        ]

    residuals = pieces(residual_refs)
    current = jnp.concatenate([rms(r).astype(bf16) for r in residuals], axis=0)
    behind = jnp.concatenate([r.astype(bf16) for r in pieces(rim_refs)], axis=0)
    projected = dot(current, proj_ref[...]).astype(bf16)
    before = dot(behind, proj_ref[:, width:]).astype(bf16)
    bias = bias_ref[...]
    mixed = []
    for at in range(0, tile * steps, rows):
        mine, past = projected[at : at + rows], before[at : at + rows]
        keys = jnp.concatenate([past[:, :width], mine[:, width : 2 * width]], axis=0)
        held = jnp.concatenate([past[:, width:], mine[:, 2 * width :]], axis=0)
        mixed.append(attend(mine[:, :width], keys, held, head_size, bias))
    merged = dot(jnp.concatenate(mixed, axis=0), merge_ref[...])
    lane = lax.broadcasted_iota(jnp.int32, (steps, group, agents), 2)
    place = lax.broadcasted_iota(jnp.int32, (steps, group, agents), 1)
    total = values_ref[...]
    for n, residual in enumerate(residuals):
        final = rms(residual + merged[n * rows : (n + 1) * rows])
        value = jnp.sum(final * weight_ref[...], axis=-1, keepdims=True)
        spot = lane == place + (turn * tile + n * group)
        total = total + jnp.sum(
            jnp.where(spot, value.reshape(steps, group, 1), 0.0), axis=1
        )
    values_ref[...] = total

    @pl.when(turn == pl.num_programs(0) - 1)
    def _():
        found = values_ref[...]
        boot = boot_ref[...]
        advantages = suffix(found, rewards_ref[...], done_ref[...], boot, jnp.zeros_like(boot))
        edge_ref[...] = jnp.concatenate([found[:1], advantages[0]], axis=0)


def time_stage(residuals, rims, offset, proj, merge, weight, done, rewards, boot):
    part_steps = [r.shape[0] for r in residuals]
    steps = sum(part_steps)
    _, agents, width = residuals[0].shape
    tile = math.gcd(agents, 32)
    whole = lambda i, o: (0, 0)

    def blocks(arrays):
        return [
            pl.BlockSpec((array.shape[0], tile, width), lambda i, o: (0, i, 0))
            for array in arrays
        ]

    rows = 16 * steps
    fixed = [proj, merge, weight, done, rewards, boot]
    return pl.pallas_call(
        functools.partial(time_kernel, len(residuals), steps, tile, width // HEADS),
        grid_spec=pltpu.PrefetchScalarGridSpec(
            num_scalar_prefetch=1,
            grid=(agents // tile,),
            in_specs=blocks(residuals)
            + blocks(rims)
            + [pl.BlockSpec(array.shape, whole) for array in fixed],
            out_specs=[
                pl.BlockSpec((steps, agents), whole),
                pl.BlockSpec((2, agents), whole),
            ],
            scratch_shapes=[pltpu.VMEM((rows, rows), f32)],
        ),
        out_shape=[
            jax.ShapeDtypeStruct((steps, agents), f32),
            jax.ShapeDtypeStruct((2, agents), f32),
        ],
        compiler_params=pltpu.CompilerParams(vmem_limit_bytes=28 * MIB),
        cost_estimate=pl.CostEstimate(flops=0, bytes_accessed=rows, transcendentals=0),
        name="time_stage",
    )(offset, *residuals, *rims, *fixed)


def advantage_kernel(last_ref, values_ref, rewards_ref, done_ref, boot_ref, edge_ref, out_ref, mine_ref):
    last = last_ref[0] > 0
    arriving = edge_ref[...]
    boot = boot_ref[...]
    found = values_ref[...]
    next_value = jnp.where(last, boot, arriving[:1])
    next_advantage = jnp.where(last, 0.0, arriving[1:2])
    rows = suffix(found, rewards_ref[...], done_ref[...], next_value, next_advantage)
    out_ref[...] = jnp.concatenate(rows, axis=0)
    mine_ref[...] = jnp.concatenate([found[:1], rows[0]], axis=0)


def advantage_stage(last, values, rewards, done, boot, edge):
    return pl.pallas_call(
        advantage_kernel,
        in_specs=[pl.BlockSpec(memory_space=pltpu.SMEM)]
        + [pl.BlockSpec(memory_space=pltpu.VMEM)] * 5,
        out_specs=[pl.BlockSpec(memory_space=pltpu.VMEM)] * 2,
        out_shape=[
            jax.ShapeDtypeStruct(values.shape, f32),
            jax.ShapeDtypeStruct(edge.shape, f32),
        ],
        name="advantage_stage",
    )(last, values, rewards, done, boot, edge)


def exchange_slots(embedded, lists, capacity):
    steps, agents, width = embedded.shape
    blocks = lax.axis_size("agent")
    list_length = lists.shape[1]
    named = lists.reshape(-1)
    row_steps = jnp.arange(named.shape[0], dtype=jnp.int32) // list_length
    hits = (named[:, None] == jnp.arange(blocks, dtype=jnp.int32)[None, :]).astype(jnp.int32)
    slot = jnp.sum((jnp.cumsum(hits, axis=0) - hits) * hits, axis=1)
    slot_hits = (slot[:, None] == jnp.arange(capacity, dtype=jnp.int32)[None, :]).astype(jnp.int32)
    requests = jnp.sum(
        (hits * row_steps[:, None])[:, :, None] * slot_hits[:, None, :], axis=0
    )
    wanted = lax.all_to_all(requests, "agent", split_axis=0, concat_axis=0, tiled=True)
    outgoing = embedded[wanted.reshape(-1)].reshape(blocks, capacity, agents, width)
    arrived = lax.all_to_all(outgoing, "agent", split_axis=0, concat_axis=0, tiled=True)
    return arrived.reshape(blocks * capacity, agents, width), named * capacity + slot


OUTWARD_READY = {1: (0, 1, 1), 2: (1, 3, 3), 3: (2, 3, 4)}
ACROSS_READY = {0: (1, 2, 2), 1: (0, 0, 0), 2: (1, 3, 3), 3: (2, 3, 4)}
OUTWARD_DUE = (3, 4, 4)
ACROSS_DUE = (3, 4, 5)


def relay_sizes(steps, capacity):
    half, quarter = steps // 2, steps // 4
    chunks = [half, quarter, quarter]
    outward = [half, half, half, half, quarter + 2]
    across = [quarter, half, half, half - 1, quarter + 2, quarter + 2]
    return chunks, outward, across


def relay_codes(outward, across):
    names = {}
    code = 1
    for name, count in (("edge", len(outward)), ("swap", 2), ("far", 3), ("across", len(across))):
        names[name] = [code + n for n in range(count)]
        code += count
    names["own"] = 0
    return names


def inner_place(codes, starts, u, k):
    behind = starts[k] - starts[min(k, 1)]
    if u == 0:
        return codes["edge"][min(k, 1)] * SPAN + behind
    if u == 1:
        return codes["own"] * SPAN + starts[k]
    if u == 2:
        return codes["swap"][min(k, 1)] * SPAN + behind
    return codes["far"][k] * SPAN


def plan_kernel(steps, list_length, chunks, outward, across, place_ref, lists_ref, out_ref, in_ref, flag_ref, eloc, yloc, room):
    codes = relay_codes(outward, across)
    column, row = place_ref[0], place_ref[1]
    far_side = column >= COLUMNS // 2
    mirror = lambda u: jnp.where(far_side, COLUMNS - 1 - u, u)
    me = mirror(column)
    inner = me == 1
    starts = [sum(chunks[:k]) for k in range(len(chunks))]
    e_base = [sum(outward[:b]) for b in range(len(outward))]
    y_base = [sum(outward) + sum(across[:b]) for b in range(len(across))]
    block = lambda c, r: c * ROWS + r
    entry = lambda c, r, t, j: lists_ref[((c * ROWS + r) * steps + t) * list_length + j]

    def clear(n, _):
        out_ref[n] = -1
        return 0

    lax.fori_loop(0, sum(outward) + sum(across), clear, 0)

    @pl.when(me == 0)
    def _():
        for n in range(outward[1]):
            out_ref[e_base[1] + n] = codes["own"] * SPAN + starts[1] + n

    def named(place, r, t, source):
        hit = entry(place, r, t, 0) == source
        for j in range(1, list_length):
            hit = hit | (entry(place, r, t, j) == source)
        return hit

    def choose(sizes, ready):
        batch = jnp.int32(-1)
        for b in range(len(sizes) - 1, -1, -1):
            batch = jnp.where((room[b] < sizes[b]) & (b >= ready), b, batch)
        return batch

    def base_of(bases, batch):
        base = jnp.int32(0)
        for b, value in enumerate(bases):
            base = jnp.where(batch == b, value, base)
        return base

    def empty(sizes):
        for b in range(len(sizes)):
            room[b] = 0

    for turn in range(2):
        sender = row if turn == 0 else 1 - row
        empty(outward)
        room[0] = outward[0]
        for k, count in enumerate(chunks):
            for u in (1, 2, 3):

                def first_piece(n, _):
                    eloc[(turn * COLUMNS + 1) * steps + n] = n
                    return 0

                if u == 1 and k == 0:
                    lax.fori_loop(0, count, first_piece, 0)
                    continue

                def outer_piece(n, _, u=u, k=k):
                    t = starts[k] + n
                    source = block(mirror(u), sender)
                    need = named(0, 0, t, source)
                    for r in range(1, ROWS):
                        need = need | named(0, r, t, source)
                    batch = choose(outward, OUTWARD_READY[u][k])
                    eloc[(turn * COLUMNS + u) * steps + t] = -1

                    @pl.when(need & (batch >= 0))
                    def _():
                        slot = room[batch]
                        room[batch] = slot + 1
                        eloc[(turn * COLUMNS + u) * steps + t] = batch * SPAN + slot
                        if turn == 0:

                            @pl.when(inner)
                            def _():
                                out_ref[base_of(e_base, batch) + slot] = inner_place(codes, starts, u, k) + n

                    return 0

                lax.fori_loop(0, count, outer_piece, 0)

    for turn in range(2):
        sender = row if turn == 0 else 1 - row
        empty(across)
        for k, count in enumerate(chunks):
            for u in range(COLUMNS):

                def row_piece(n, _, u=u, k=k):
                    t = starts[k] + n
                    need = named(me, 1 - sender, t, block(mirror(u), sender))
                    if u == 0:
                        lies = jnp.int32(codes["own"] * SPAN) + t
                        when = jnp.int32(0)
                    else:
                        where = eloc[(turn * COLUMNS + u) * steps + t]
                        lies = codes["edge"][0] * SPAN + where
                        when = jnp.where(where < 0, len(across), where // SPAN + 1)
                    when = jnp.where(inner, ACROSS_READY[u][k], when)
                    lies = jnp.where(inner, inner_place(codes, starts, u, k) + n, lies)
                    batch = choose(across, when)
                    yloc[(turn * COLUMNS + u) * steps + t] = -1

                    @pl.when(need & (batch >= 0))
                    def _():
                        slot = room[batch]
                        room[batch] = slot + 1
                        yloc[(turn * COLUMNS + u) * steps + t] = batch * SPAN + slot
                        if turn == 0:
                            out_ref[base_of(y_base, batch) + slot] = lies

                    return 0

                lax.fori_loop(0, count, row_piece, 0)

    flag_ref[0] = 0
    for k, count in enumerate(chunks):

        def listed_piece(n, _, k=k):
            t = starts[k] + n // list_length
            source = entry(me, row, t, n % list_length)
            u = mirror(source // ROWS)
            same = source % ROWS == row
            e = eloc[u * steps + t]
            y = yloc[(COLUMNS + u) * steps + t]
            first = jnp.int32(0)
            for w in (0, 2, 3):
                first = jnp.where(u == w, inner_place(codes, starts, w, k), first)
            direct = jnp.where(inner, first + t - starts[k], codes["edge"][0] * SPAN + e)
            direct = jnp.where(u == me, codes["own"] * SPAN + t, direct)
            local = inner | (u == me)
            bad = jnp.where(
                same,
                jnp.logical_not(local) & ((e < 0) | (e // SPAN > OUTWARD_DUE[k])),
                (y < 0) | (y // SPAN > ACROSS_DUE[k]),
            )
            place = jnp.where(same, direct, codes["across"][0] * SPAN + y)
            in_ref[t * list_length + n % list_length] = jnp.where(bad, codes["own"] * SPAN, place)

            @pl.when(bad)
            def _():
                flag_ref[0] = 1

            return 0

        lax.fori_loop(0, count * list_length, listed_piece, 0)


def plan(lists_near, place, steps, list_length, chunks, outward, across):
    smem = pl.BlockSpec(memory_space=pltpu.SMEM)
    slots = sum(outward) + sum(across)
    return pl.pallas_call(
        functools.partial(plan_kernel, steps, list_length, chunks, outward, across),
        in_specs=[smem, smem],
        out_specs=[smem] * 3,
        out_shape=[
            jax.ShapeDtypeStruct((slots,), jnp.int32),
            jax.ShapeDtypeStruct((steps * list_length,), jnp.int32),
            jax.ShapeDtypeStruct((1,), jnp.int32),
        ],
        scratch_shapes=[
            pltpu.SMEM((2 * COLUMNS * steps,), jnp.int32),
            pltpu.SMEM((2 * COLUMNS * steps,), jnp.int32),
            pltpu.SMEM((max(len(outward), len(across)),), jnp.int32),
        ],
        name="plan",
    )(place, lists_near)


def shared(value, axes):
    count = lax.axis_size(axes)
    rows = jnp.broadcast_to(value[None], (count,) + value.shape)
    return lax.all_to_all(rows, axes, split_axis=0, concat_axis=0, tiled=True)


def column_pairs(moves):
    return [(a * ROWS + r, b * ROWS + r) for a, b in moves for r in range(ROWS)]


def relay(embedded, lists, capacity, attention, own_projection):
    steps, agents, width = embedded.shape
    list_length = lists.shape[1]
    chunks, outward, across = relay_sizes(steps, capacity)
    codes = relay_codes(outward, across)
    starts = [sum(chunks[:k]) for k in range(len(chunks))]
    e_base = [sum(outward[:b]) for b in range(len(outward))]
    y_base = [sum(outward) + sum(across[:b]) for b in range(len(across))]
    index = lax.axis_index("agent")
    place = jnp.stack([index // ROWS, index % ROWS]).astype(jnp.int32)
    send = lambda value, pairs: lax.ppermute(value, "agent", pairs)
    edges = column_pairs([(0, 1), (1, 0), (2, 3), (3, 2)])
    swap = column_pairs([(1, 2), (2, 1)])
    over = [(c * ROWS + r, c * ROWS + 1 - r) for c in range(COLUMNS) for r in range(ROWS)]
    own, edge, swapped, far, rows = (codes[n] for n in ("own", "edge", "swap", "far", "across"))
    arrays = {own: embedded}

    def pick(names):
        return {code: arrays[code] for code in names}

    def across_part(n):
        return (y_base[n], across[n], None)

    def stage(n, reads, settled, after=(), flag=None):
        parts = [across_part(n)]
        if n < len(outward):
            parts.append((e_base[n], outward[n], None))
        if n == 1:
            parts.append((None, outward[1], starts[1]))
        after = tuple(arrays[rows[b]] for b in settled) + tuple(after)
        packed = pack(out_table, pick([own] + reads), parts, after, flag)
        if n < len(outward):
            arrays[edge[n]] = send(packed[1], edges)
        arrays[rows[n]] = send(packed[0], over)
        return packed

    mine = lists.reshape(-1)
    beside = send(mine, over)
    pair = jnp.stack([jnp.where(index % ROWS == r, mine, beside) for r in range(ROWS)])
    inward = column_pairs([(0, 1), (COLUMNS - 1, COLUMNS - 2)])
    outer_pair = send(pair, inward)
    column = index // ROWS
    outer = (column == 0) | (column == COLUMNS - 1)
    near = jnp.concatenate([jnp.where(outer, pair, outer_pair), pair], axis=0).reshape(-1)
    begin = jnp.minimum(near[0], 0)
    first = lax.dynamic_slice_in_dim(embedded, begin, chunks[0], 0)
    arrays[edge[0]] = send(first, edges)
    arrays[swapped[0]] = send(first, swap)
    out_table, in_table, flag = plan(
        near, place, steps, list_length, chunks, outward, across
    )
    (token,) = pack(out_table, pick([own]), [across_part(0)])
    arrays[rows[0]] = send(token, over)
    arrays[far[0]] = send(arrays[edge[0]], swap)
    reads = edge[:1] + swapped[:1]
    packed = stage(1, reads, (0,), (token,))
    arrays[swapped[1]] = send(packed[2], swap)
    for k in (1, 2):
        at = starts[k] - starts[1]
        arrays[far[k]] = send(arrays[edge[1]][at : at + chunks[k]], swap)
    reads = reads + edge[1:2] + far[:1]
    projected = own_projection(packed[:1])
    packed = stage(2, reads, (1,), (projected,))
    reads = reads + edge[2:3] + swapped[1:] + far[1:2]
    packed = stage(3, reads, (2,), packed[:1])
    reads = reads + edge[3:4] + far[2:3]
    packed = stage(4, reads, (3,), packed[:1])

    def attend_chunk(k, after):
        return attention(
            starts[k], chunks[k], due(arrays, codes, starts, k), in_table, projected, after
        )

    done = [attend_chunk(0, packed[:1])]
    reads = reads + edge[4:5]
    packed = stage(5, reads, (4,), (done[0][0],), flag)
    done.append(attend_chunk(1, packed[:1]))
    crowded = jnp.max(lax.all_gather(packed[-1], ("groups", "agent", "tm")))
    done.append(attend_chunk(2, (done[1][0],)))
    return done, crowded


def due(arrays, codes, starts, k):
    wanted = {codes["own"], *codes["edge"][: OUTWARD_DUE[k] + 1]}
    wanted |= {inner_place(codes, starts, u, k) // SPAN for u in (0, 2, 3)}
    wanted |= set(codes["across"][: ACROSS_DUE[k] + 1])
    return {code: arrays[code] for code in sorted(wanted)}


def body(
    embedded,
    block_lists,
    done_flags,
    rewards,
    bootstrap,
    agent_proj,
    agent_merge,
    time_proj,
    time_merge,
    value_weight,
):
    steps, agents, width = embedded.shape
    list_length = block_lists.shape[2]
    blocks = lax.axis_size("agent")
    lists = block_lists[0]
    capacity = max(2, (2 * steps * list_length + blocks - 1) // blocks)
    spans = lax.axis_size("tm")
    index = lax.axis_index("tm")
    offset = (index * steps).astype(jnp.int32).reshape(1)
    boot = bootstrap.reshape(1, agents)
    forward = [(i, i + 1) for i in range(spans - 1)]
    backward = [(i + 1, i) for i in range(spans - 1)]

    def own_projection(after=()):
        return own_stage(embedded, agent_proj, after)

    def attention(first, count, arrays, table, projected, after=()):
        residual, normed = agent_stage(
            embedded,
            projected,
            arrays,
            table,
            first,
            count,
            list_length,
            agent_proj,
            agent_merge,
            after,
        )
        return residual, lax.ppermute(normed, "tm", forward)

    def finish(done):
        residuals, rims = [part[0] for part in done], [part[1] for part in done]
        values, edge = time_stage(
            residuals,
            rims,
            offset,
            time_proj,
            time_merge,
            value_weight.reshape(1, width),
            done_flags,
            rewards,
            boot,
        )
        last = (index == spans - 1).astype(jnp.int32).reshape(1)
        for _ in range(max(1, spans - 1)):
            arriving = lax.ppermute(edge, "tm", backward)
            advantages, edge = advantage_stage(last, values, rewards, done_flags, boot, arriving)
        return values, advantages

    def padded():
        pool, where = exchange_slots(embedded, lists, capacity)
        return finish([attention(0, steps, {1: pool}, where + SPAN, own_projection())])

    if blocks != COLUMNS * ROWS or steps % 4:
        return padded()
    done, crowded = relay(embedded, lists, capacity, attention, own_projection)
    found = finish(done)
    return lax.cond(crowded > 0, padded, lambda: found)


def solution(mesh):
    placed = (
        P(("groups", "tm"), "agent", None),
        P(("groups", "agent"), "tm", None),
        P(("groups", "tm"), "agent"),
        P(("groups", "tm"), "agent"),
        P(("groups", "agent")),
        P(),
        P(),
        P(),
        P(),
        P(),
    )
    return jax.shard_map(
        body,
        mesh=mesh,
        in_specs=placed,
        out_specs=(P(("groups", "tm"), "agent"), P(("groups", "tm"), "agent")),
        check_vma=False,
    )
```

```python
import functools
import math

import jax
import jax.numpy as jnp
from jax import lax
from jax.experimental import pallas as pl
from jax.experimental.pallas import tpu as pltpu
from jax.sharding import PartitionSpec as P

HEADS = 8
WINDOW = 16
discount = 0.9997
trace_decay = 0.995
epsilon = 1e-06
bf16 = jnp.bfloat16
f32 = jnp.float32
MIB = 1024 * 1024
SPAN = 1024
COLUMNS = 4
ROWS = 2


def rms(values):
    return values * lax.rsqrt(jnp.mean(values * values, axis=-1, keepdims=True) + epsilon)


def dot(a, b):
    return jnp.dot(a, b, preferred_element_type=f32)


def dot_t(a, b):
    return lax.dot_general(a, b, (((1,), (1,)), ((), ())), preferred_element_type=f32)


def attend(queries, keys, values, head_size, bias):
    rows, width = queries.shape
    scale = head_size ** (-0.5) * math.log2(math.e)
    pair = 2 * head_size
    lane = lax.broadcasted_iota(jnp.int32, (rows, pair), 1)
    first = lane < head_size
    ones = jnp.ones((keys.shape[0], pair), bf16)
    mixed = []
    for at in range(0, width, pair):
        both = queries[:, at : at + pair]
        none = jnp.zeros_like(both)
        stacked = jnp.concatenate(
            [jnp.where(first, both, none), jnp.where(first, none, both)], axis=0
        )
        scores = dot_t(stacked, keys[:, at : at + pair])
        if bias is not None:
            scores = scores + bias
        weights = jnp.exp2((scores - jnp.max(scores, axis=-1, keepdims=True)) * scale).astype(bf16)
        summed = dot(weights, jnp.concatenate([values[:, at : at + pair], ones], axis=1))
        result = summed[:, :pair] / summed[:, pair:]
        mixed.append(jnp.where(first, result[:rows], result[rows:]).astype(bf16))
    return jnp.concatenate(mixed, axis=1)


def fetch(entry, arrays, target, sem):
    for code, ref in arrays.items():

        @pl.when(entry // SPAN == code)
        def _(ref=ref):
            pltpu.make_async_copy(ref.at[entry % SPAN], target, sem).start()


def own_kernel(idle, own_ref, proj_ref, *refs):
    projected_ref = refs[idle]
    together, agents, width = own_ref.shape
    mine = rms(own_ref[...].astype(f32).reshape(together * agents, width)).astype(bf16)
    projected = dot(mine, proj_ref[...]).astype(bf16)
    projected_ref[...] = projected.reshape(together, agents, proj_ref.shape[1])


def own_stage(embedded, proj, after=()):
    steps, agents, width = embedded.shape
    together = math.gcd(steps, 4)
    return pl.pallas_call(
        functools.partial(own_kernel, len(after)),
        grid=(steps // together,),
        in_specs=[
            pl.BlockSpec((together, agents, width), lambda i: (i, 0, 0)),
            pl.BlockSpec(proj.shape, lambda i: (0, 0)),
        ]
        + [pl.BlockSpec(memory_space=pltpu.HBM)] * len(after),
        out_specs=pl.BlockSpec((together, agents, proj.shape[1]), lambda i: (i, 0, 0)),
        out_shape=jax.ShapeDtypeStruct((steps, agents, proj.shape[1]), bf16),
        compiler_params=pltpu.CompilerParams(vmem_limit_bytes=18 * MIB),
        name="own_stage",
    )(embedded, proj, *after)


def agent_kernel(
    list_length, first_step, codes, idle, head_size, table_ref, own_ref, projected_ref, *refs
):
    arrays = dict(zip(codes, refs))
    proj_ref, merge_ref, residual_ref, normed_ref, held_ref, sems = refs[len(codes) + idle :]
    together, agents, width = own_ref.shape
    turn = pl.program_id(0)
    pieces = [(s, j) for s in range(together) for j in range(list_length)]

    def begin(turn):
        slot = turn % 2
        for n, (s, j) in enumerate(pieces):
            entry = table_ref[(first_step + turn * together + s) * list_length + j]
            fetch(entry, arrays, held_ref.at[slot, n], sems.at[slot, n])

    @pl.when(turn == 0)
    def _():
        begin(turn)

    @pl.when(turn + 1 < pl.num_programs(0))
    def _():
        begin(turn + 1)

    slot = turn % 2
    for n in range(len(pieces)):
        pltpu.make_async_copy(refs[0].at[0], held_ref.at[slot, n], sems.at[slot, n]).wait()
    own = own_ref[...].astype(f32).reshape(together * agents, width)
    listed = held_ref[slot].astype(f32).reshape(len(pieces) * agents, width)
    theirs = rms(listed).astype(bf16)
    projected = projected_ref[...].reshape(together * agents, 3 * width)
    queries, near = projected[:, :width], projected[:, width:]
    away = dot(theirs, proj_ref[:, width:]).astype(bf16)
    mixed = []
    for s in range(together):
        here = slice(s * agents, (s + 1) * agents)
        there = slice(s * list_length * agents, (s + 1) * list_length * agents)
        keyvals = jnp.concatenate([near[here], away[there]], axis=0)
        mixed.append(
            attend(queries[here], keyvals[:, :width], keyvals[:, width:], head_size, None)
        )
    residual = own + dot(jnp.concatenate(mixed, axis=0), merge_ref[...])
    residual_ref[...] = residual.reshape(together, agents, width)
    normed_ref[...] = rms(residual).astype(bf16).reshape(together, agents, width)


def agent_stage(
    embedded, projected, arrays, table, first_step, steps, list_length, proj, merge, after=()
):
    _, agents, width = embedded.shape
    together = math.gcd(steps, math.gcd(first_step, 2))
    piece = (together, agents, width)
    whole = lambda i, w: (0, 0)
    flops = 2 * steps * agents * width * width * (4 + 2 * list_length + 2 * (1 + list_length))
    return pl.pallas_call(
        functools.partial(
            agent_kernel, list_length, first_step, tuple(arrays), len(after), width // HEADS
        ),
        grid_spec=pltpu.PrefetchScalarGridSpec(
            num_scalar_prefetch=1,
            grid=(steps // together,),
            in_specs=[
                pl.BlockSpec((together, agents, cols), lambda i, w: (first_step // together + i, 0, 0))
                for cols in (width, 3 * width)
            ]
            + [pl.BlockSpec(memory_space=pltpu.HBM)] * (len(arrays) + len(after))
            + [pl.BlockSpec(proj.shape, whole), pl.BlockSpec(merge.shape, whole)],
            out_specs=[pl.BlockSpec(piece, lambda i, w: (i, 0, 0))] * 2,
            scratch_shapes=[
                pltpu.VMEM((2, together * list_length, agents, width), bf16),
                pltpu.SemaphoreType.DMA((2, together * list_length)),
            ],
        ),
        out_shape=[
            jax.ShapeDtypeStruct((steps, agents, width), f32),
            jax.ShapeDtypeStruct((steps, agents, width), bf16),
        ],
        compiler_params=pltpu.CompilerParams(vmem_limit_bytes=18 * MIB),
        cost_estimate=pl.CostEstimate(
            flops=5 * flops, bytes_accessed=steps * agents * width * 12, transcendentals=0
        ),
        name="agent_stage",
    )(table, embedded, projected, *arrays.values(), *after, proj, merge)


def pack_kernel(codes, parts, idle, table_ref, *refs):
    arrays = dict(zip(codes, refs))
    outs, (held_ref, in_sems, out_sems) = refs[len(codes) + idle : -3], refs[-3:]
    slots = []
    for out, (offset, count, first) in zip(outs, parts):
        slots += [(offset, first, n, out.at[n]) for n in range(count)]

    def guarded(offset, n, action):
        if offset is None:
            action()
        else:
            pl.when(table_ref[offset + n] >= 0)(action)

    for at, (offset, first, n, _) in enumerate(slots):
        if offset is None:
            own = arrays[0].at[first + n]
            pltpu.make_async_copy(own, held_ref.at[at], in_sems.at[at]).start()
        else:
            fetch(table_ref[offset + n], arrays, held_ref.at[at], in_sems.at[at])
    for at, (offset, first, n, target) in enumerate(slots):

        def pass_on(at=at, target=target):
            pltpu.make_async_copy(refs[0].at[0], held_ref.at[at], in_sems.at[at]).wait()
            pltpu.make_async_copy(held_ref.at[at], target, out_sems.at[at]).start()

        guarded(offset, n, pass_on)
    for at, (offset, first, n, target) in enumerate(slots):

        def finish(at=at, target=target):
            pltpu.make_async_copy(held_ref.at[at], target, out_sems.at[at]).wait()

        guarded(offset, n, finish)


def pack(table, arrays, parts, after=()):
    piece = next(iter(arrays.values())).shape[1:]
    slots = sum(count for _, count, _ in parts)
    smem = pl.BlockSpec(memory_space=pltpu.SMEM)
    hbm = pl.BlockSpec(memory_space=pltpu.HBM)
    out_specs = [hbm] * len(parts)
    out_shape = [jax.ShapeDtypeStruct((count,) + piece, bf16) for _, count, _ in parts]
    return pl.pallas_call(
        functools.partial(pack_kernel, tuple(arrays), tuple(parts), len(after)),
        in_specs=[smem] + [hbm] * (len(arrays) + len(after)),
        out_specs=out_specs,
        out_shape=out_shape,
        scratch_shapes=[
            pltpu.VMEM((slots,) + piece, bf16),
            pltpu.SemaphoreType.DMA((slots,)),
            pltpu.SemaphoreType.DMA((slots,)),
        ],
        cost_estimate=pl.CostEstimate(
            flops=0, bytes_accessed=piece[0] * piece[1], transcendentals=0
        ),
        compiler_params=pltpu.CompilerParams(
            vmem_limit_bytes=slots * piece[0] * piece[1] * 2 + 2 * MIB
        ),
        name="pack",
    )(table, *arrays.values(), *after)


def suffix(values, rewards, done, next_value, next_advantage):
    steps = values.shape[0]
    living = 1.0 - done.astype(f32)
    running, following, rows = next_advantage, next_value, [None] * steps
    for step in range(steps - 1, -1, -1):
        alive = living[step : step + 1]
        value = values[step : step + 1]
        change = rewards[step : step + 1] + discount * alive * following - value
        running = change + discount * trace_decay * alive * running
        rows[step] = running
        following = value
    return rows


def time_kernel(parts, steps, tile, head_size, offset_ref, *refs):
    refs = list(refs)
    residual_refs = [refs.pop(0) for _ in range(parts)]
    rim_refs = [refs.pop(0) for _ in range(parts)]
    proj_ref, merge_ref, weight_ref, done_ref, rewards_ref, boot_ref = refs[:6]
    values_ref, edge_ref, bias_ref = refs[6:]
    width = proj_ref.shape[0]
    turn = pl.program_id(0)
    group = 8
    rows = steps * group
    agents = values_ref.shape[1]

    @pl.when(turn == 0)
    def _():
        r = lax.broadcasted_iota(jnp.int32, (2 * rows, 2 * rows), 0) % rows
        c = lax.broadcasted_iota(jnp.int32, (2 * rows, 2 * rows), 1)
        query_step = r // group
        key_step = c // group - steps
        allowed = (
            (r % group == c % group)
            & (key_step <= query_step)
            & (key_step > query_step - WINDOW)
            & (key_step + offset_ref[0] >= 0)
        )
        bias_ref[...] = jnp.where(allowed, 0.0, -1e30)
        values_ref[...] = jnp.zeros_like(values_ref)

    def pieces(part_refs):
        whole = jnp.concatenate([ref[...].astype(f32) for ref in part_refs], axis=0)
        return [
            whole[:, at : at + group].reshape(rows, width) for at in range(0, tile, group)
        ]

    residuals = pieces(residual_refs)
    current = jnp.concatenate([rms(r).astype(bf16) for r in residuals], axis=0)
    behind = jnp.concatenate([r.astype(bf16) for r in pieces(rim_refs)], axis=0)
    projected = dot(current, proj_ref[...]).astype(bf16)
    before = dot(behind, proj_ref[:, width:]).astype(bf16)
    bias = bias_ref[...]
    mixed = []
    for at in range(0, tile * steps, rows):
        mine, past = projected[at : at + rows], before[at : at + rows]
        keys = jnp.concatenate([past[:, :width], mine[:, width : 2 * width]], axis=0)
        held = jnp.concatenate([past[:, width:], mine[:, 2 * width :]], axis=0)
        mixed.append(attend(mine[:, :width], keys, held, head_size, bias))
    merged = dot(jnp.concatenate(mixed, axis=0), merge_ref[...])
    lane = lax.broadcasted_iota(jnp.int32, (steps, group, agents), 2)
    place = lax.broadcasted_iota(jnp.int32, (steps, group, agents), 1)
    total = values_ref[...]
    for n, residual in enumerate(residuals):
        final = rms(residual + merged[n * rows : (n + 1) * rows])
        value = jnp.sum(final * weight_ref[...], axis=-1, keepdims=True)
        spot = lane == place + (turn * tile + n * group)
        total = total + jnp.sum(
            jnp.where(spot, value.reshape(steps, group, 1), 0.0), axis=1
        )
    values_ref[...] = total

    @pl.when(turn == pl.num_programs(0) - 1)
    def _():
        found = values_ref[...]
        boot = boot_ref[...]
        advantages = suffix(found, rewards_ref[...], done_ref[...], boot, jnp.zeros_like(boot))
        edge_ref[...] = jnp.concatenate([found[:1], advantages[0]], axis=0)


def time_stage(residuals, rims, offset, proj, merge, weight, done, rewards, boot):
    part_steps = [r.shape[0] for r in residuals]
    steps = sum(part_steps)
    _, agents, width = residuals[0].shape
    tile = math.gcd(agents, 32)
    whole = lambda i, o: (0, 0)

    def blocks(arrays):
        return [
            pl.BlockSpec((array.shape[0], tile, width), lambda i, o: (0, i, 0))
            for array in arrays
        ]

    rows = 16 * steps
    fixed = [proj, merge, weight, done, rewards, boot]
    return pl.pallas_call(
        functools.partial(time_kernel, len(residuals), steps, tile, width // HEADS),
        grid_spec=pltpu.PrefetchScalarGridSpec(
            num_scalar_prefetch=1,
            grid=(agents // tile,),
            in_specs=blocks(residuals)
            + blocks(rims)
            + [pl.BlockSpec(array.shape, whole) for array in fixed],
            out_specs=[
                pl.BlockSpec((steps, agents), whole),
                pl.BlockSpec((2, agents), whole),
            ],
            scratch_shapes=[pltpu.VMEM((rows, rows), f32)],
        ),
        out_shape=[
            jax.ShapeDtypeStruct((steps, agents), f32),
            jax.ShapeDtypeStruct((2, agents), f32),
        ],
        compiler_params=pltpu.CompilerParams(vmem_limit_bytes=20 * MIB),
        cost_estimate=pl.CostEstimate(flops=0, bytes_accessed=rows, transcendentals=0),
        name="time_stage",
    )(offset, *residuals, *rims, *fixed)


def advantage_kernel(last_ref, values_ref, rewards_ref, done_ref, boot_ref, edge_ref, out_ref, mine_ref):
    last = last_ref[0] > 0
    arriving = edge_ref[...]
    boot = boot_ref[...]
    found = values_ref[...]
    next_value = jnp.where(last, boot, arriving[:1])
    next_advantage = jnp.where(last, 0.0, arriving[1:2])
    rows = suffix(found, rewards_ref[...], done_ref[...], next_value, next_advantage)
    out_ref[...] = jnp.concatenate(rows, axis=0)
    mine_ref[...] = jnp.concatenate([found[:1], rows[0]], axis=0)


def advantage_stage(last, values, rewards, done, boot, edge):
    return pl.pallas_call(
        advantage_kernel,
        in_specs=[pl.BlockSpec(memory_space=pltpu.SMEM)]
        + [pl.BlockSpec(memory_space=pltpu.VMEM)] * 5,
        out_specs=[pl.BlockSpec(memory_space=pltpu.VMEM)] * 2,
        out_shape=[
            jax.ShapeDtypeStruct(values.shape, f32),
            jax.ShapeDtypeStruct(edge.shape, f32),
        ],
        name="advantage_stage",
    )(last, values, rewards, done, boot, edge)


def exchange_slots(embedded, lists, capacity):
    steps, agents, width = embedded.shape
    blocks = lax.axis_size("agent")
    list_length = lists.shape[1]
    named = lists.reshape(-1)
    row_steps = jnp.arange(named.shape[0], dtype=jnp.int32) // list_length
    hits = (named[:, None] == jnp.arange(blocks, dtype=jnp.int32)[None, :]).astype(jnp.int32)
    slot = jnp.sum((jnp.cumsum(hits, axis=0) - hits) * hits, axis=1)
    slot_hits = (slot[:, None] == jnp.arange(capacity, dtype=jnp.int32)[None, :]).astype(jnp.int32)
    requests = jnp.sum(
        (hits * row_steps[:, None])[:, :, None] * slot_hits[:, None, :], axis=0
    )
    wanted = lax.all_to_all(requests, "agent", split_axis=0, concat_axis=0, tiled=True)
    outgoing = embedded[wanted.reshape(-1)].reshape(blocks, capacity, agents, width)
    arrived = lax.all_to_all(outgoing, "agent", split_axis=0, concat_axis=0, tiled=True)
    return arrived.reshape(blocks * capacity, agents, width), named * capacity + slot


OUTWARD_READY = {1: (0, 1, 1), 2: (1, 3, 3), 3: (2, 3, 4)}
ACROSS_READY = {0: (1, 2, 2), 1: (0, 0, 0), 2: (1, 3, 3), 3: (2, 3, 4)}
OUTWARD_DUE = (3, 4, 4)
ACROSS_DUE = (3, 4, 5)


def relay_sizes(steps, capacity):
    half, quarter = steps // 2, steps // 4
    chunks = [half, quarter, quarter]
    outward = [half, half, half, half, quarter + 2]
    across = [quarter, half, half, half - 1, quarter + 2, quarter + 2]
    return chunks, outward, across


def relay_codes(outward, across):
    names = {}
    code = 1
    for name, count in (("edge", len(outward)), ("swap", 2), ("far", 3), ("across", len(across))):
        names[name] = [code + n for n in range(count)]
        code += count
    names["own"] = 0
    return names


def inner_place(codes, starts, u, k):
    behind = starts[k] - starts[min(k, 1)]
    if u == 0:
        return codes["edge"][min(k, 1)] * SPAN + behind
    if u == 1:
        return codes["own"] * SPAN + starts[k]
    if u == 2:
        return codes["swap"][min(k, 1)] * SPAN + behind
    return codes["far"][k] * SPAN


def plan_kernel(steps, list_length, chunks, outward, across, place_ref, lists_ref, out_ref, in_ref, flag_ref, eloc, yloc, room):
    codes = relay_codes(outward, across)
    column, row = place_ref[0], place_ref[1]
    far_side = column >= COLUMNS // 2
    mirror = lambda u: jnp.where(far_side, COLUMNS - 1 - u, u)
    me = mirror(column)
    inner = me == 1
    starts = [sum(chunks[:k]) for k in range(len(chunks))]
    e_base = [sum(outward[:b]) for b in range(len(outward))]
    y_base = [sum(outward) + sum(across[:b]) for b in range(len(across))]
    block = lambda c, r: c * ROWS + r
    entry = lambda c, r, t, j: lists_ref[((c * ROWS + r) * steps + t) * list_length + j]

    def clear(n, _):
        out_ref[n] = -1
        return 0

    lax.fori_loop(0, sum(outward) + sum(across), clear, 0)

    @pl.when(me == 0)
    def _():
        for n in range(outward[1]):
            out_ref[e_base[1] + n] = codes["own"] * SPAN + starts[1] + n

    def named(place, r, t, source):
        hit = entry(place, r, t, 0) == source
        for j in range(1, list_length):
            hit = hit | (entry(place, r, t, j) == source)
        return hit

    def choose(sizes, ready):
        batch = jnp.int32(-1)
        for b in range(len(sizes) - 1, -1, -1):
            batch = jnp.where((room[b] < sizes[b]) & (b >= ready), b, batch)
        return batch

    def base_of(bases, batch):
        base = jnp.int32(0)
        for b, value in enumerate(bases):
            base = jnp.where(batch == b, value, base)
        return base

    def empty(sizes):
        for b in range(len(sizes)):
            room[b] = 0

    for turn in range(2):
        sender = row if turn == 0 else 1 - row
        empty(outward)
        room[0] = outward[0]
        for k, count in enumerate(chunks):
            for u in (1, 2, 3):

                def first_piece(n, _):
                    eloc[(turn * COLUMNS + 1) * steps + n] = n
                    return 0

                if u == 1 and k == 0:
                    lax.fori_loop(0, count, first_piece, 0)
                    continue

                def outer_piece(n, _, u=u, k=k):
                    t = starts[k] + n
                    source = block(mirror(u), sender)
                    need = named(0, 0, t, source)
                    for r in range(1, ROWS):
                        need = need | named(0, r, t, source)
                    batch = choose(outward, OUTWARD_READY[u][k])
                    eloc[(turn * COLUMNS + u) * steps + t] = -1

                    @pl.when(need & (batch >= 0))
                    def _():
                        slot = room[batch]
                        room[batch] = slot + 1
                        eloc[(turn * COLUMNS + u) * steps + t] = batch * SPAN + slot
                        if turn == 0:

                            @pl.when(inner)
                            def _():
                                out_ref[base_of(e_base, batch) + slot] = inner_place(codes, starts, u, k) + n

                    return 0

                lax.fori_loop(0, count, outer_piece, 0)

    for turn in range(2):
        sender = row if turn == 0 else 1 - row
        empty(across)
        for k, count in enumerate(chunks):
            for u in range(COLUMNS):

                def row_piece(n, _, u=u, k=k):
                    t = starts[k] + n
                    need = named(me, 1 - sender, t, block(mirror(u), sender))
                    if u == 0:
                        lies = jnp.int32(codes["own"] * SPAN) + t
                        when = jnp.int32(0)
                    else:
                        where = eloc[(turn * COLUMNS + u) * steps + t]
                        lies = codes["edge"][0] * SPAN + where
                        when = jnp.where(where < 0, len(across), where // SPAN + 1)
                    when = jnp.where(inner, ACROSS_READY[u][k], when)
                    lies = jnp.where(inner, inner_place(codes, starts, u, k) + n, lies)
                    batch = choose(across, when)
                    yloc[(turn * COLUMNS + u) * steps + t] = -1

                    @pl.when(need & (batch >= 0))
                    def _():
                        slot = room[batch]
                        room[batch] = slot + 1
                        yloc[(turn * COLUMNS + u) * steps + t] = batch * SPAN + slot
                        if turn == 0:
                            out_ref[base_of(y_base, batch) + slot] = lies

                    return 0

                lax.fori_loop(0, count, row_piece, 0)

    flag_ref[0] = 0
    for k, count in enumerate(chunks):

        def listed_piece(n, _, k=k):
            t = starts[k] + n // list_length
            source = entry(me, row, t, n % list_length)
            u = mirror(source // ROWS)
            same = source % ROWS == row
            e = eloc[u * steps + t]
            y = yloc[(COLUMNS + u) * steps + t]
            first = jnp.int32(0)
            for w in (0, 2, 3):
                first = jnp.where(u == w, inner_place(codes, starts, w, k), first)
            direct = jnp.where(inner, first + t - starts[k], codes["edge"][0] * SPAN + e)
            direct = jnp.where(u == me, codes["own"] * SPAN + t, direct)
            local = inner | (u == me)
            bad = jnp.where(
                same,
                jnp.logical_not(local) & ((e < 0) | (e // SPAN > OUTWARD_DUE[k])),
                (y < 0) | (y // SPAN > ACROSS_DUE[k]),
            )
            place = jnp.where(same, direct, codes["across"][0] * SPAN + y)
            in_ref[t * list_length + n % list_length] = jnp.where(bad, codes["own"] * SPAN, place)

            @pl.when(bad)
            def _():
                flag_ref[0] = 1

            return 0

        lax.fori_loop(0, count * list_length, listed_piece, 0)


def plan(lists_near, place, steps, list_length, chunks, outward, across):
    smem = pl.BlockSpec(memory_space=pltpu.SMEM)
    slots = sum(outward) + sum(across)
    return pl.pallas_call(
        functools.partial(plan_kernel, steps, list_length, chunks, outward, across),
        in_specs=[smem, smem],
        out_specs=[smem] * 3,
        out_shape=[
            jax.ShapeDtypeStruct((slots,), jnp.int32),
            jax.ShapeDtypeStruct((steps * list_length,), jnp.int32),
            jax.ShapeDtypeStruct((1,), jnp.int32),
        ],
        scratch_shapes=[
            pltpu.SMEM((2 * COLUMNS * steps,), jnp.int32),
            pltpu.SMEM((2 * COLUMNS * steps,), jnp.int32),
            pltpu.SMEM((max(len(outward), len(across)),), jnp.int32),
        ],
        name="plan",
    )(place, lists_near)


def shared(value, axes):
    count = lax.axis_size(axes)
    rows = jnp.broadcast_to(value[None], (count,) + value.shape)
    return lax.all_to_all(rows, axes, split_axis=0, concat_axis=0, tiled=True)


def column_pairs(moves):
    return [(a * ROWS + r, b * ROWS + r) for a, b in moves for r in range(ROWS)]


def relay(embedded, lists, capacity, attention, own_projection):
    steps, agents, width = embedded.shape
    list_length = lists.shape[1]
    chunks, outward, across = relay_sizes(steps, capacity)
    codes = relay_codes(outward, across)
    starts = [sum(chunks[:k]) for k in range(len(chunks))]
    e_base = [sum(outward[:b]) for b in range(len(outward))]
    y_base = [sum(outward) + sum(across[:b]) for b in range(len(across))]
    index = lax.axis_index("agent")
    place = jnp.stack([index // ROWS, index % ROWS]).astype(jnp.int32)
    send = lambda value, pairs: lax.ppermute(value, "agent", pairs)
    edges = column_pairs([(0, 1), (1, 0), (2, 3), (3, 2)])
    swap = column_pairs([(1, 2), (2, 1)])
    over = [(c * ROWS + r, c * ROWS + 1 - r) for c in range(COLUMNS) for r in range(ROWS)]
    own, edge, swapped, far, rows = (codes[n] for n in ("own", "edge", "swap", "far", "across"))
    arrays = {own: embedded}

    def pick(names):
        return {code: arrays[code] for code in names}

    def across_part(n):
        return (y_base[n], across[n], None)

    def stage(n, reads, settled, after=()):
        parts = [across_part(n)]
        if n < len(outward):
            parts.append((e_base[n], outward[n], None))
        if n == 1:
            parts.append((None, outward[1], starts[1]))
        after = tuple(arrays[rows[b]] for b in settled) + tuple(after)
        packed = pack(out_table, pick([own] + reads), parts, after)
        if n < len(outward):
            arrays[edge[n]] = send(packed[1], edges)
        arrays[rows[n]] = send(packed[0], over)
        return packed

    mine = lists.reshape(-1)
    beside = send(mine, over)
    pair = jnp.stack([jnp.where(index % ROWS == r, mine, beside) for r in range(ROWS)])
    inward = column_pairs([(0, 1), (COLUMNS - 1, COLUMNS - 2)])
    outer_pair = send(pair, inward)
    column = index // ROWS
    outer = (column == 0) | (column == COLUMNS - 1)
    near = jnp.concatenate([jnp.where(outer, pair, outer_pair), pair], axis=0).reshape(-1)
    begin = jnp.minimum(near[0], 0)
    first = lax.dynamic_slice_in_dim(embedded, begin, chunks[0], 0)
    arrays[edge[0]] = send(first, edges)
    arrays[swapped[0]] = send(first, swap)
    out_table, in_table, flag = plan(
        near, place, steps, list_length, chunks, outward, across
    )
    (token,) = pack(out_table, pick([own]), [across_part(0)])
    arrays[rows[0]] = send(token, over)
    crowded = jnp.max(shared(flag, ("groups", "agent", "tm")))
    arrays[far[0]] = send(arrays[edge[0]], swap)
    reads = edge[:1] + swapped[:1]
    packed = stage(1, reads, (0,), (token, crowded.reshape(1)))
    arrays[swapped[1]] = send(packed[2], swap)
    for k in (1, 2):
        at = starts[k] - starts[1]
        arrays[far[k]] = send(arrays[edge[1]][at : at + chunks[k]], swap)
    reads = reads + edge[1:2] + far[:1]
    projected = own_projection(packed[:1])
    packed = stage(2, reads, (1,), (projected,))
    reads = reads + edge[2:3] + swapped[1:] + far[1:2]
    packed = stage(3, reads, (2,), packed[:1])
    reads = reads + edge[3:4] + far[2:3]
    packed = stage(4, reads, (3,), packed[:1])

    def attend_chunk(k, after):
        return attention(
            starts[k], chunks[k], due(arrays, codes, starts, k), in_table, projected, after
        )

    done = [attend_chunk(0, packed[:1])]
    reads = reads + edge[4:5]
    packed = stage(5, reads, (4,), (done[0][0],))
    done.append(attend_chunk(1, packed[:1]))
    done.append(attend_chunk(2, (done[1][0],)))
    return done, crowded


def due(arrays, codes, starts, k):
    wanted = {codes["own"], *codes["edge"][: OUTWARD_DUE[k] + 1]}
    wanted |= {inner_place(codes, starts, u, k) // SPAN for u in (0, 2, 3)}
    wanted |= set(codes["across"][: ACROSS_DUE[k] + 1])
    return {code: arrays[code] for code in sorted(wanted)}


def body(
    embedded,
    block_lists,
    done_flags,
    rewards,
    bootstrap,
    agent_proj,
    agent_merge,
    time_proj,
    time_merge,
    value_weight,
):
    steps, agents, width = embedded.shape
    list_length = block_lists.shape[2]
    blocks = lax.axis_size("agent")
    lists = block_lists[0]
    capacity = max(2, (2 * steps * list_length + blocks - 1) // blocks)
    spans = lax.axis_size("tm")
    index = lax.axis_index("tm")
    offset = (index * steps).astype(jnp.int32).reshape(1)
    boot = bootstrap.reshape(1, agents)
    forward = [(i, i + 1) for i in range(spans - 1)]
    backward = [(i + 1, i) for i in range(spans - 1)]

    def own_projection(after=()):
        return own_stage(embedded, agent_proj, after)

    def attention(first, count, arrays, table, projected, after=()):
        residual, normed = agent_stage(
            embedded,
            projected,
            arrays,
            table,
            first,
            count,
            list_length,
            agent_proj,
            agent_merge,
            after,
        )
        return residual, lax.ppermute(normed, "tm", forward)

    def finish(done):
        residuals, rims = [part[0] for part in done], [part[1] for part in done]
        values, edge = time_stage(
            residuals,
            rims,
            offset,
            time_proj,
            time_merge,
            value_weight.reshape(1, width),
            done_flags,
            rewards,
            boot,
        )
        last = (index == spans - 1).astype(jnp.int32).reshape(1)
        for _ in range(max(1, spans - 1)):
            arriving = lax.ppermute(edge, "tm", backward)
            advantages, edge = advantage_stage(last, values, rewards, done_flags, boot, arriving)
        return values, advantages

    def padded():
        pool, where = exchange_slots(embedded, lists, capacity)
        return finish([attention(0, steps, {1: pool}, where + SPAN, own_projection())])

    if blocks != COLUMNS * ROWS or steps % 4:
        return padded()
    done, crowded = relay(embedded, lists, capacity, attention, own_projection)
    found = finish(done)
    return lax.cond(crowded > 0, padded, lambda: found)


def solution(mesh):
    placed = (
        P(("groups", "tm"), "agent", None),
        P(("groups", "agent"), "tm", None),
        P(("groups", "tm"), "agent"),
        P(("groups", "tm"), "agent"),
        P(("groups", "agent")),
        P(),
        P(),
        P(),
        P(),
        P(),
    )
    return jax.shard_map(
        body,
        mesh=mesh,
        in_specs=placed,
        out_specs=(P(("groups", "tm"), "agent"), P(("groups", "tm"), "agent")),
        check_vma=False,
    )
```

```python
import functools
import math

import jax
import jax.numpy as jnp
from jax import lax
from jax.experimental import pallas as pl
from jax.experimental.pallas import tpu as pltpu
from jax.sharding import PartitionSpec as P

HEADS = 8
WINDOW = 16
discount = 0.9997
trace_decay = 0.995
epsilon = 1e-06
bf16 = jnp.bfloat16
f32 = jnp.float32
MIB = 1024 * 1024
SPAN = 1024
COLUMNS = 4
ROWS = 2


def rms(values):
    return values * lax.rsqrt(jnp.mean(values * values, axis=-1, keepdims=True) + epsilon)


def dot(a, b):
    return jnp.dot(a, b, preferred_element_type=f32)


def dot_t(a, b):
    return lax.dot_general(a, b, (((1,), (1,)), ((), ())), preferred_element_type=f32)


def attend(queries, keys, values, head_size, bias):
    rows, width = queries.shape
    scale = head_size ** (-0.5) * math.log2(math.e)
    pair = 2 * head_size
    lane = lax.broadcasted_iota(jnp.int32, (rows, pair), 1)
    first = lane < head_size
    ones = jnp.ones((keys.shape[0], pair), bf16)
    mixed = []
    for at in range(0, width, pair):
        both = queries[:, at : at + pair]
        none = jnp.zeros_like(both)
        stacked = jnp.concatenate(
            [jnp.where(first, both, none), jnp.where(first, none, both)], axis=0
        )
        scores = dot_t(stacked, keys[:, at : at + pair])
        if bias is not None:
            scores = scores + bias
        weights = jnp.exp2((scores - jnp.max(scores, axis=-1, keepdims=True)) * scale).astype(bf16)
        summed = dot(weights, jnp.concatenate([values[:, at : at + pair], ones], axis=1))
        result = summed[:, :pair] / summed[:, pair:]
        mixed.append(jnp.where(first, result[:rows], result[rows:]).astype(bf16))
    return jnp.concatenate(mixed, axis=1)


def fetch(entry, arrays, target, sem):
    for code, ref in arrays.items():

        @pl.when(entry // SPAN == code)
        def _(ref=ref):
            pltpu.make_async_copy(ref.at[entry % SPAN], target, sem).start()


def own_kernel(idle, own_ref, proj_ref, flag_ref, *refs):
    projected_ref, tile_ref = refs[idle:]
    tile_ref[...] = jnp.full(tile_ref.shape, flag_ref[0], jnp.int32)
    together, agents, width = own_ref.shape
    mine = rms(own_ref[...].astype(f32).reshape(together * agents, width)).astype(bf16)
    projected = dot(mine, proj_ref[...]).astype(bf16)
    projected_ref[...] = projected.reshape(together, agents, proj_ref.shape[1])


def own_stage(embedded, proj, flag, after=()):
    steps, agents, width = embedded.shape
    together = math.gcd(steps, 4)
    return pl.pallas_call(
        functools.partial(own_kernel, len(after)),
        grid=(steps // together,),
        in_specs=[
            pl.BlockSpec((together, agents, width), lambda i: (i, 0, 0)),
            pl.BlockSpec(proj.shape, lambda i: (0, 0)),
            pl.BlockSpec(memory_space=pltpu.SMEM),
        ]
        + [pl.BlockSpec(memory_space=pltpu.HBM)] * len(after),
        out_specs=[
            pl.BlockSpec((together, agents, proj.shape[1]), lambda i: (i, 0, 0)),
            pl.BlockSpec((8, 128), lambda i: (0, 0)),
        ],
        out_shape=[
            jax.ShapeDtypeStruct((steps, agents, proj.shape[1]), bf16),
            jax.ShapeDtypeStruct((8, 128), jnp.int32),
        ],
        compiler_params=pltpu.CompilerParams(vmem_limit_bytes=18 * MIB),
        name="own_stage",
    )(embedded, proj, flag, *after)


def agent_kernel(
    list_length, first_step, codes, idle, head_size, table_ref, own_ref, projected_ref, *refs
):
    arrays = dict(zip(codes, refs))
    proj_ref, merge_ref, residual_ref, normed_ref, held_ref, sems = refs[len(codes) + idle :]
    together, agents, width = own_ref.shape
    turn = pl.program_id(0)
    pieces = [(s, j) for s in range(together) for j in range(list_length)]

    def begin(turn):
        slot = turn % 2
        for n, (s, j) in enumerate(pieces):
            entry = table_ref[(first_step + turn * together + s) * list_length + j]
            fetch(entry, arrays, held_ref.at[slot, n], sems.at[slot, n])

    @pl.when(turn == 0)
    def _():
        begin(turn)

    @pl.when(turn + 1 < pl.num_programs(0))
    def _():
        begin(turn + 1)

    slot = turn % 2
    for n in range(len(pieces)):
        pltpu.make_async_copy(refs[0].at[0], held_ref.at[slot, n], sems.at[slot, n]).wait()
    own = own_ref[...].astype(f32).reshape(together * agents, width)
    listed = held_ref[slot].astype(f32).reshape(len(pieces) * agents, width)
    theirs = rms(listed).astype(bf16)
    projected = projected_ref[...].reshape(together * agents, 3 * width)
    queries, near = projected[:, :width], projected[:, width:]
    away = dot(theirs, proj_ref[:, width:]).astype(bf16)
    mixed = []
    for s in range(together):
        here = slice(s * agents, (s + 1) * agents)
        there = slice(s * list_length * agents, (s + 1) * list_length * agents)
        keyvals = jnp.concatenate([near[here], away[there]], axis=0)
        mixed.append(
            attend(queries[here], keyvals[:, :width], keyvals[:, width:], head_size, None)
        )
    residual = own + dot(jnp.concatenate(mixed, axis=0), merge_ref[...])
    residual_ref[...] = residual.reshape(together, agents, width)
    normed_ref[...] = rms(residual).astype(bf16).reshape(together, agents, width)


def agent_stage(
    embedded, projected, arrays, table, first_step, steps, list_length, proj, merge, after=()
):
    _, agents, width = embedded.shape
    together = math.gcd(steps, math.gcd(first_step, 2))
    piece = (together, agents, width)
    whole = lambda i, w: (0, 0)
    flops = 2 * steps * agents * width * width * (4 + 2 * list_length + 2 * (1 + list_length))
    return pl.pallas_call(
        functools.partial(
            agent_kernel, list_length, first_step, tuple(arrays), len(after), width // HEADS
        ),
        grid_spec=pltpu.PrefetchScalarGridSpec(
            num_scalar_prefetch=1,
            grid=(steps // together,),
            in_specs=[
                pl.BlockSpec((together, agents, cols), lambda i, w: (first_step // together + i, 0, 0))
                for cols in (width, 3 * width)
            ]
            + [pl.BlockSpec(memory_space=pltpu.HBM)] * (len(arrays) + len(after))
            + [pl.BlockSpec(proj.shape, whole), pl.BlockSpec(merge.shape, whole)],
            out_specs=[pl.BlockSpec(piece, lambda i, w: (i, 0, 0))] * 2,
            scratch_shapes=[
                pltpu.VMEM((2, together * list_length, agents, width), bf16),
                pltpu.SemaphoreType.DMA((2, together * list_length)),
            ],
        ),
        out_shape=[
            jax.ShapeDtypeStruct((steps, agents, width), f32),
            jax.ShapeDtypeStruct((steps, agents, width), bf16),
        ],
        compiler_params=pltpu.CompilerParams(vmem_limit_bytes=18 * MIB),
        cost_estimate=pl.CostEstimate(
            flops=5 * flops, bytes_accessed=steps * agents * width * 12, transcendentals=0
        ),
        name="agent_stage",
    )(table, embedded, projected, *arrays.values(), *after, proj, merge)


def pack_kernel(codes, parts, idle, table_ref, *refs):
    arrays = dict(zip(codes, refs))
    outs, (held_ref, in_sems, out_sems) = refs[len(codes) + idle : -3], refs[-3:]
    slots = []
    for out, (offset, count, first) in zip(outs, parts):
        slots += [(offset, first, n, out.at[n]) for n in range(count)]

    def guarded(offset, n, action):
        if offset is None:
            action()
        else:
            pl.when(table_ref[offset + n] >= 0)(action)

    for at, (offset, first, n, _) in enumerate(slots):
        if offset is None:
            own = arrays[0].at[first + n]
            pltpu.make_async_copy(own, held_ref.at[at], in_sems.at[at]).start()
        else:
            fetch(table_ref[offset + n], arrays, held_ref.at[at], in_sems.at[at])
    for at, (offset, first, n, target) in enumerate(slots):

        def pass_on(at=at, target=target):
            pltpu.make_async_copy(refs[0].at[0], held_ref.at[at], in_sems.at[at]).wait()
            pltpu.make_async_copy(held_ref.at[at], target, out_sems.at[at]).start()

        guarded(offset, n, pass_on)
    for at, (offset, first, n, target) in enumerate(slots):

        def finish(at=at, target=target):
            pltpu.make_async_copy(held_ref.at[at], target, out_sems.at[at]).wait()

        guarded(offset, n, finish)


def pack(table, arrays, parts, after=()):
    piece = next(iter(arrays.values())).shape[1:]
    slots = sum(count for _, count, _ in parts)
    smem = pl.BlockSpec(memory_space=pltpu.SMEM)
    hbm = pl.BlockSpec(memory_space=pltpu.HBM)
    out_specs = [hbm] * len(parts)
    out_shape = [jax.ShapeDtypeStruct((count,) + piece, bf16) for _, count, _ in parts]
    return pl.pallas_call(
        functools.partial(pack_kernel, tuple(arrays), tuple(parts), len(after)),
        in_specs=[smem] + [hbm] * (len(arrays) + len(after)),
        out_specs=out_specs,
        out_shape=out_shape,
        scratch_shapes=[
            pltpu.VMEM((slots,) + piece, bf16),
            pltpu.SemaphoreType.DMA((slots,)),
            pltpu.SemaphoreType.DMA((slots,)),
        ],
        cost_estimate=pl.CostEstimate(
            flops=0, bytes_accessed=piece[0] * piece[1], transcendentals=0
        ),
        compiler_params=pltpu.CompilerParams(
            vmem_limit_bytes=slots * piece[0] * piece[1] * 2 + 2 * MIB
        ),
        name="pack",
    )(table, *arrays.values(), *after)


def suffix(values, rewards, done, next_value, next_advantage):
    steps = values.shape[0]
    living = 1.0 - done.astype(f32)
    running, following, rows = next_advantage, next_value, [None] * steps
    for step in range(steps - 1, -1, -1):
        alive = living[step : step + 1]
        value = values[step : step + 1]
        change = rewards[step : step + 1] + discount * alive * following - value
        running = change + discount * trace_decay * alive * running
        rows[step] = running
        following = value
    return rows


def time_kernel(parts, steps, tile, head_size, offset_ref, *refs):
    refs = list(refs)
    residual_refs = [refs.pop(0) for _ in range(parts)]
    rim_refs = [refs.pop(0) for _ in range(parts)]
    proj_ref, merge_ref, weight_ref, done_ref, rewards_ref, boot_ref = refs[:6]
    values_ref, edge_ref, bias_ref = refs[6:]
    width = proj_ref.shape[0]
    turn = pl.program_id(0)
    group = 8
    rows = steps * group
    agents = values_ref.shape[1]

    @pl.when(turn == 0)
    def _():
        r = lax.broadcasted_iota(jnp.int32, (2 * rows, 2 * rows), 0) % rows
        c = lax.broadcasted_iota(jnp.int32, (2 * rows, 2 * rows), 1)
        query_step = r // group
        key_step = c // group - steps
        allowed = (
            (r % group == c % group)
            & (key_step <= query_step)
            & (key_step > query_step - WINDOW)
            & (key_step + offset_ref[0] >= 0)
        )
        bias_ref[...] = jnp.where(allowed, 0.0, -1e30)
        values_ref[...] = jnp.zeros_like(values_ref)

    def pieces(part_refs):
        whole = jnp.concatenate([ref[...].astype(f32) for ref in part_refs], axis=0)
        return [
            whole[:, at : at + group].reshape(rows, width) for at in range(0, tile, group)
        ]

    residuals = pieces(residual_refs)
    current = jnp.concatenate([rms(r).astype(bf16) for r in residuals], axis=0)
    behind = jnp.concatenate([r.astype(bf16) for r in pieces(rim_refs)], axis=0)
    projected = dot(current, proj_ref[...]).astype(bf16)
    before = dot(behind, proj_ref[:, width:]).astype(bf16)
    bias = bias_ref[...]
    mixed = []
    for at in range(0, tile * steps, rows):
        mine, past = projected[at : at + rows], before[at : at + rows]
        keys = jnp.concatenate([past[:, :width], mine[:, width : 2 * width]], axis=0)
        held = jnp.concatenate([past[:, width:], mine[:, 2 * width :]], axis=0)
        mixed.append(attend(mine[:, :width], keys, held, head_size, bias))
    merged = dot(jnp.concatenate(mixed, axis=0), merge_ref[...])
    lane = lax.broadcasted_iota(jnp.int32, (steps, group, agents), 2)
    place = lax.broadcasted_iota(jnp.int32, (steps, group, agents), 1)
    total = values_ref[...]
    for n, residual in enumerate(residuals):
        final = rms(residual + merged[n * rows : (n + 1) * rows])
        value = jnp.sum(final * weight_ref[...], axis=-1, keepdims=True)
        spot = lane == place + (turn * tile + n * group)
        total = total + jnp.sum(
            jnp.where(spot, value.reshape(steps, group, 1), 0.0), axis=1
        )
    values_ref[...] = total

    @pl.when(turn == pl.num_programs(0) - 1)
    def _():
        found = values_ref[...]
        boot = boot_ref[...]
        advantages = suffix(found, rewards_ref[...], done_ref[...], boot, jnp.zeros_like(boot))
        edge_ref[...] = jnp.concatenate([found[:1], advantages[0]], axis=0)


def time_stage(residuals, rims, offset, proj, merge, weight, done, rewards, boot):
    part_steps = [r.shape[0] for r in residuals]
    steps = sum(part_steps)
    _, agents, width = residuals[0].shape
    tile = math.gcd(agents, 32)
    whole = lambda i, o: (0, 0)

    def blocks(arrays):
        return [
            pl.BlockSpec((array.shape[0], tile, width), lambda i, o: (0, i, 0))
            for array in arrays
        ]

    rows = 16 * steps
    fixed = [proj, merge, weight, done, rewards, boot]
    return pl.pallas_call(
        functools.partial(time_kernel, len(residuals), steps, tile, width // HEADS),
        grid_spec=pltpu.PrefetchScalarGridSpec(
            num_scalar_prefetch=1,
            grid=(agents // tile,),
            in_specs=blocks(residuals)
            + blocks(rims)
            + [pl.BlockSpec(array.shape, whole) for array in fixed],
            out_specs=[
                pl.BlockSpec((steps, agents), whole),
                pl.BlockSpec((2, agents), whole),
            ],
            scratch_shapes=[pltpu.VMEM((rows, rows), f32)],
        ),
        out_shape=[
            jax.ShapeDtypeStruct((steps, agents), f32),
            jax.ShapeDtypeStruct((2, agents), f32),
        ],
        compiler_params=pltpu.CompilerParams(vmem_limit_bytes=20 * MIB),
        cost_estimate=pl.CostEstimate(flops=0, bytes_accessed=rows, transcendentals=0),
        name="time_stage",
    )(offset, *residuals, *rims, *fixed)


def advantage_kernel(last_ref, values_ref, rewards_ref, done_ref, boot_ref, edge_ref, out_ref, mine_ref):
    last = last_ref[0] > 0
    arriving = edge_ref[...]
    boot = boot_ref[...]
    found = values_ref[...]
    next_value = jnp.where(last, boot, arriving[:1])
    next_advantage = jnp.where(last, 0.0, arriving[1:2])
    rows = suffix(found, rewards_ref[...], done_ref[...], next_value, next_advantage)
    out_ref[...] = jnp.concatenate(rows, axis=0)
    mine_ref[...] = jnp.concatenate([found[:1], rows[0]], axis=0)


def advantage_stage(last, values, rewards, done, boot, edge):
    return pl.pallas_call(
        advantage_kernel,
        in_specs=[pl.BlockSpec(memory_space=pltpu.SMEM)]
        + [pl.BlockSpec(memory_space=pltpu.VMEM)] * 5,
        out_specs=[pl.BlockSpec(memory_space=pltpu.VMEM)] * 2,
        out_shape=[
            jax.ShapeDtypeStruct(values.shape, f32),
            jax.ShapeDtypeStruct(edge.shape, f32),
        ],
        name="advantage_stage",
    )(last, values, rewards, done, boot, edge)


def exchange_slots(embedded, lists, capacity):
    steps, agents, width = embedded.shape
    blocks = lax.axis_size("agent")
    list_length = lists.shape[1]
    named = lists.reshape(-1)
    row_steps = jnp.arange(named.shape[0], dtype=jnp.int32) // list_length
    hits = (named[:, None] == jnp.arange(blocks, dtype=jnp.int32)[None, :]).astype(jnp.int32)
    slot = jnp.sum((jnp.cumsum(hits, axis=0) - hits) * hits, axis=1)
    slot_hits = (slot[:, None] == jnp.arange(capacity, dtype=jnp.int32)[None, :]).astype(jnp.int32)
    requests = jnp.sum(
        (hits * row_steps[:, None])[:, :, None] * slot_hits[:, None, :], axis=0
    )
    wanted = lax.all_to_all(requests, "agent", split_axis=0, concat_axis=0, tiled=True)
    outgoing = embedded[wanted.reshape(-1)].reshape(blocks, capacity, agents, width)
    arrived = lax.all_to_all(outgoing, "agent", split_axis=0, concat_axis=0, tiled=True)
    return arrived.reshape(blocks * capacity, agents, width), named * capacity + slot


OUTWARD_READY = {1: (0, 1, 1), 2: (1, 3, 3), 3: (2, 3, 4)}
ACROSS_READY = {0: (1, 2, 2), 1: (0, 0, 0), 2: (1, 3, 3), 3: (2, 3, 4)}
OUTWARD_DUE = (3, 4, 4)
ACROSS_DUE = (3, 4, 5)


def relay_sizes(steps, capacity):
    half, quarter = steps // 2, steps // 4
    chunks = [half, quarter, quarter]
    outward = [half, half, half, half, quarter + 2]
    across = [quarter, half, half, half - 1, quarter + 2, quarter + 2]
    return chunks, outward, across


def relay_codes(outward, across):
    names = {}
    code = 1
    for name, count in (("edge", len(outward)), ("swap", 2), ("far", 3), ("across", len(across))):
        names[name] = [code + n for n in range(count)]
        code += count
    names["own"] = 0
    return names


def inner_place(codes, starts, u, k):
    behind = starts[k] - starts[min(k, 1)]
    if u == 0:
        return codes["edge"][min(k, 1)] * SPAN + behind
    if u == 1:
        return codes["own"] * SPAN + starts[k]
    if u == 2:
        return codes["swap"][min(k, 1)] * SPAN + behind
    return codes["far"][k] * SPAN


def plan_kernel(steps, list_length, chunks, outward, across, place_ref, lists_ref, out_ref, in_ref, flag_ref, eloc, yloc, room):
    codes = relay_codes(outward, across)
    column, row = place_ref[0], place_ref[1]
    far_side = column >= COLUMNS // 2
    mirror = lambda u: jnp.where(far_side, COLUMNS - 1 - u, u)
    me = mirror(column)
    inner = me == 1
    starts = [sum(chunks[:k]) for k in range(len(chunks))]
    e_base = [sum(outward[:b]) for b in range(len(outward))]
    y_base = [sum(outward) + sum(across[:b]) for b in range(len(across))]
    block = lambda c, r: c * ROWS + r
    entry = lambda c, r, t, j: lists_ref[((c * ROWS + r) * steps + t) * list_length + j]

    def clear(n, _):
        out_ref[n] = -1
        return 0

    lax.fori_loop(0, sum(outward) + sum(across), clear, 0)

    @pl.when(me == 0)
    def _():
        for n in range(outward[1]):
            out_ref[e_base[1] + n] = codes["own"] * SPAN + starts[1] + n

    def named(place, r, t, source):
        hit = entry(place, r, t, 0) == source
        for j in range(1, list_length):
            hit = hit | (entry(place, r, t, j) == source)
        return hit

    def choose(sizes, ready):
        batch = jnp.int32(-1)
        for b in range(len(sizes) - 1, -1, -1):
            batch = jnp.where((room[b] < sizes[b]) & (b >= ready), b, batch)
        return batch

    def base_of(bases, batch):
        base = jnp.int32(0)
        for b, value in enumerate(bases):
            base = jnp.where(batch == b, value, base)
        return base

    def empty(sizes):
        for b in range(len(sizes)):
            room[b] = 0

    for turn in range(2):
        sender = row if turn == 0 else 1 - row
        empty(outward)
        room[0] = outward[0]
        for k, count in enumerate(chunks):
            for u in (1, 2, 3):

                def first_piece(n, _):
                    eloc[(turn * COLUMNS + 1) * steps + n] = n
                    return 0

                if u == 1 and k == 0:
                    lax.fori_loop(0, count, first_piece, 0)
                    continue

                def outer_piece(n, _, u=u, k=k):
                    t = starts[k] + n
                    source = block(mirror(u), sender)
                    need = named(0, 0, t, source)
                    for r in range(1, ROWS):
                        need = need | named(0, r, t, source)
                    batch = choose(outward, OUTWARD_READY[u][k])
                    eloc[(turn * COLUMNS + u) * steps + t] = -1

                    @pl.when(need & (batch >= 0))
                    def _():
                        slot = room[batch]
                        room[batch] = slot + 1
                        eloc[(turn * COLUMNS + u) * steps + t] = batch * SPAN + slot
                        if turn == 0:

                            @pl.when(inner)
                            def _():
                                out_ref[base_of(e_base, batch) + slot] = inner_place(codes, starts, u, k) + n

                    return 0

                lax.fori_loop(0, count, outer_piece, 0)

    for turn in range(2):
        sender = row if turn == 0 else 1 - row
        empty(across)
        for k, count in enumerate(chunks):
            for u in range(COLUMNS):

                def row_piece(n, _, u=u, k=k):
                    t = starts[k] + n
                    need = named(me, 1 - sender, t, block(mirror(u), sender))
                    if u == 0:
                        lies = jnp.int32(codes["own"] * SPAN) + t
                        when = jnp.int32(0)
                    else:
                        where = eloc[(turn * COLUMNS + u) * steps + t]
                        lies = codes["edge"][0] * SPAN + where
                        when = jnp.where(where < 0, len(across), where // SPAN + 1)
                    when = jnp.where(inner, ACROSS_READY[u][k], when)
                    lies = jnp.where(inner, inner_place(codes, starts, u, k) + n, lies)
                    batch = choose(across, when)
                    yloc[(turn * COLUMNS + u) * steps + t] = -1

                    @pl.when(need & (batch >= 0))
                    def _():
                        slot = room[batch]
                        room[batch] = slot + 1
                        yloc[(turn * COLUMNS + u) * steps + t] = batch * SPAN + slot
                        if turn == 0:
                            out_ref[base_of(y_base, batch) + slot] = lies

                    return 0

                lax.fori_loop(0, count, row_piece, 0)

    flag_ref[0] = 0
    for k, count in enumerate(chunks):

        def listed_piece(n, _, k=k):
            t = starts[k] + n // list_length
            source = entry(me, row, t, n % list_length)
            u = mirror(source // ROWS)
            same = source % ROWS == row
            e = eloc[u * steps + t]
            y = yloc[(COLUMNS + u) * steps + t]
            first = jnp.int32(0)
            for w in (0, 2, 3):
                first = jnp.where(u == w, inner_place(codes, starts, w, k), first)
            direct = jnp.where(inner, first + t - starts[k], codes["edge"][0] * SPAN + e)
            direct = jnp.where(u == me, codes["own"] * SPAN + t, direct)
            local = inner | (u == me)
            bad = jnp.where(
                same,
                jnp.logical_not(local) & ((e < 0) | (e // SPAN > OUTWARD_DUE[k])),
                (y < 0) | (y // SPAN > ACROSS_DUE[k]),
            )
            place = jnp.where(same, direct, codes["across"][0] * SPAN + y)
            in_ref[t * list_length + n % list_length] = jnp.where(bad, codes["own"] * SPAN, place)

            @pl.when(bad)
            def _():
                flag_ref[0] = 1

            return 0

        lax.fori_loop(0, count * list_length, listed_piece, 0)


def plan(lists_near, place, steps, list_length, chunks, outward, across):
    smem = pl.BlockSpec(memory_space=pltpu.SMEM)
    slots = sum(outward) + sum(across)
    return pl.pallas_call(
        functools.partial(plan_kernel, steps, list_length, chunks, outward, across),
        in_specs=[smem, smem],
        out_specs=[smem] * 3,
        out_shape=[
            jax.ShapeDtypeStruct((slots,), jnp.int32),
            jax.ShapeDtypeStruct((steps * list_length,), jnp.int32),
            jax.ShapeDtypeStruct((1,), jnp.int32),
        ],
        scratch_shapes=[
            pltpu.SMEM((2 * COLUMNS * steps,), jnp.int32),
            pltpu.SMEM((2 * COLUMNS * steps,), jnp.int32),
            pltpu.SMEM((max(len(outward), len(across)),), jnp.int32),
        ],
        name="plan",
    )(place, lists_near)


def shared(value, axes):
    count = lax.axis_size(axes)
    rows = jnp.broadcast_to(value[None], (count,) + value.shape)
    return lax.all_to_all(rows, axes, split_axis=0, concat_axis=0, tiled=True)


def column_pairs(moves):
    return [(a * ROWS + r, b * ROWS + r) for a, b in moves for r in range(ROWS)]


def relay(embedded, lists, capacity, attention, own_projection):
    steps, agents, width = embedded.shape
    list_length = lists.shape[1]
    chunks, outward, across = relay_sizes(steps, capacity)
    codes = relay_codes(outward, across)
    starts = [sum(chunks[:k]) for k in range(len(chunks))]
    e_base = [sum(outward[:b]) for b in range(len(outward))]
    y_base = [sum(outward) + sum(across[:b]) for b in range(len(across))]
    index = lax.axis_index("agent")
    place = jnp.stack([index // ROWS, index % ROWS]).astype(jnp.int32)
    send = lambda value, pairs: lax.ppermute(value, "agent", pairs)
    edges = column_pairs([(0, 1), (1, 0), (2, 3), (3, 2)])
    swap = column_pairs([(1, 2), (2, 1)])
    over = [(c * ROWS + r, c * ROWS + 1 - r) for c in range(COLUMNS) for r in range(ROWS)]
    own, edge, swapped, far, rows = (codes[n] for n in ("own", "edge", "swap", "far", "across"))
    arrays = {own: embedded}

    def pick(names):
        return {code: arrays[code] for code in names}

    def across_part(n):
        return (y_base[n], across[n], None)

    def stage(n, reads, settled, after=()):
        parts = [across_part(n)]
        if n < len(outward):
            parts.append((e_base[n], outward[n], None))
        after = tuple(arrays[rows[b]] for b in settled) + tuple(after)
        packed = pack(out_table, pick([own] + reads), parts, after)
        if n < len(outward):
            arrays[edge[n]] = send(packed[1], edges)
        arrays[rows[n]] = send(packed[0], over)
        return packed

    mine = lists.reshape(-1)
    beside = send(mine, over)
    pair = jnp.stack([jnp.where(index % ROWS == r, mine, beside) for r in range(ROWS)])
    inward = column_pairs([(0, 1), (COLUMNS - 1, COLUMNS - 2)])
    outer_pair = send(pair, inward)
    column = index // ROWS
    outer = (column == 0) | (column == COLUMNS - 1)
    near = jnp.concatenate([jnp.where(outer, pair, outer_pair), pair], axis=0).reshape(-1)
    begin = jnp.minimum(near[0], 0)
    first = lax.dynamic_slice_in_dim(embedded, begin, chunks[0], 0)
    arrays[edge[0]] = send(first, edges)
    arrays[swapped[0]] = send(first, swap)
    out_table, in_table, flag = plan(
        near, place, steps, list_length, chunks, outward, across
    )
    (token,) = pack(out_table, pick([own]), [across_part(0)])
    arrays[rows[0]] = send(token, over)
    arrays[far[0]] = send(arrays[edge[0]], swap)
    reads = edge[:1] + swapped[:1]
    packed = stage(1, reads, (0,), (token,))
    projected, tile = own_projection(flag, packed[:1])
    crowded = jnp.max(shared(tile[0, :1], ("groups", "agent", "tm")))
    (second,) = pack(out_table, pick([own]), [(None, outward[1], starts[1])], (crowded.reshape(1),))
    arrays[swapped[1]] = send(second, swap)
    for k in (1, 2):
        at = starts[k] - starts[1]
        arrays[far[k]] = send(arrays[edge[1]][at : at + chunks[k]], swap)
    reads = reads + edge[1:2] + far[:1]
    packed = stage(2, reads, (1,), (second,))
    reads = reads + edge[2:3] + swapped[1:] + far[1:2]
    packed = stage(3, reads, (2,), packed[:1])
    reads = reads + edge[3:4] + far[2:3]
    packed = stage(4, reads, (3,), packed[:1])

    def attend_chunk(k, after):
        return attention(
            starts[k], chunks[k], due(arrays, codes, starts, k), in_table, projected, after
        )

    done = [attend_chunk(0, packed[:1])]
    reads = reads + edge[4:5]
    packed = stage(5, reads, (4,), (done[0][0],))
    done.append(attend_chunk(1, packed[:1]))
    done.append(attend_chunk(2, (done[1][0],)))
    return done, crowded


def due(arrays, codes, starts, k):
    wanted = {codes["own"], *codes["edge"][: OUTWARD_DUE[k] + 1]}
    wanted |= {inner_place(codes, starts, u, k) // SPAN for u in (0, 2, 3)}
    wanted |= set(codes["across"][: ACROSS_DUE[k] + 1])
    return {code: arrays[code] for code in sorted(wanted)}


def body(
    embedded,
    block_lists,
    done_flags,
    rewards,
    bootstrap,
    agent_proj,
    agent_merge,
    time_proj,
    time_merge,
    value_weight,
):
    steps, agents, width = embedded.shape
    list_length = block_lists.shape[2]
    blocks = lax.axis_size("agent")
    lists = block_lists[0]
    capacity = max(2, (2 * steps * list_length + blocks - 1) // blocks)
    spans = lax.axis_size("tm")
    index = lax.axis_index("tm")
    offset = (index * steps).astype(jnp.int32).reshape(1)
    boot = bootstrap.reshape(1, agents)
    forward = [(i, i + 1) for i in range(spans - 1)]
    backward = [(i + 1, i) for i in range(spans - 1)]

    def own_projection(flag, after=()):
        return own_stage(embedded, agent_proj, flag, after)

    def attention(first, count, arrays, table, projected, after=()):
        residual, normed = agent_stage(
            embedded,
            projected,
            arrays,
            table,
            first,
            count,
            list_length,
            agent_proj,
            agent_merge,
            after,
        )
        return residual, lax.ppermute(normed, "tm", forward)

    def finish(done):
        residuals, rims = [part[0] for part in done], [part[1] for part in done]
        values, edge = time_stage(
            residuals,
            rims,
            offset,
            time_proj,
            time_merge,
            value_weight.reshape(1, width),
            done_flags,
            rewards,
            boot,
        )
        last = (index == spans - 1).astype(jnp.int32).reshape(1)
        for _ in range(max(1, spans - 1)):
            arriving = lax.ppermute(edge, "tm", backward)
            advantages, edge = advantage_stage(last, values, rewards, done_flags, boot, arriving)
        return values, advantages

    def padded():
        pool, where = exchange_slots(embedded, lists, capacity)
        return finish([attention(0, steps, {1: pool}, where + SPAN, own_projection(offset)[0])])

    if blocks != COLUMNS * ROWS or steps % 4:
        return padded()
    done, crowded = relay(embedded, lists, capacity, attention, own_projection)
    found = finish(done)
    return lax.cond(crowded > 0, padded, lambda: found)


def solution(mesh):
    placed = (
        P(("groups", "tm"), "agent", None),
        P(("groups", "agent"), "tm", None),
        P(("groups", "tm"), "agent"),
        P(("groups", "tm"), "agent"),
        P(("groups", "agent")),
        P(),
        P(),
        P(),
        P(),
        P(),
    )
    return jax.shard_map(
        body,
        mesh=mesh,
        in_specs=placed,
        out_specs=(P(("groups", "tm"), "agent"), P(("groups", "tm"), "agent")),
        check_vma=False,
    )
```

```python
import functools
import math

import jax
import jax.numpy as jnp
from jax import lax
from jax.experimental import pallas as pl
from jax.experimental.pallas import tpu as pltpu
from jax.sharding import PartitionSpec as P

HEADS = 8
WINDOW = 16
discount = 0.9997
trace_decay = 0.995
epsilon = 1e-06
bf16 = jnp.bfloat16
f32 = jnp.float32
MIB = 1024 * 1024
SPAN = 1024
COLUMNS = 4
ROWS = 2


def rms(values):
    return values * lax.rsqrt(jnp.mean(values * values, axis=-1, keepdims=True) + epsilon)


def dot(a, b):
    return jnp.dot(a, b, preferred_element_type=f32)


def dot_t(a, b):
    return lax.dot_general(a, b, (((1,), (1,)), ((), ())), preferred_element_type=f32)


def attend(queries, keys, values, head_size, bias):
    rows, width = queries.shape
    scale = head_size ** (-0.5) * math.log2(math.e)
    pair = 2 * head_size
    lane = lax.broadcasted_iota(jnp.int32, (rows, pair), 1)
    first = lane < head_size
    ones = jnp.ones((keys.shape[0], pair), bf16)
    mixed = []
    for at in range(0, width, pair):
        both = queries[:, at : at + pair]
        none = jnp.zeros_like(both)
        stacked = jnp.concatenate(
            [jnp.where(first, both, none), jnp.where(first, none, both)], axis=0
        )
        scores = dot_t(stacked, keys[:, at : at + pair])
        if bias is not None:
            scores = scores + bias
        weights = jnp.exp2((scores - jnp.max(scores, axis=-1, keepdims=True)) * scale).astype(bf16)
        summed = dot(weights, jnp.concatenate([values[:, at : at + pair], ones], axis=1))
        result = summed[:, :pair] / summed[:, pair:]
        mixed.append(jnp.where(first, result[:rows], result[rows:]).astype(bf16))
    return jnp.concatenate(mixed, axis=1)


def fetch(entry, arrays, target, sem):
    for code, ref in arrays.items():

        @pl.when(entry // SPAN == code)
        def _(ref=ref):
            pltpu.make_async_copy(ref.at[entry % SPAN], target, sem).start()


def own_kernel(idle, own_ref, proj_ref, *refs):
    projected_ref = refs[idle]
    together, agents, width = own_ref.shape
    mine = rms(own_ref[...].astype(f32).reshape(together * agents, width)).astype(bf16)
    projected = dot(mine, proj_ref[...]).astype(bf16)
    projected_ref[...] = projected.reshape(together, agents, proj_ref.shape[1])


def own_stage(embedded, proj, after=()):
    steps, agents, width = embedded.shape
    together = math.gcd(steps, 4)
    return pl.pallas_call(
        functools.partial(own_kernel, len(after)),
        grid=(steps // together,),
        in_specs=[
            pl.BlockSpec((together, agents, width), lambda i: (i, 0, 0)),
            pl.BlockSpec(proj.shape, lambda i: (0, 0)),
        ]
        + [pl.BlockSpec(memory_space=pltpu.HBM)] * len(after),
        out_specs=pl.BlockSpec((together, agents, proj.shape[1]), lambda i: (i, 0, 0)),
        out_shape=jax.ShapeDtypeStruct((steps, agents, proj.shape[1]), bf16),
        compiler_params=pltpu.CompilerParams(vmem_limit_bytes=24 * MIB),
        name="own_stage",
    )(embedded, proj, *after)


def agent_kernel(
    list_length, first_step, codes, idle, head_size, table_ref, own_ref, projected_ref, *refs
):
    arrays = dict(zip(codes, refs))
    proj_ref, merge_ref, residual_ref, normed_ref, held_ref, sems = refs[len(codes) + idle :]
    together, agents, width = own_ref.shape
    turn = pl.program_id(0)
    pieces = [(s, j) for s in range(together) for j in range(list_length)]

    def begin(turn):
        slot = turn % 2
        for n, (s, j) in enumerate(pieces):
            entry = table_ref[(first_step + turn * together + s) * list_length + j]
            fetch(entry, arrays, held_ref.at[slot, n], sems.at[slot, n])

    @pl.when(turn == 0)
    def _():
        begin(turn)

    @pl.when(turn + 1 < pl.num_programs(0))
    def _():
        begin(turn + 1)

    slot = turn % 2
    for n in range(len(pieces)):
        pltpu.make_async_copy(refs[0].at[0], held_ref.at[slot, n], sems.at[slot, n]).wait()
    own = own_ref[...].astype(f32).reshape(together * agents, width)
    listed = held_ref[slot].astype(f32).reshape(len(pieces) * agents, width)
    theirs = rms(listed).astype(bf16)
    projected = projected_ref[...].reshape(together * agents, 3 * width)
    queries, near = projected[:, :width], projected[:, width:]
    away = dot(theirs, proj_ref[:, width:]).astype(bf16)
    mixed = []
    for s in range(together):
        here = slice(s * agents, (s + 1) * agents)
        there = slice(s * list_length * agents, (s + 1) * list_length * agents)
        keyvals = jnp.concatenate([near[here], away[there]], axis=0)
        mixed.append(
            attend(queries[here], keyvals[:, :width], keyvals[:, width:], head_size, None)
        )
    residual = own + dot(jnp.concatenate(mixed, axis=0), merge_ref[...])
    residual_ref[...] = residual.reshape(together, agents, width)
    normed_ref[...] = rms(residual).astype(bf16).reshape(together, agents, width)


def agent_stage(
    embedded, projected, arrays, table, first_step, steps, list_length, proj, merge, after=()
):
    _, agents, width = embedded.shape
    together = math.gcd(steps, math.gcd(first_step, 4 if steps > 4 else 2))
    piece = (together, agents, width)
    whole = lambda i, w: (0, 0)
    flops = 2 * steps * agents * width * width * (4 + 2 * list_length + 2 * (1 + list_length))
    return pl.pallas_call(
        functools.partial(
            agent_kernel, list_length, first_step, tuple(arrays), len(after), width // HEADS
        ),
        grid_spec=pltpu.PrefetchScalarGridSpec(
            num_scalar_prefetch=1,
            grid=(steps // together,),
            in_specs=[
                pl.BlockSpec((together, agents, cols), lambda i, w: (first_step // together + i, 0, 0))
                for cols in (width, 3 * width)
            ]
            + [pl.BlockSpec(memory_space=pltpu.HBM)] * (len(arrays) + len(after))
            + [pl.BlockSpec(proj.shape, whole), pl.BlockSpec(merge.shape, whole)],
            out_specs=[pl.BlockSpec(piece, lambda i, w: (i, 0, 0))] * 2,
            scratch_shapes=[
                pltpu.VMEM((2, together * list_length, agents, width), bf16),
                pltpu.SemaphoreType.DMA((2, together * list_length)),
            ],
        ),
        out_shape=[
            jax.ShapeDtypeStruct((steps, agents, width), f32),
            jax.ShapeDtypeStruct((steps, agents, width), bf16),
        ],
        compiler_params=pltpu.CompilerParams(vmem_limit_bytes=24 * MIB),
        cost_estimate=pl.CostEstimate(
            flops=5 * flops, bytes_accessed=steps * agents * width * 12, transcendentals=0
        ),
        name="agent_stage",
    )(table, embedded, projected, *arrays.values(), *after, proj, merge)


def pack_kernel(codes, parts, idle, table_ref, *refs):
    arrays = dict(zip(codes, refs))
    outs, (held_ref, in_sems, out_sems) = refs[len(codes) + idle : -3], refs[-3:]
    slots = []
    for out, (offset, count, first) in zip(outs, parts):
        slots += [(offset, first, n, out.at[n]) for n in range(count)]

    def guarded(offset, n, action):
        if offset is None:
            action()
        else:
            pl.when(table_ref[offset + n] >= 0)(action)

    for at, (offset, first, n, _) in enumerate(slots):
        if offset is None:
            own = arrays[0].at[first + n]
            pltpu.make_async_copy(own, held_ref.at[at], in_sems.at[at]).start()
        else:
            fetch(table_ref[offset + n], arrays, held_ref.at[at], in_sems.at[at])
    for at, (offset, first, n, target) in enumerate(slots):

        def pass_on(at=at, target=target):
            pltpu.make_async_copy(refs[0].at[0], held_ref.at[at], in_sems.at[at]).wait()
            pltpu.make_async_copy(held_ref.at[at], target, out_sems.at[at]).start()

        guarded(offset, n, pass_on)
    for at, (offset, first, n, target) in enumerate(slots):

        def finish(at=at, target=target):
            pltpu.make_async_copy(held_ref.at[at], target, out_sems.at[at]).wait()

        guarded(offset, n, finish)


def pack(table, arrays, parts, after=()):
    piece = next(iter(arrays.values())).shape[1:]
    slots = sum(count for _, count, _ in parts)
    smem = pl.BlockSpec(memory_space=pltpu.SMEM)
    hbm = pl.BlockSpec(memory_space=pltpu.HBM)
    out_specs = [hbm] * len(parts)
    out_shape = [jax.ShapeDtypeStruct((count,) + piece, bf16) for _, count, _ in parts]
    return pl.pallas_call(
        functools.partial(pack_kernel, tuple(arrays), tuple(parts), len(after)),
        in_specs=[smem] + [hbm] * (len(arrays) + len(after)),
        out_specs=out_specs,
        out_shape=out_shape,
        scratch_shapes=[
            pltpu.VMEM((slots,) + piece, bf16),
            pltpu.SemaphoreType.DMA((slots,)),
            pltpu.SemaphoreType.DMA((slots,)),
        ],
        cost_estimate=pl.CostEstimate(
            flops=0, bytes_accessed=piece[0] * piece[1], transcendentals=0
        ),
        compiler_params=pltpu.CompilerParams(
            vmem_limit_bytes=slots * piece[0] * piece[1] * 2 + 2 * MIB
        ),
        name="pack",
    )(table, *arrays.values(), *after)


def suffix(values, rewards, done, next_value, next_advantage):
    steps = values.shape[0]
    living = 1.0 - done.astype(f32)
    running, following, rows = next_advantage, next_value, [None] * steps
    for step in range(steps - 1, -1, -1):
        alive = living[step : step + 1]
        value = values[step : step + 1]
        change = rewards[step : step + 1] + discount * alive * following - value
        running = change + discount * trace_decay * alive * running
        rows[step] = running
        following = value
    return rows


def time_kernel(parts, steps, tile, head_size, offset_ref, *refs):
    refs = list(refs)
    residual_refs = [refs.pop(0) for _ in range(parts)]
    rim_refs = [refs.pop(0) for _ in range(parts)]
    proj_ref, merge_ref, weight_ref, done_ref, rewards_ref, boot_ref = refs[:6]
    values_ref, edge_ref, bias_ref = refs[6:]
    width = proj_ref.shape[0]
    turn = pl.program_id(0)
    group = 8
    rows = steps * group
    agents = values_ref.shape[1]

    @pl.when(turn == 0)
    def _():
        r = lax.broadcasted_iota(jnp.int32, (2 * rows, 2 * rows), 0) % rows
        c = lax.broadcasted_iota(jnp.int32, (2 * rows, 2 * rows), 1)
        query_step = r // group
        key_step = c // group - steps
        allowed = (
            (r % group == c % group)
            & (key_step <= query_step)
            & (key_step > query_step - WINDOW)
            & (key_step + offset_ref[0] >= 0)
        )
        bias_ref[...] = jnp.where(allowed, 0.0, -1e30)
        values_ref[...] = jnp.zeros_like(values_ref)

    def pieces(part_refs):
        whole = jnp.concatenate([ref[...].astype(f32) for ref in part_refs], axis=0)
        return [
            whole[:, at : at + group].reshape(rows, width) for at in range(0, tile, group)
        ]

    residuals = pieces(residual_refs)
    current = jnp.concatenate([rms(r).astype(bf16) for r in residuals], axis=0)
    behind = jnp.concatenate([r.astype(bf16) for r in pieces(rim_refs)], axis=0)
    projected = dot(current, proj_ref[...]).astype(bf16)
    before = dot(behind, proj_ref[:, width:]).astype(bf16)
    bias = bias_ref[...]
    mixed = []
    for at in range(0, tile * steps, rows):
        mine, past = projected[at : at + rows], before[at : at + rows]
        keys = jnp.concatenate([past[:, :width], mine[:, width : 2 * width]], axis=0)
        held = jnp.concatenate([past[:, width:], mine[:, 2 * width :]], axis=0)
        mixed.append(attend(mine[:, :width], keys, held, head_size, bias))
    merged = dot(jnp.concatenate(mixed, axis=0), merge_ref[...])
    lane = lax.broadcasted_iota(jnp.int32, (steps, group, agents), 2)
    place = lax.broadcasted_iota(jnp.int32, (steps, group, agents), 1)
    total = values_ref[...]
    for n, residual in enumerate(residuals):
        final = rms(residual + merged[n * rows : (n + 1) * rows])
        value = jnp.sum(final * weight_ref[...], axis=-1, keepdims=True)
        spot = lane == place + (turn * tile + n * group)
        total = total + jnp.sum(
            jnp.where(spot, value.reshape(steps, group, 1), 0.0), axis=1
        )
    values_ref[...] = total

    @pl.when(turn == pl.num_programs(0) - 1)
    def _():
        found = values_ref[...]
        boot = boot_ref[...]
        advantages = suffix(found, rewards_ref[...], done_ref[...], boot, jnp.zeros_like(boot))
        edge_ref[...] = jnp.concatenate([found[:1], advantages[0]], axis=0)


def time_stage(residuals, rims, offset, proj, merge, weight, done, rewards, boot):
    part_steps = [r.shape[0] for r in residuals]
    steps = sum(part_steps)
    _, agents, width = residuals[0].shape
    tile = math.gcd(agents, 64)
    whole = lambda i, o: (0, 0)

    def blocks(arrays):
        return [
            pl.BlockSpec((array.shape[0], tile, width), lambda i, o: (0, i, 0))
            for array in arrays
        ]

    rows = 16 * steps
    fixed = [proj, merge, weight, done, rewards, boot]
    return pl.pallas_call(
        functools.partial(time_kernel, len(residuals), steps, tile, width // HEADS),
        grid_spec=pltpu.PrefetchScalarGridSpec(
            num_scalar_prefetch=1,
            grid=(agents // tile,),
            in_specs=blocks(residuals)
            + blocks(rims)
            + [pl.BlockSpec(array.shape, whole) for array in fixed],
            out_specs=[
                pl.BlockSpec((steps, agents), whole),
                pl.BlockSpec((2, agents), whole),
            ],
            scratch_shapes=[pltpu.VMEM((rows, rows), f32)],
        ),
        out_shape=[
            jax.ShapeDtypeStruct((steps, agents), f32),
            jax.ShapeDtypeStruct((2, agents), f32),
        ],
        compiler_params=pltpu.CompilerParams(vmem_limit_bytes=40 * MIB),
        cost_estimate=pl.CostEstimate(flops=0, bytes_accessed=rows, transcendentals=0),
        name="time_stage",
    )(offset, *residuals, *rims, *fixed)


def advantage_kernel(last_ref, values_ref, rewards_ref, done_ref, boot_ref, edge_ref, out_ref, mine_ref):
    last = last_ref[0] > 0
    arriving = edge_ref[...]
    boot = boot_ref[...]
    found = values_ref[...]
    next_value = jnp.where(last, boot, arriving[:1])
    next_advantage = jnp.where(last, 0.0, arriving[1:2])
    rows = suffix(found, rewards_ref[...], done_ref[...], next_value, next_advantage)
    out_ref[...] = jnp.concatenate(rows, axis=0)
    mine_ref[...] = jnp.concatenate([found[:1], rows[0]], axis=0)


def advantage_stage(last, values, rewards, done, boot, edge):
    return pl.pallas_call(
        advantage_kernel,
        in_specs=[pl.BlockSpec(memory_space=pltpu.SMEM)]
        + [pl.BlockSpec(memory_space=pltpu.VMEM)] * 5,
        out_specs=[pl.BlockSpec(memory_space=pltpu.VMEM)] * 2,
        out_shape=[
            jax.ShapeDtypeStruct(values.shape, f32),
            jax.ShapeDtypeStruct(edge.shape, f32),
        ],
        name="advantage_stage",
    )(last, values, rewards, done, boot, edge)


def exchange_slots(embedded, lists, capacity):
    steps, agents, width = embedded.shape
    blocks = lax.axis_size("agent")
    list_length = lists.shape[1]
    named = lists.reshape(-1)
    row_steps = jnp.arange(named.shape[0], dtype=jnp.int32) // list_length
    hits = (named[:, None] == jnp.arange(blocks, dtype=jnp.int32)[None, :]).astype(jnp.int32)
    slot = jnp.sum((jnp.cumsum(hits, axis=0) - hits) * hits, axis=1)
    slot_hits = (slot[:, None] == jnp.arange(capacity, dtype=jnp.int32)[None, :]).astype(jnp.int32)
    requests = jnp.sum(
        (hits * row_steps[:, None])[:, :, None] * slot_hits[:, None, :], axis=0
    )
    wanted = lax.all_to_all(requests, "agent", split_axis=0, concat_axis=0, tiled=True)
    outgoing = embedded[wanted.reshape(-1)].reshape(blocks, capacity, agents, width)
    arrived = lax.all_to_all(outgoing, "agent", split_axis=0, concat_axis=0, tiled=True)
    return arrived.reshape(blocks * capacity, agents, width), named * capacity + slot


OUTWARD_READY = {1: (0, 1, 1), 2: (1, 3, 3), 3: (2, 3, 4)}
ACROSS_READY = {0: (1, 2, 2), 1: (0, 0, 0), 2: (1, 3, 3), 3: (2, 3, 4)}
OUTWARD_DUE = (3, 4, 4)
ACROSS_DUE = (3, 4, 5)


def relay_sizes(steps, capacity):
    half, quarter = steps // 2, steps // 4
    chunks = [half, quarter, quarter]
    outward = [half, half, half, half, quarter + 2]
    across = [quarter, half, half, half - 1, quarter + 2, quarter + 2]
    return chunks, outward, across


def relay_codes(outward, across):
    names = {}
    code = 1
    for name, count in (("edge", len(outward)), ("swap", 2), ("far", 3), ("across", len(across))):
        names[name] = [code + n for n in range(count)]
        code += count
    names["own"] = 0
    return names


def inner_place(codes, starts, u, k):
    behind = starts[k] - starts[min(k, 1)]
    if u == 0:
        return codes["edge"][min(k, 1)] * SPAN + behind
    if u == 1:
        return codes["own"] * SPAN + starts[k]
    if u == 2:
        return codes["swap"][min(k, 1)] * SPAN + behind
    return codes["far"][k] * SPAN


def plan_kernel(steps, list_length, chunks, outward, across, place_ref, lists_ref, out_ref, in_ref, flag_ref, eloc, yloc, room):
    codes = relay_codes(outward, across)
    column, row = place_ref[0], place_ref[1]
    far_side = column >= COLUMNS // 2
    mirror = lambda u: jnp.where(far_side, COLUMNS - 1 - u, u)
    me = mirror(column)
    inner = me == 1
    starts = [sum(chunks[:k]) for k in range(len(chunks))]
    e_base = [sum(outward[:b]) for b in range(len(outward))]
    y_base = [sum(outward) + sum(across[:b]) for b in range(len(across))]
    block = lambda c, r: c * ROWS + r
    entry = lambda c, r, t, j: lists_ref[((c * ROWS + r) * steps + t) * list_length + j]

    def clear(n, _):
        out_ref[n] = -1
        return 0

    lax.fori_loop(0, sum(outward) + sum(across), clear, 0)

    @pl.when(me == 0)
    def _():
        for n in range(outward[1]):
            out_ref[e_base[1] + n] = codes["own"] * SPAN + starts[1] + n

    def named(place, r, t, source):
        hit = entry(place, r, t, 0) == source
        for j in range(1, list_length):
            hit = hit | (entry(place, r, t, j) == source)
        return hit

    def choose(sizes, ready):
        batch = jnp.int32(-1)
        for b in range(len(sizes) - 1, -1, -1):
            batch = jnp.where((room[b] < sizes[b]) & (b >= ready), b, batch)
        return batch

    def base_of(bases, batch):
        base = jnp.int32(0)
        for b, value in enumerate(bases):
            base = jnp.where(batch == b, value, base)
        return base

    def empty(sizes):
        for b in range(len(sizes)):
            room[b] = 0

    for turn in range(2):
        sender = row if turn == 0 else 1 - row
        empty(outward)
        room[0] = outward[0]
        for k, count in enumerate(chunks):
            for u in (1, 2, 3):

                def first_piece(n, _):
                    eloc[(turn * COLUMNS + 1) * steps + n] = n
                    return 0

                if u == 1 and k == 0:
                    lax.fori_loop(0, count, first_piece, 0)
                    continue

                def outer_piece(n, _, u=u, k=k):
                    t = starts[k] + n
                    source = block(mirror(u), sender)
                    need = named(0, 0, t, source)
                    for r in range(1, ROWS):
                        need = need | named(0, r, t, source)
                    batch = choose(outward, OUTWARD_READY[u][k])
                    eloc[(turn * COLUMNS + u) * steps + t] = -1

                    @pl.when(need & (batch >= 0))
                    def _():
                        slot = room[batch]
                        room[batch] = slot + 1
                        eloc[(turn * COLUMNS + u) * steps + t] = batch * SPAN + slot
                        if turn == 0:

                            @pl.when(inner)
                            def _():
                                out_ref[base_of(e_base, batch) + slot] = inner_place(codes, starts, u, k) + n

                    return 0

                lax.fori_loop(0, count, outer_piece, 0)

    for turn in range(2):
        sender = row if turn == 0 else 1 - row
        empty(across)
        for k, count in enumerate(chunks):
            for u in range(COLUMNS):

                def row_piece(n, _, u=u, k=k):
                    t = starts[k] + n
                    need = named(me, 1 - sender, t, block(mirror(u), sender))
                    if u == 0:
                        lies = jnp.int32(codes["own"] * SPAN) + t
                        when = jnp.int32(0)
                    else:
                        where = eloc[(turn * COLUMNS + u) * steps + t]
                        lies = codes["edge"][0] * SPAN + where
                        when = jnp.where(where < 0, len(across), where // SPAN + 1)
                    when = jnp.where(inner, ACROSS_READY[u][k], when)
                    lies = jnp.where(inner, inner_place(codes, starts, u, k) + n, lies)
                    batch = choose(across, when)
                    yloc[(turn * COLUMNS + u) * steps + t] = -1

                    @pl.when(need & (batch >= 0))
                    def _():
                        slot = room[batch]
                        room[batch] = slot + 1
                        yloc[(turn * COLUMNS + u) * steps + t] = batch * SPAN + slot
                        if turn == 0:
                            out_ref[base_of(y_base, batch) + slot] = lies

                    return 0

                lax.fori_loop(0, count, row_piece, 0)

    flag_ref[0] = 0
    for k, count in enumerate(chunks):

        def listed_piece(n, _, k=k):
            t = starts[k] + n // list_length
            source = entry(me, row, t, n % list_length)
            u = mirror(source // ROWS)
            same = source % ROWS == row
            e = eloc[u * steps + t]
            y = yloc[(COLUMNS + u) * steps + t]
            first = jnp.int32(0)
            for w in (0, 2, 3):
                first = jnp.where(u == w, inner_place(codes, starts, w, k), first)
            direct = jnp.where(inner, first + t - starts[k], codes["edge"][0] * SPAN + e)
            direct = jnp.where(u == me, codes["own"] * SPAN + t, direct)
            local = inner | (u == me)
            bad = jnp.where(
                same,
                jnp.logical_not(local) & ((e < 0) | (e // SPAN > OUTWARD_DUE[k])),
                (y < 0) | (y // SPAN > ACROSS_DUE[k]),
            )
            place = jnp.where(same, direct, codes["across"][0] * SPAN + y)
            in_ref[t * list_length + n % list_length] = jnp.where(bad, codes["own"] * SPAN, place)

            @pl.when(bad)
            def _():
                flag_ref[0] = 1

            return 0

        lax.fori_loop(0, count * list_length, listed_piece, 0)


def plan(lists_near, place, steps, list_length, chunks, outward, across):
    smem = pl.BlockSpec(memory_space=pltpu.SMEM)
    slots = sum(outward) + sum(across)
    return pl.pallas_call(
        functools.partial(plan_kernel, steps, list_length, chunks, outward, across),
        in_specs=[smem, smem],
        out_specs=[smem] * 3,
        out_shape=[
            jax.ShapeDtypeStruct((slots,), jnp.int32),
            jax.ShapeDtypeStruct((steps * list_length,), jnp.int32),
            jax.ShapeDtypeStruct((1,), jnp.int32),
        ],
        scratch_shapes=[
            pltpu.SMEM((2 * COLUMNS * steps,), jnp.int32),
            pltpu.SMEM((2 * COLUMNS * steps,), jnp.int32),
            pltpu.SMEM((max(len(outward), len(across)),), jnp.int32),
        ],
        name="plan",
    )(place, lists_near)


def shared(value, axes):
    count = lax.axis_size(axes)
    rows = jnp.broadcast_to(value[None], (count,) + value.shape)
    return lax.all_to_all(rows, axes, split_axis=0, concat_axis=0, tiled=True)


def column_pairs(moves):
    return [(a * ROWS + r, b * ROWS + r) for a, b in moves for r in range(ROWS)]


def relay(embedded, lists, capacity, attention, own_projection):
    steps, agents, width = embedded.shape
    list_length = lists.shape[1]
    chunks, outward, across = relay_sizes(steps, capacity)
    codes = relay_codes(outward, across)
    starts = [sum(chunks[:k]) for k in range(len(chunks))]
    e_base = [sum(outward[:b]) for b in range(len(outward))]
    y_base = [sum(outward) + sum(across[:b]) for b in range(len(across))]
    index = lax.axis_index("agent")
    place = jnp.stack([index // ROWS, index % ROWS]).astype(jnp.int32)
    send = lambda value, pairs: lax.ppermute(value, "agent", pairs)
    edges = column_pairs([(0, 1), (1, 0), (2, 3), (3, 2)])
    swap = column_pairs([(1, 2), (2, 1)])
    over = [(c * ROWS + r, c * ROWS + 1 - r) for c in range(COLUMNS) for r in range(ROWS)]
    own, edge, swapped, far, rows = (codes[n] for n in ("own", "edge", "swap", "far", "across"))
    arrays = {own: embedded}

    def pick(names):
        return {code: arrays[code] for code in names}

    def across_part(n):
        return (y_base[n], across[n], None)

    def stage(n, reads, settled, after=()):
        parts = [across_part(n)]
        if n < len(outward):
            parts.append((e_base[n], outward[n], None))
        if n == 1:
            parts.append((None, outward[1], starts[1]))
        after = tuple(arrays[rows[b]] for b in settled) + tuple(after)
        packed = pack(out_table, pick([own] + reads), parts, after)
        if n < len(outward):
            arrays[edge[n]] = send(packed[1], edges)
        arrays[rows[n]] = send(packed[0], over)
        return packed

    mine = lists.reshape(-1)
    beside = send(mine, over)
    pair = jnp.stack([jnp.where(index % ROWS == r, mine, beside) for r in range(ROWS)])
    inward = column_pairs([(0, 1), (COLUMNS - 1, COLUMNS - 2)])
    outer_pair = send(pair, inward)
    column = index // ROWS
    outer = (column == 0) | (column == COLUMNS - 1)
    near = jnp.concatenate([jnp.where(outer, pair, outer_pair), pair], axis=0).reshape(-1)
    begin = jnp.minimum(near[0], 0)
    first = lax.dynamic_slice_in_dim(embedded, begin, chunks[0], 0)
    arrays[edge[0]] = send(first, edges)
    arrays[swapped[0]] = send(first, swap)
    out_table, in_table, flag = plan(
        near, place, steps, list_length, chunks, outward, across
    )
    (token,) = pack(out_table, pick([own]), [across_part(0)])
    arrays[rows[0]] = send(token, over)
    crowded = jnp.max(shared(flag, ("groups", "agent", "tm")))
    arrays[far[0]] = send(arrays[edge[0]], swap)
    reads = edge[:1] + swapped[:1]
    packed = stage(1, reads, (0,), (token, crowded.reshape(1)))
    arrays[swapped[1]] = send(packed[2], swap)
    for k in (1, 2):
        at = starts[k] - starts[1]
        arrays[far[k]] = send(arrays[edge[1]][at : at + chunks[k]], swap)
    reads = reads + edge[1:2] + far[:1]
    projected = own_projection(packed[:1])
    packed = stage(2, reads, (1,), (projected,))
    reads = reads + edge[2:3] + swapped[1:] + far[1:2]
    packed = stage(3, reads, (2,), packed[:1])
    reads = reads + edge[3:4] + far[2:3]
    packed = stage(4, reads, (3,), packed[:1])

    def attend_chunk(k, after):
        return attention(
            starts[k], chunks[k], due(arrays, codes, starts, k), in_table, projected, after
        )

    done = [attend_chunk(0, packed[:1])]
    reads = reads + edge[4:5]
    packed = stage(5, reads, (4,), (done[0][0],))
    done.append(attend_chunk(1, packed[:1]))
    done.append(attend_chunk(2, (done[1][0],)))
    return done, crowded


def due(arrays, codes, starts, k):
    wanted = {codes["own"], *codes["edge"][: OUTWARD_DUE[k] + 1]}
    wanted |= {inner_place(codes, starts, u, k) // SPAN for u in (0, 2, 3)}
    wanted |= set(codes["across"][: ACROSS_DUE[k] + 1])
    return {code: arrays[code] for code in sorted(wanted)}


def body(
    embedded,
    block_lists,
    done_flags,
    rewards,
    bootstrap,
    agent_proj,
    agent_merge,
    time_proj,
    time_merge,
    value_weight,
):
    steps, agents, width = embedded.shape
    list_length = block_lists.shape[2]
    blocks = lax.axis_size("agent")
    lists = block_lists[0]
    capacity = max(2, (2 * steps * list_length + blocks - 1) // blocks)
    spans = lax.axis_size("tm")
    index = lax.axis_index("tm")
    offset = (index * steps).astype(jnp.int32).reshape(1)
    boot = bootstrap.reshape(1, agents)
    forward = [(i, i + 1) for i in range(spans - 1)]
    backward = [(i + 1, i) for i in range(spans - 1)]

    def own_projection(after=()):
        return own_stage(embedded, agent_proj, after)

    def attention(first, count, arrays, table, projected, after=()):
        residual, normed = agent_stage(
            embedded,
            projected,
            arrays,
            table,
            first,
            count,
            list_length,
            agent_proj,
            agent_merge,
            after,
        )
        return residual, lax.ppermute(normed, "tm", forward)

    def finish(done):
        residuals, rims = [part[0] for part in done], [part[1] for part in done]
        values, edge = time_stage(
            residuals,
            rims,
            offset,
            time_proj,
            time_merge,
            value_weight.reshape(1, width),
            done_flags,
            rewards,
            boot,
        )
        last = (index == spans - 1).astype(jnp.int32).reshape(1)
        for _ in range(max(1, spans - 1)):
            arriving = lax.ppermute(edge, "tm", backward)
            advantages, edge = advantage_stage(last, values, rewards, done_flags, boot, arriving)
        return values, advantages

    def padded():
        pool, where = exchange_slots(embedded, lists, capacity)
        return finish([attention(0, steps, {1: pool}, where + SPAN, own_projection())])

    if blocks != COLUMNS * ROWS or steps % 4:
        return padded()
    done, crowded = relay(embedded, lists, capacity, attention, own_projection)
    found = finish(done)
    return lax.cond(crowded > 0, padded, lambda: found)


def solution(mesh):
    placed = (
        P(("groups", "tm"), "agent", None),
        P(("groups", "agent"), "tm", None),
        P(("groups", "tm"), "agent"),
        P(("groups", "tm"), "agent"),
        P(("groups", "agent")),
        P(),
        P(),
        P(),
        P(),
        P(),
    )
    return jax.shard_map(
        body,
        mesh=mesh,
        in_specs=placed,
        out_specs=(P(("groups", "tm"), "agent"), P(("groups", "tm"), "agent")),
        check_vma=False,
    )
```
